128 devices in a mesh: depth: 16 (over x_lo, z, core), mod: 8 (over x_hi, y).
Axes of the slice: x: 4 (x_hi: 2, x_lo: 2; x = x_hi * 2 + x_lo), y: 4, z: 4, core: 2. Of those that a mesh axis runs over, the one named last changes fastest.
Arguments:
- tokens: bfloat16 [64, 1024, 768], P('depth', 'mod'), may hold values from -40 to 40
- cotangent: bfloat16 [64, 1024, 768], P('depth', 'mod'), may hold values from -6 to 6
- lesion: int32 [64, 1024], P('depth', 'mod'), may hold values 0 or 1
- w_qkv: bfloat16 [768, 2304], replicated, may hold values from -5 to 5
- w_out: bfloat16 [768, 768], replicated, may hold values from -0.21875 to 0.21875
- norm_gain: float32 [768], replicated, may hold values from 0.5 to 1.5
Outputs:
- mixed: bfloat16 [64, 1024, 768], P('depth', 'mod')
- grad_tokens: bfloat16 [64, 1024, 768], P('depth', 'mod')
- grad_qkv_weight: float32 [768, 2304], P(('depth', 'mod'))
- grad_out_weight: float32 [768, 768], P(('depth', 'mod'))
- grad_gain: float32 [768], P(('depth', 'mod'))
The draws below stay inside these ranges and needn't reach their ends.
All inputs are finite; a program needn't handle non-finite values. No bound on the sum of `lesion` on one device may be relied on, other than what follows from the above.
Results may differ from the reference program's by a relative error of at most 0.007.
The reference program's roundings to bfloat16 on the way count: a program that leaves them out, or rounds other values in their place, can miss the bound.
Values may be sent and summed in bfloat16 or wider, within the bound.
No kernel may reach another device: no remote copies, remote signals or barrier semaphores. Data moves between devices by JAX's collectives and lax.ppermute only.
A program may use at most 128 MiB of HBM per device.

```python
import math
import jax
import jax.numpy as jnp
from jax import lax

D = 768
HEADS = 12
HEAD_DIM = 64
DEPTH = 64
ROWS_ALL = 512


def draw_tokens(key, part):
    first, second = jax.random.split(jax.random.fold_in(key, 11), 2)
    scales = jnp.exp(jax.random.uniform(second, (DEPTH, 2 * ROWS_ALL, 1), minval=math.log(0.5), maxval=math.log(5.0)))
    field = jnp.clip(jax.random.normal(first, (DEPTH, 2 * ROWS_ALL, D)), -6.0, 6.0)
    return (field * scales).astype(jnp.bfloat16)


def draw_w_qkv(key, part):
    first, second, third = jax.random.split(jax.random.fold_in(key, 23), 3)
    norm_scale = float(D) ** (-0.5)
    keys_part = jnp.clip(jax.random.normal(first, (D, D)), -6.0, 6.0) * norm_scale
    values_part = jnp.clip(jax.random.normal(second, (D, D)), -6.0, 6.0) * norm_scale
    noise = jnp.clip(jax.random.normal(third, (D, D)), -6.0, 6.0) * norm_scale
    query_part = noise
    return jnp.concatenate([query_part, keys_part, values_part], axis=1).astype(jnp.bfloat16)


def with_ends(result, rng, smallest, high):
    dims = result.shape
    place = [jax.random.randint(jax.random.fold_in(rng, axis), (), 0, dims[axis]) for axis in range(len(dims))]
    result = result.at[tuple(place)].set(smallest)
    longest = dims.index(max(dims))
    place[longest] = (place[longest] + 1) % dims[longest]
    return result.at[tuple(place)].set(high)


def block_scale(own_key, dims, pieces, smallest, largest):
    loudness = 1.0
    for dim, parts in pieces:
        heights = jax.random.uniform(jax.random.fold_in(jax.random.fold_in(own_key, 6), dim), (parts,), jnp.float32, smallest / len(pieces), largest / len(pieces))
        loudness = loudness * jnp.repeat(jnp.exp(heights), dims[dim] // parts).reshape((-1,) + (1,) * (len(dims) - 1 - dim))
    return loudness


def normal_values(stream_key, shape, spread, most, pieces=(), kind=jnp.bfloat16):
    drawn = jax.random.normal(stream_key, shape, jnp.float32) * spread
    if len(pieces) > 0:
        drawn = block_scale(stream_key, shape, pieces, -0.22, 0.18) * drawn
    return jnp.clip(drawn, min=-most, max=most).astype(kind)


def setup_inputs(seed: int = 0) -> dict:
    arg_keys = jax.random.split(jax.random.key(seed), 7)
    return {
        "tokens": draw_tokens(jax.random.fold_in(arg_keys[6], 71), 0),
        "cotangent": normal_values(arg_keys[1], (DEPTH, 2 * ROWS_ALL, D), 1.0, 6.0, ((0, 16), (1, 8))),
        "lesion": with_ends((jax.random.randint(arg_keys[2], (DEPTH, 2 * ROWS_ALL), 0, 4) < 1).astype(jnp.int32), jax.random.fold_in(arg_keys[2], 1), 0, 1),
        "w_qkv": draw_w_qkv(jax.random.fold_in(arg_keys[6], 71), 0),
        "w_out": normal_values(arg_keys[4], (D, D), D ** -0.5, 0.21875),
        "norm_gain": jnp.clip(1.0 + 0.1 * jax.random.normal(arg_keys[5], (D,), jnp.float32), 0.5, 1.5),
    }


EPS = 1e-06
LESION_GAIN = 3.0

def rounded(value):
    return lax.optimization_barrier(value.astype(jnp.bfloat16)).astype(jnp.float32)

def reference(tokens, cotangent, lesion, w_qkv, w_out, norm_gain):
    width = D
    scale = float(HEAD_DIM) ** (-0.5)
    depth_len = DEPTH
    block = math.gcd(ROWS_ALL, 32)
    nblocks = ROWS_ALL // block

    def to_blocks(field):
        shaped = field.reshape((depth_len, 2, ROWS_ALL) + field.shape[2:])
        order = (2, 1, 0) + tuple(range(3, shaped.ndim))
        moved = jnp.transpose(shaped, order)
        return moved.reshape((nblocks, block) + moved.shape[1:])

    def from_blocks(field):
        merged = field.reshape((ROWS_ALL,) + field.shape[2:])
        order = (2, 1, 0) + tuple(range(3, merged.ndim))
        return jnp.transpose(merged, order).reshape((depth_len, 2 * ROWS_ALL) + field.shape[4:])

    def block_step(carry, inputs):
        qkv_acc, out_acc, gain_acc = carry
        xb, gb, lb = inputs
        pb = xb.shape[0]
        xf = xb.astype(jnp.float32)
        inv_rms = lax.rsqrt(lax.optimization_barrier(jnp.mean(xf * xf, axis=-1, keepdims=True)) + EPS)
        unit = xf * inv_rms
        normed = (unit * norm_gain).astype(jnp.bfloat16)
        flat = normed.reshape(-1, width)
        qkv = jnp.dot(flat, w_qkv, preferred_element_type=jnp.float32).astype(jnp.bfloat16)
        qkv = qkv.reshape(pb, 2, depth_len, 3 * width)
        query = qkv[..., :width]
        key_own = qkv[..., width:2 * width]
        value_own = qkv[..., 2 * width:]
        keys = jnp.concatenate([key_own, key_own[:, ::-1]], axis=2)
        values = jnp.concatenate([value_own, value_own[:, ::-1]], axis=2)
        q4 = query.reshape(pb, 2, depth_len, HEADS, HEAD_DIM).astype(jnp.float32)
        k4 = keys.reshape(pb, 2, 2 * depth_len, HEADS, HEAD_DIM).astype(jnp.float32)
        v4 = values.reshape(pb, 2, 2 * depth_len, HEADS, HEAD_DIM).astype(jnp.float32)
        scores = jnp.einsum('bmqhd,bmkhd->bmhqk', q4, k4) * scale
        top = lax.optimization_barrier(jnp.max(scores, axis=-1, keepdims=True))
        expd = jnp.exp(scores - top)
        probs = expd / lax.optimization_barrier(jnp.sum(expd, axis=-1, keepdims=True))
        probs_bf = rounded(probs)
        attn = jnp.einsum('bmhqk,bmkhd->bmqhd', probs_bf, v4).astype(jnp.bfloat16)
        attn_flat = attn.reshape(-1, width)
        proj = jnp.dot(attn_flat, w_out, preferred_element_type=jnp.float32).astype(jnp.bfloat16)
        mixed = (xf + proj.reshape(xf.shape).astype(jnp.float32)).astype(jnp.bfloat16)
        weight = 1.0 + LESION_GAIN * lb.astype(jnp.float32)
        grad_y = (gb.astype(jnp.float32) * weight[..., None]).astype(jnp.bfloat16)
        gy_flat = grad_y.reshape(-1, width)
        out_acc = out_acc + jnp.dot(attn_flat.T, gy_flat, preferred_element_type=jnp.float32)
        grad_attn = jnp.dot(gy_flat, w_out.T, preferred_element_type=jnp.float32).astype(jnp.bfloat16)
        go4 = grad_attn.reshape(pb, 2, depth_len, HEADS, HEAD_DIM).astype(jnp.float32)
        dprob = jnp.einsum('bmqhd,bmkhd->bmhqk', go4, v4)
        delta = lax.optimization_barrier(jnp.sum(probs * dprob, axis=-1, keepdims=True))
        dscore = rounded(probs * (dprob - delta) * scale)
        grad_query = jnp.einsum('bmhqk,bmkhd->bmqhd', dscore, k4).astype(jnp.bfloat16)
        grad_query = grad_query.reshape(pb, 2, depth_len, width)
        kterm = jnp.einsum('bmhqk,bmqhd->bmkhd', dscore, q4).reshape(pb, 2, 2 * depth_len, width)
        vterm = jnp.einsum('bmhqk,bmqhd->bmkhd', probs_bf, go4).reshape(pb, 2, 2 * depth_len, width)
        grad_key = (kterm[:, :, :depth_len] + kterm[:, ::-1, depth_len:].astype(jnp.bfloat16).astype(jnp.float32)).astype(jnp.bfloat16)
        grad_value = (vterm[:, :, :depth_len] + vterm[:, ::-1, depth_len:].astype(jnp.bfloat16).astype(jnp.float32)).astype(jnp.bfloat16)
        grad_qkv = jnp.concatenate([grad_query, grad_key, grad_value], axis=-1).reshape(-1, 3 * width)
        qkv_acc = qkv_acc + jnp.dot(flat.T, grad_qkv, preferred_element_type=jnp.float32)
        grad_normed = jnp.dot(grad_qkv, w_qkv.T, preferred_element_type=jnp.float32).astype(jnp.bfloat16)
        grad_normed = grad_normed.reshape(xf.shape).astype(jnp.float32)
        gain_acc = gain_acc + lax.optimization_barrier(jnp.sum(grad_normed * unit, axis=(0, 1, 2)))
        dunit = grad_normed * norm_gain
        dxn = inv_rms * (dunit - unit * lax.optimization_barrier(jnp.mean(dunit * unit, axis=-1, keepdims=True)))
        grad_tokens = (grad_y.astype(jnp.float32) + dxn).astype(jnp.bfloat16)
        return ((qkv_acc, out_acc, gain_acc), (mixed, grad_tokens))
    init = (jnp.zeros((width, 3 * width), jnp.float32), jnp.zeros((width, width), jnp.float32), jnp.zeros((width,), jnp.float32))
    carry, outputs = lax.scan(block_step, init, (to_blocks(tokens), to_blocks(cotangent), to_blocks(lesion)))
    mixed = from_blocks(outputs[0])
    grad_tokens = from_blocks(outputs[1])
    return (mixed, grad_tokens, carry[0], carry[1], carry[2])
```

```python
import jax
import jax.numpy as jnp
import numpy as np
from jax import lax
from jax.experimental import pallas as pl
from jax.experimental.pallas import tpu as pltpu
from jax.sharding import PartitionSpec as P

HEADS = 12
HEAD_DIM = 64
EPS = 1e-06
LESION_GAIN = 3.0
D = 768
TOK = 512
AXES = ("depth", "mod")
BF = jnp.bfloat16
F32 = jnp.float32
MB = 1024 * 1024


def place(xlo, z, c, xhi, y):
    return (xlo * 8 + z * 2 + c) * 8 + xhi * 4 + y


def parts_of(i):
    d, m = divmod(i, 8)
    return d // 8, (d // 2) % 4, d % 2, m // 4, m % 4


PLANE = [
    [place(a, z, c, b, y) for a in range(2) for z in range(4) for c in range(2) for b in range(2)]
    for y in range(4)
]
CHIPS = [
    [place(a, z, c, b, y) for a in range(2) for z in range(4) for b in range(2)]
    for c in range(2)
    for y in range(4)
]
CORE_SWAP = [(i, i ^ 8) for i in range(128)]


def y_shift(s):
    out = []
    for i in range(128):
        a, z, c, b, y = parts_of(i)
        out.append((i, place(a, z, c, b, (y + s) % 4)))
    return out


def feature_table():
    table = np.zeros((8, D), np.int32)
    for c in range(2):
        for y in range(4):
            n = 0
            for rc in range(2):
                for ry in range(4):
                    for a in range(2):
                        for z in range(4):
                            for b in range(2):
                                i = place(a, z, c ^ rc, b, (y + ry) % 4)
                                for r in range(6):
                                    table[c * 4 + y, n] = 6 * i + r
                                    n += 1
    return table


FEATURES = feature_table()


def dot(a, b, ca, cb):
    return lax.dot_general(a, b, (((ca,), (cb,)), ((), ())), preferred_element_type=F32)


def send_order():
    i = lax.broadcasted_iota(jnp.int32, (TOK, TOK), 0)
    s = lax.broadcasted_iota(jnp.int32, (TOK, TOK), 1)
    src = ((i >> 2) & 3) * 128 + (i >> 4) * 4 + (i & 3)
    return s == src


def position_order():
    i = lax.broadcasted_iota(jnp.int32, (TOK, TOK), 0)
    s = lax.broadcasted_iota(jnp.int32, (TOK, TOK), 1)
    return s == (i & 127) * 4 + (i >> 7)


def onehot(mask):
    return jnp.where(mask, 1.0, 0.0).astype(BF)


def pack_kernel(tok_ref, cot_ref, les_ref, out_ref):
    mask = send_order()
    les = les_ref[...]
    weight = 1.0 + LESION_GAIN * les.astype(F32)
    row = jnp.concatenate([weight[d : d + 1, :] for d in range(4)], axis=1)
    plain = onehot(mask)
    scaled = jnp.where(mask, row, 0.0).astype(BF)
    t = dot(plain, tok_ref[...].reshape(TOK, D), 1, 0).astype(BF)
    out_ref[:, 0] = t.reshape(32, 16, D)
    g = dot(scaled, cot_ref[...].reshape(TOK, D), 1, 0).astype(BF)
    out_ref[:, 1] = g.reshape(32, 16, D)


def unpack_kernel(in_ref, mixed_ref, grad_ref):
    sel = onehot(send_order())
    a = dot(sel, in_ref[:, 0].reshape(TOK, D), 0, 0).astype(BF)
    mixed_ref[...] = a.reshape(4, 128, D)
    b = dot(sel, in_ref[:, 1].reshape(TOK, D), 0, 0).astype(BF)
    grad_ref[...] = b.reshape(4, 128, D)


def normalise(x):
    xf = x.astype(F32)
    inv_rms = lax.rsqrt(jnp.mean(xf * xf, axis=-1, keepdims=True) + EPS)
    return xf, inv_rms, xf * inv_rms


def main_kernel(
    recv_ref, gain_ref, feat_ref, wqkv_ref, wout_ref,
    keep_ref, send_ref, attn_ref, dqkv_ref,
    qkv_ref, ga_ref, norm_ref, gy_ref, lhs_ref,
):
    scale = float(HEAD_DIM) ** (-0.5)
    _, _, unit = normalise(recv_ref[:, 0].reshape(TOK, D))
    normed = (unit * gain_ref[...]).astype(BF)
    order = onehot(position_order())
    norm_ref[...] = dot(order, normed, 1, 0).astype(BF)
    gy_ref[...] = dot(order, recv_ref[:, 1].reshape(TOK, D), 1, 0).astype(BF)

    def project(n, _):
        cols = pl.ds(pl.multiple_of(n * 768, 768), 768)
        qkv_ref[:, cols] = dot(norm_ref[...], wqkv_ref[:, cols], 1, 0).astype(BF)
        return 0

    lax.fori_loop(0, 3, project, 0)
    ga_ref[...] = dot(gy_ref[...], wout_ref[...], 1, 1).astype(BF)
    first = lax.broadcasted_iota(jnp.int32, (128, 128), 1) < 64

    def split(x):
        zero = jnp.zeros_like(x)
        return jnp.concatenate([jnp.where(first, x, zero), jnp.where(first, zero, x)], axis=0)

    def heads(hp, _):
        base = pl.multiple_of(hp * 128, 128)
        for p in range(4):
            rows = slice(p * 128, (p + 1) * 128)
            q = qkv_ref[rows, pl.ds(base, 128)]
            kb = split(qkv_ref[rows, pl.ds(base + D, 128)])
            vb = split(qkv_ref[rows, pl.ds(base + 2 * D, 128)])
            ga = ga_ref[rows, pl.ds(base, 128)]
            s = (dot(kb, q, 1, 1) * scale).reshape(2, 128, 128)
            e = jnp.exp(s - jnp.max(s, axis=1, keepdims=True))
            probs = e * (1.0 / jnp.sum(e, axis=1, keepdims=True))
            dp = dot(vb, ga, 1, 1).reshape(2, 128, 128)
            delta = jnp.sum(probs * dp, axis=1, keepdims=True)
            ds = (probs * (dp - delta) * scale).astype(BF).reshape(256, 128)
            pb = probs.astype(BF).reshape(256, 128)
            attn_ref[rows, pl.ds(base, 128)] = dot(pb, vb, 0, 0).astype(BF)
            dqkv_ref[rows, pl.ds(base, 128)] = dot(ds, kb, 0, 0).astype(BF)
            dk = dot(ds, q, 1, 0)
            dv = dot(pb, ga, 1, 0)
            dqkv_ref[rows, pl.ds(base + D, 128)] = jnp.where(first, dk[:128], dk[128:]).astype(BF)
            dqkv_ref[rows, pl.ds(base + 2 * D, 128)] = jnp.where(first, dv[:128], dv[128:]).astype(BF)
        return 0

    lax.fori_loop(0, HEADS // 2, heads, 0)
    pick = onehot(lax.broadcasted_iota(jnp.int32, (D, D), 0) == feat_ref[...])
    lhs_ref[...] = dot(pick, norm_ref[...], 0, 1).astype(BF)

    def weight_grad(n, _):
        cols = pl.ds(pl.multiple_of(n * 768, 768), 768)
        g = dot(lhs_ref[...], dqkv_ref[:, cols], 1, 0).astype(BF)
        keep_ref[:, cols] = g[:384]
        send_ref[:, cols] = g[384:]
        return 0

    lax.fori_loop(0, 3, weight_grad, 0)
    lhs_ref[...] = dot(pick, attn_ref[...], 0, 1).astype(BF)
    g = dot(lhs_ref[...], gy_ref[...], 1, 0).astype(BF)
    keep_ref[:, 3 * D :] = g[:384]
    send_ref[:, 3 * D :] = g[384:]


def token_kernel(recv_ref, gain_ref, attn_ref, dqkv_ref, wqkv_ref, wout_ref, ret_ref, gain_out_ref):
    order = onehot(position_order())
    gn = dot(dqkv_ref[...], wqkv_ref[...], 1, 1).astype(BF)
    gn = dot(order, gn, 0, 0)
    xf, inv_rms, unit = normalise(recv_ref[:, 0].reshape(TOK, D))
    gain_out_ref[...] = jnp.sum(gn * unit, axis=0, keepdims=True)
    dunit = gn * gain_ref[...]
    back = inv_rms * (dunit - unit * jnp.mean(dunit * unit, axis=-1, keepdims=True))
    gy = recv_ref[:, 1].reshape(TOK, D).astype(F32)
    ret_ref[:, 1] = (gy + back).astype(BF).reshape(32, 16, D)
    attn = dot(order, attn_ref[...], 0, 0).astype(BF)
    proj = dot(attn, wout_ref[...], 1, 0).astype(BF)
    ret_ref[:, 0] = (xf + proj.astype(F32)).astype(BF).reshape(32, 16, D)


def pair_sum_kernel(a_ref, b_ref, o0, o1, o2, o3):
    s = (a_ref[...].astype(F32) + b_ref[...].astype(F32)).astype(BF)
    for n, o in enumerate((o0, o1, o2, o3)):
        o[...] = s[n * 96 : (n + 1) * 96]


def ring_sum_kernel(a, b, c, d, o):
    s = (a[...].astype(F32) + b[...].astype(F32)) + (c[...].astype(F32) + d[...].astype(F32))
    o[...] = s.astype(BF)


def params(mb):
    return pltpu.CompilerParams(vmem_limit_bytes=mb * MB)


def cost(flops, nbytes):
    return pl.CostEstimate(flops=int(flops), bytes_accessed=int(nbytes), transcendentals=0)


def shape(*dims, dtype=BF):
    return jax.ShapeDtypeStruct(dims, dtype)


def per_device(tokens, cotangent, lesion, w_qkv, w_out, norm_gain):
    gain = norm_gain.reshape(1, D)
    core = lax.axis_index("depth") & 1
    y = lax.axis_index("mod") & 3
    feat = lax.dynamic_slice(jnp.asarray(FEATURES), (core * 4 + y, 0), (1, D))
    packed = pl.pallas_call(
        pack_kernel, out_shape=shape(32, 2, 16, D), compiler_params=params(24),
        cost_estimate=cost(1e9, 4e6), name="pack",
    )(tokens, cotangent, lesion)
    recv = lax.all_to_all(packed, AXES, 0, 0, tiled=True, axis_index_groups=PLANE)
    keep, send, attn, dqkv = pl.pallas_call(
        main_kernel,
        out_shape=(shape(384, 4 * D), shape(384, 4 * D), shape(TOK, D), shape(TOK, 3 * D)),
        scratch_shapes=[
            pltpu.VMEM((TOK, 3 * D), BF), pltpu.VMEM((TOK, D), BF), pltpu.VMEM((TOK, D), BF),
            pltpu.VMEM((TOK, D), BF), pltpu.VMEM((D, TOK), BF),
        ],
        compiler_params=params(48), cost_estimate=cost(1e10, 1.5e7), name="main",
    )(recv, gain, feat, w_qkv, w_out)
    got = lax.ppermute(send, AXES, CORE_SWAP)
    ret, gain_part = pl.pallas_call(
        token_kernel, out_shape=(shape(32, 2, 16, D), shape(1, D, dtype=F32)),
        compiler_params=params(40), cost_estimate=cost(3.5e9, 1.2e7), name="token_grads",
    )(recv, gain, attn, dqkv, w_qkv, w_out)
    quarters = pl.pallas_call(
        pair_sum_kernel, out_shape=tuple(shape(96, 4 * D) for _ in range(4)),
        compiler_params=params(24), cost_estimate=cost(1e6, 7e6), name="pair_sum",
    )(keep, got)
    moved = [lax.ppermute(quarters[s], AXES, y_shift(s)) for s in range(1, 4)]
    back = lax.all_to_all(ret, AXES, 0, 0, tiled=True, axis_index_groups=PLANE)
    mine = pl.pallas_call(
        ring_sum_kernel, out_shape=shape(96, 4 * D), compiler_params=params(24),
        cost_estimate=cost(1e6, 3e6), name="ring_sum",
    )(quarters[0], *moved)
    mixed, grad_tokens = pl.pallas_call(
        unpack_kernel, out_shape=(shape(4, 128, D), shape(4, 128, D)),
        compiler_params=params(24), cost_estimate=cost(1e9, 4e6), name="unpack",
    )(back)
    last = lax.all_to_all(
        mine.reshape(16, 144, 128), AXES, 0, 0, tiled=True, axis_index_groups=CHIPS
    )
    share = jnp.sum(last.astype(F32), axis=0).reshape(6, 4 * D)
    gain_share = lax.psum_scatter(gain_part.reshape(D), AXES, scatter_dimension=0, tiled=True)
    return mixed, grad_tokens, share[:, : 3 * D], share[:, 3 * D :], gain_share


def solution(mesh):
    in_specs = (P("depth", "mod", None), P("depth", "mod", None), P("depth", "mod"), P(), P(), P())
    out_specs = (
        P("depth", "mod", None),
        P("depth", "mod", None),
        P(("depth", "mod"), None),
        P(("depth", "mod"), None),
        P(("depth", "mod")),
    )
    return jax.shard_map(
        per_device, mesh=mesh, in_specs=in_specs, out_specs=out_specs, check_vma=False
    )
```

```python
import jax
import jax.numpy as jnp
import numpy as np
from jax import lax
from jax.experimental import pallas as pl
from jax.experimental.pallas import tpu as pltpu
from jax.sharding import PartitionSpec as P

HEADS = 12
HEAD_DIM = 64
EPS = 1e-06
LESION_GAIN = 3.0
D = 768
TOK = 512
AXES = ("depth", "mod")
BF = jnp.bfloat16
F32 = jnp.float32
MB = 1024 * 1024
WIDE = 4 * D + 128
MAIN_MB = 24
TOKEN_MB = 20


def place(xlo, z, c, xhi, y):
    return (xlo * 8 + z * 2 + c) * 8 + xhi * 4 + y


def parts_of(i):
    d, m = divmod(i, 8)
    return d // 8, (d // 2) % 4, d % 2, m // 4, m % 4


PLANE = [
    [place(a, z, c, b, y) for a in range(2) for z in range(4) for c in range(2) for b in range(2)]
    for y in range(4)
]
CHIPS = [
    [place(a, z, c, b, y) for a in range(2) for z in range(4) for b in range(2)]
    for c in range(2)
    for y in range(4)
]
CORE_SWAP = [(i, i ^ 8) for i in range(128)]


def y_shift(s):
    out = []
    for i in range(128):
        a, z, c, b, y = parts_of(i)
        out.append((i, place(a, z, c, b, (y + s) % 4)))
    return out


def feature_table():
    table = np.zeros((8, D), np.int32)
    for c in range(2):
        for y in range(4):
            n = 0
            for rc in range(2):
                for ry in range(4):
                    for a in range(2):
                        for z in range(4):
                            for b in range(2):
                                i = place(a, z, c ^ rc, b, (y + ry) % 4)
                                for r in range(6):
                                    table[c * 4 + y, n] = 6 * i + r
                                    n += 1
    return table


FEATURES = feature_table()


def dot(a, b, ca, cb):
    return lax.dot_general(a, b, (((ca,), (cb,)), ((), ())), preferred_element_type=F32)


def send_order():
    i = lax.broadcasted_iota(jnp.int32, (TOK, TOK), 0)
    s = lax.broadcasted_iota(jnp.int32, (TOK, TOK), 1)
    src = ((i >> 2) & 3) * 128 + (i >> 4) * 4 + (i & 3)
    return s == src


def position_order():
    i = lax.broadcasted_iota(jnp.int32, (TOK, TOK), 0)
    s = lax.broadcasted_iota(jnp.int32, (TOK, TOK), 1)
    return s == (i & 127) * 4 + (i >> 7)


def onehot(mask):
    return jnp.where(mask, 1.0, 0.0).astype(BF)


def pack_kernel(tok_ref, cot_ref, les_ref, out_ref):
    mask = send_order()
    les = les_ref[...]
    weight = 1.0 + LESION_GAIN * les.astype(F32)
    row = jnp.concatenate([weight[d : d + 1, :] for d in range(4)], axis=1)
    plain = onehot(mask)
    scaled = jnp.where(mask, row, 0.0).astype(BF)
    t = dot(plain, tok_ref[...].reshape(TOK, D), 1, 0).astype(BF)
    out_ref[:, 0] = t.reshape(32, 16, D)
    g = dot(scaled, cot_ref[...].reshape(TOK, D), 1, 0).astype(BF)
    out_ref[:, 1] = g.reshape(32, 16, D)


def unpack_kernel(in_ref, mixed_ref, grad_ref):
    sel = onehot(send_order())
    a = dot(sel, in_ref[:, 0].reshape(TOK, D), 0, 0).astype(BF)
    mixed_ref[...] = a.reshape(4, 128, D)
    b = dot(sel, in_ref[:, 1].reshape(TOK, D), 0, 0).astype(BF)
    grad_ref[...] = b.reshape(4, 128, D)


def normalise(x):
    xf = x.astype(F32)
    inv_rms = lax.rsqrt(jnp.mean(xf * xf, axis=-1, keepdims=True) + EPS)
    return xf, inv_rms, xf * inv_rms


def main_kernel(
    recv_ref, gain_ref, feat_ref, wqkv_ref, wout_ref,
    keep_ref, send_ref, attn_ref, dqkv_ref,
    qkv_ref, ga_ref, norm_ref, gy_ref, lhs_ref,
):
    scale = float(HEAD_DIM) ** (-0.5)
    _, _, unit = normalise(recv_ref[:, 0].reshape(TOK, D))
    normed = (unit * gain_ref[...]).astype(BF)
    order = onehot(position_order())
    norm_ref[...] = dot(order, normed, 1, 0).astype(BF)
    gy_ref[...] = dot(order, recv_ref[:, 1].reshape(TOK, D), 1, 0).astype(BF)

    def project(n, _):
        cols = pl.ds(pl.multiple_of(n * 768, 768), 768)
        qkv_ref[:, cols] = dot(norm_ref[...], wqkv_ref[:, cols], 1, 0).astype(BF)
        return 0

    lax.fori_loop(0, 3, project, 0)
    ga_ref[...] = dot(gy_ref[...], wout_ref[...], 1, 1).astype(BF)
    first = lax.broadcasted_iota(jnp.int32, (128, 128), 1) < 64

    def split(x):
        zero = jnp.zeros_like(x)
        return jnp.concatenate([jnp.where(first, x, zero), jnp.where(first, zero, x)], axis=0)

    def heads(hp, _):
        base = pl.multiple_of(hp * 128, 128)
        for p in range(4):
            rows = slice(p * 128, (p + 1) * 128)
            q = qkv_ref[rows, pl.ds(base, 128)]
            kb = split(qkv_ref[rows, pl.ds(base + D, 128)])
            vb = split(qkv_ref[rows, pl.ds(base + 2 * D, 128)])
            ga = ga_ref[rows, pl.ds(base, 128)]
            s = (dot(kb, q, 1, 1) * scale).reshape(2, 128, 128)
            e = jnp.exp(s - jnp.max(s, axis=1, keepdims=True))
            probs = e * (1.0 / jnp.sum(e, axis=1, keepdims=True))
            dp = dot(vb, ga, 1, 1).reshape(2, 128, 128)
            delta = jnp.sum(probs * dp, axis=1, keepdims=True)
            ds = (probs * (dp - delta) * scale).astype(BF).reshape(256, 128)
            pb = probs.astype(BF).reshape(256, 128)
            attn_ref[rows, pl.ds(base, 128)] = dot(pb, vb, 0, 0).astype(BF)
            dqkv_ref[rows, pl.ds(base, 128)] = dot(ds, kb, 0, 0).astype(BF)
            dk = dot(ds, q, 1, 0)
            dv = dot(pb, ga, 1, 0)
            dqkv_ref[rows, pl.ds(base + D, 128)] = jnp.where(first, dk[:128], dk[128:]).astype(BF)
            dqkv_ref[rows, pl.ds(base + 2 * D, 128)] = jnp.where(first, dv[:128], dv[128:]).astype(BF)
        return 0

    lax.fori_loop(0, HEADS // 2, heads, 0)
    pick = onehot(lax.broadcasted_iota(jnp.int32, (D, D), 0) == feat_ref[...])
    lhs_ref[...] = dot(pick, norm_ref[...], 0, 1).astype(BF)

    def weight_grad(n, _):
        cols = pl.ds(pl.multiple_of(n * 768, 768), 768)
        g = dot(lhs_ref[...], dqkv_ref[:, cols], 1, 0).astype(BF)
        keep_ref[:, cols] = g[:384]
        send_ref[:, cols] = g[384:]
        return 0

    lax.fori_loop(0, 3, weight_grad, 0)
    lhs_ref[...] = dot(pick, attn_ref[...], 0, 1).astype(BF)
    g = dot(lhs_ref[...], gy_ref[...], 1, 0).astype(BF)
    keep_ref[:, 3 * D :] = g[:384]
    send_ref[:, 3 * D :] = g[384:]


def split_sum(v):
    v = jnp.sum(v, axis=1, keepdims=True)
    lane = lax.broadcasted_iota(jnp.int32, (v.shape[0], 128), 1)
    high = v.astype(BF).astype(F32)
    return jnp.where(lane == 0, high, jnp.where(lane == 1, v - high, 0.0)).astype(BF)


def token_kernel(
    recv_ref, gain_ref, feat_ref, attn_ref, dqkv_ref, wqkv_ref, wout_ref,
    ret_ref, gkeep_ref, gsend_ref,
):
    order = onehot(position_order())
    gn = dot(dqkv_ref[...], wqkv_ref[...], 1, 1).astype(BF)
    gn = dot(order, gn, 0, 0)
    xf, inv_rms, unit = normalise(recv_ref[:, 0].reshape(TOK, D))
    g = jnp.sum(gn * unit, axis=0, keepdims=True)
    high = g.astype(BF).astype(F32)
    mid = (g - high).astype(BF).astype(F32)
    terms = jnp.concatenate([high, mid, g - high - mid, jnp.zeros((125, D), F32)], axis=0)
    pick = onehot(lax.broadcasted_iota(jnp.int32, (D, D), 0) == feat_ref[...])
    cols = dot(pick, terms.astype(BF), 0, 1)
    gkeep_ref[...] = cols[:384]
    gsend_ref[...] = cols[384:]
    dunit = gn * gain_ref[...]
    back = inv_rms * (dunit - unit * jnp.mean(dunit * unit, axis=-1, keepdims=True))
    gy = recv_ref[:, 1].reshape(TOK, D).astype(F32)
    ret_ref[:, 1] = (gy + back).astype(BF).reshape(32, 16, D)
    attn = dot(order, attn_ref[...], 0, 0).astype(BF)
    proj = dot(attn, wout_ref[...], 1, 0).astype(BF)
    ret_ref[:, 0] = (xf + proj.astype(F32)).astype(BF).reshape(32, 16, D)


def pair_sum_kernel(a_ref, b_ref, ga_ref, gb_ref, o0, o1, o2, o3):
    s = (a_ref[...].astype(F32) + b_ref[...].astype(F32)).astype(BF)
    g = split_sum(ga_ref[...] + gb_ref[...])
    for n, o in enumerate((o0, o1, o2, o3)):
        o[:, : 4 * D] = s[n * 96 : (n + 1) * 96]
        o[:, 4 * D :] = g[n * 96 : (n + 1) * 96]


def ring_sum_kernel(a, b, c, d, o):
    s = (a[...].astype(F32) + b[...].astype(F32)) + (c[...].astype(F32) + d[...].astype(F32))
    o[:, : 4 * D] = s[:, : 4 * D].astype(BF)
    o[:, 4 * D :] = split_sum(s[:, 4 * D :])


def params(mb):
    return pltpu.CompilerParams(vmem_limit_bytes=mb * MB)


def cost(flops, nbytes):
    return pl.CostEstimate(flops=int(flops), bytes_accessed=int(nbytes), transcendentals=0)


def shape(*dims, dtype=BF):
    return jax.ShapeDtypeStruct(dims, dtype)


def per_device(tokens, cotangent, lesion, w_qkv, w_out, norm_gain):
    gain = norm_gain.reshape(1, D)
    core = lax.axis_index("depth") & 1
    y = lax.axis_index("mod") & 3
    feat = lax.dynamic_slice(jnp.asarray(FEATURES), (core * 4 + y, 0), (1, D))
    packed = pl.pallas_call(
        pack_kernel, out_shape=shape(32, 2, 16, D), compiler_params=params(16),
        cost_estimate=cost(1e9, 4e6), name="pack",
    )(tokens, cotangent, lesion)
    recv = lax.all_to_all(packed, AXES, 0, 0, tiled=True, axis_index_groups=PLANE)
    keep, send, attn, dqkv = pl.pallas_call(
        main_kernel,
        out_shape=(shape(384, 4 * D), shape(384, 4 * D), shape(TOK, D), shape(TOK, 3 * D)),
        scratch_shapes=[
            pltpu.VMEM((TOK, 3 * D), BF), pltpu.VMEM((TOK, D), BF), pltpu.VMEM((TOK, D), BF),
            pltpu.VMEM((TOK, D), BF), pltpu.VMEM((D, TOK), BF),
        ],
        compiler_params=params(MAIN_MB), cost_estimate=cost(1e10, 1.5e7), name="main",
    )(recv, gain, feat, w_qkv, w_out)
    got = lax.ppermute(send, AXES, CORE_SWAP)
    ret, gain_keep, gain_send = pl.pallas_call(
        token_kernel,
        out_shape=(shape(32, 2, 16, D), shape(384, 128, dtype=F32), shape(384, 128, dtype=F32)),
        compiler_params=params(TOKEN_MB), cost_estimate=cost(3.5e9, 1.2e7), name="token_grads",
    )(recv, gain, feat, attn, dqkv, w_qkv, w_out)
    gain_got = lax.ppermute(gain_send, AXES, CORE_SWAP)
    quarters = pl.pallas_call(
        pair_sum_kernel, out_shape=tuple(shape(96, WIDE) for _ in range(4)),
        compiler_params=params(16), cost_estimate=cost(1e6, 7e6), name="pair_sum",
    )(keep, got, gain_keep, gain_got)
    moved = [lax.ppermute(quarters[s], AXES, y_shift(s)) for s in range(1, 4)]
    back = lax.all_to_all(ret, AXES, 0, 0, tiled=True, axis_index_groups=PLANE)
    mine = pl.pallas_call(
        ring_sum_kernel, out_shape=shape(96, WIDE), compiler_params=params(16),
        cost_estimate=cost(1e6, 3e6), name="ring_sum",
    )(quarters[0], *moved)
    mixed, grad_tokens = pl.pallas_call(
        unpack_kernel, out_shape=(shape(4, 128, D), shape(4, 128, D)),
        compiler_params=params(24), cost_estimate=cost(1e9, 4e6), name="unpack",
    )(back)
    last = lax.all_to_all(
        mine.reshape(16, 150, 128), AXES, 0, 0, tiled=True, axis_index_groups=CHIPS
    )
    share = jnp.sum(last.astype(F32), axis=0).reshape(6, WIDE)
    gain_share = jnp.sum(share[:, 4 * D :], axis=1)
    return mixed, grad_tokens, share[:, : 3 * D], share[:, 3 * D : 4 * D], gain_share


def solution(mesh):
    in_specs = (P("depth", "mod", None), P("depth", "mod", None), P("depth", "mod"), P(), P(), P())
    out_specs = (
        P("depth", "mod", None),
        P("depth", "mod", None),
        P(("depth", "mod"), None),
        P(("depth", "mod"), None),
        P(("depth", "mod")),
    )
    return jax.shard_map(
        per_device, mesh=mesh, in_specs=in_specs, out_specs=out_specs, check_vma=False
    )
```

```python
import jax
import jax.numpy as jnp
import numpy as np
from jax import lax
from jax.experimental import pallas as pl
from jax.experimental.pallas import tpu as pltpu
from jax.sharding import PartitionSpec as P

HEADS = 12
HEAD_DIM = 64
EPS = 1e-06
LESION_GAIN = 3.0
D = 768
TOK = 512
AXES = ("depth", "mod")
BF = jnp.bfloat16
F32 = jnp.float32
MB = 1024 * 1024
MAIN_MB = 46
TOKEN_MB = 20


def place(xlo, z, c, xhi, y):
    return (xlo * 8 + z * 2 + c) * 8 + xhi * 4 + y


def parts_of(i):
    d, m = divmod(i, 8)
    return d // 8, (d // 2) % 4, d % 2, m // 4, m % 4


PLANE = [
    [place(a, z, c, b, y) for a in range(2) for z in range(4) for c in range(2) for b in range(2)]
    for y in range(4)
]
CHIPS = [
    [place(a, z, c, b, y) for a in range(2) for z in range(4) for b in range(2)]
    for c in range(2)
    for y in range(4)
]
CORE_SWAP = [(i, i ^ 8) for i in range(128)]


def y_shift(s):
    out = []
    for i in range(128):
        a, z, c, b, y = parts_of(i)
        out.append((i, place(a, z, c, b, (y + s) % 4)))
    return out


def feature_table():
    table = np.zeros((8, D), np.int32)
    for c in range(2):
        for y in range(4):
            n = 0
            for rc in range(2):
                for ry in range(4):
                    for a in range(2):
                        for z in range(4):
                            for b in range(2):
                                i = place(a, z, c ^ rc, b, (y + ry) % 4)
                                for r in range(6):
                                    table[c * 4 + y, n] = 6 * i + r
                                    n += 1
    return table


FEATURES = feature_table()


def dot(a, b, ca, cb):
    return lax.dot_general(a, b, (((ca,), (cb,)), ((), ())), preferred_element_type=F32)


def send_order():
    i = lax.broadcasted_iota(jnp.int32, (TOK, TOK), 0)
    s = lax.broadcasted_iota(jnp.int32, (TOK, TOK), 1)
    src = ((i >> 2) & 3) * 128 + (i >> 4) * 4 + (i & 3)
    return s == src


def position_order():
    i = lax.broadcasted_iota(jnp.int32, (TOK, TOK), 0)
    s = lax.broadcasted_iota(jnp.int32, (TOK, TOK), 1)
    return s == (i & 127) * 4 + (i >> 7)


def onehot(mask):
    return jnp.where(mask, 1.0, 0.0).astype(BF)


def pack_kernel(tok_hbm, cot_hbm, les_hbm, out_hbm, tok_ref, cot_ref, les_ref, out_ref, sems):
    loads = [
        pltpu.make_async_copy(src, dst, sems.at[n])
        for n, (src, dst) in enumerate(
            ((les_hbm, les_ref), (tok_hbm, tok_ref), (cot_hbm, cot_ref))
        )
    ]
    for c in loads:
        c.start()
    mask = send_order()
    plain = onehot(mask)
    loads[0].wait()
    weight = 1.0 + LESION_GAIN * les_ref[...].astype(F32)
    row = jnp.concatenate([weight[d : d + 1, :] for d in range(4)], axis=1)
    scaled = jnp.where(mask, row, 0.0).astype(BF)
    loads[1].wait()
    t = dot(plain, tok_ref[...].reshape(TOK, D), 1, 0).astype(BF)
    out_ref[0] = t.reshape(32, 16, D)
    store_t = pltpu.make_async_copy(out_ref.at[0], out_hbm.at[:, 0], sems.at[3])
    store_t.start()
    loads[2].wait()
    g = dot(scaled, cot_ref[...].reshape(TOK, D), 1, 0).astype(BF)
    out_ref[1] = g.reshape(32, 16, D)
    store_g = pltpu.make_async_copy(out_ref.at[1], out_hbm.at[:, 1], sems.at[4])
    store_g.start()
    store_t.wait()
    store_g.wait()


def unpack_kernel(in_ref, mixed_ref, grad_ref, gain_ref):
    sel = onehot(send_order())
    for n, out in enumerate((mixed_ref, grad_ref)):
        base = n * 96
        x = jnp.concatenate(
            [in_ref[:, base + l * 16 : base + l * 16 + 16].reshape(TOK, 128) for l in range(6)],
            axis=1,
        )
        out[...] = dot(sel, x, 0, 0).astype(BF).reshape(4, 128, D)
    g = jnp.sum(in_ref[:, 192:].astype(F32), axis=0)
    gain_ref[...] = jnp.broadcast_to(jnp.sum(g, axis=0, keepdims=True), (8, 128))


def normalise(x):
    xf = x.astype(F32)
    inv_rms = lax.rsqrt(jnp.mean(xf * xf, axis=-1, keepdims=True) + EPS)
    return xf, inv_rms, xf * inv_rms


def main_kernel(
    recv_hbm, gain_ref, feat_ref, wqkv_hbm, wout_hbm,
    keep_ref, send_ref, attn_ref, dqkv_ref,
    recv_ref, wqkv_ref, wout_ref, qkv_ref, ga_ref, norm_ref, gy_ref, lhs_ref, sems,
):
    scale = float(HEAD_DIM) ** (-0.5)
    loads = [
        pltpu.make_async_copy(src, dst, sems.at[n])
        for n, (src, dst) in enumerate(
            ((recv_hbm, recv_ref), (wqkv_hbm, wqkv_ref), (wout_hbm, wout_ref))
        )
    ]
    for c in loads:
        c.start()
    order = onehot(position_order())
    loads[0].wait()
    _, _, unit = normalise(recv_ref[:, 0].reshape(TOK, D))
    normed = (unit * gain_ref[...]).astype(BF)
    norm_ref[...] = dot(order, normed, 1, 0).astype(BF)
    gy_ref[...] = dot(order, recv_ref[:, 1].reshape(TOK, D), 1, 0).astype(BF)
    loads[1].wait()

    def project(n, _):
        cols = pl.ds(pl.multiple_of(n * 768, 768), 768)
        qkv_ref[:, cols] = dot(norm_ref[...], wqkv_ref[:, cols], 1, 0).astype(BF)
        return 0

    lax.fori_loop(0, 3, project, 0)
    loads[2].wait()
    ga_ref[...] = dot(gy_ref[...], wout_ref[...], 1, 1).astype(BF)
    first = lax.broadcasted_iota(jnp.int32, (128, 128), 1) < 64

    def split(x):
        zero = jnp.zeros_like(x)
        return jnp.concatenate([jnp.where(first, x, zero), jnp.where(first, zero, x)], axis=0)

    def heads(hp, _):
        base = pl.multiple_of(hp * 128, 128)
        rows = [slice(p * 128, (p + 1) * 128) for p in range(4)]
        q = [qkv_ref[r, pl.ds(base, 128)] for r in rows]
        kb = [split(qkv_ref[r, pl.ds(base + D, 128)]) for r in rows]
        vb = [split(qkv_ref[r, pl.ds(base + 2 * D, 128)]) for r in rows]
        ga = [ga_ref[r, pl.ds(base, 128)] for r in rows]
        s = [dot(kb[p], q[p], 1, 1).reshape(2, 128, 128) for p in range(4)]
        dp = [dot(vb[p], ga[p], 1, 1).reshape(2, 128, 128) for p in range(4)]
        pb, ds = [], []
        for p in range(4):
            sp = s[p] * scale
            e = jnp.exp(sp - jnp.max(sp, axis=1, keepdims=True))
            probs = e * (1.0 / jnp.sum(e, axis=1, keepdims=True))
            delta = jnp.sum(probs * dp[p], axis=1, keepdims=True)
            ds.append((probs * (dp[p] - delta) * scale).astype(BF).reshape(256, 128))
            pb.append(probs.astype(BF).reshape(256, 128))
        for p in range(4):
            attn_ref[rows[p], pl.ds(base, 128)] = dot(pb[p], vb[p], 0, 0).astype(BF)
            dqkv_ref[rows[p], pl.ds(base, 128)] = dot(ds[p], kb[p], 0, 0).astype(BF)
            dk = dot(ds[p], q[p], 1, 0)
            dv = dot(pb[p], ga[p], 1, 0)
            dqkv_ref[rows[p], pl.ds(base + D, 128)] = jnp.where(first, dk[:128], dk[128:]).astype(BF)
            dqkv_ref[rows[p], pl.ds(base + 2 * D, 128)] = jnp.where(first, dv[:128], dv[128:]).astype(BF)
        return 0

    lax.fori_loop(0, HEADS // 2, heads, 0)
    pick = onehot(lax.broadcasted_iota(jnp.int32, (D, D), 0) == feat_ref[...])
    lhs_ref[...] = dot(pick, norm_ref[...], 0, 1).astype(BF)

    def weight_grad(n, _):
        cols = pl.ds(pl.multiple_of(n * 768, 768), 768)
        g = dot(lhs_ref[...], dqkv_ref[:, cols], 1, 0).astype(BF)
        keep_ref[:, cols] = g[:384]
        send_ref[:, cols] = g[384:]
        return 0

    lax.fori_loop(0, 3, weight_grad, 0)
    lhs_ref[...] = dot(pick, attn_ref[...], 0, 1).astype(BF)
    g = dot(lhs_ref[...], gy_ref[...], 1, 0).astype(BF)
    keep_ref[:, 3 * D :] = g[:384]
    send_ref[:, 3 * D :] = g[384:]


def token_kernel(recv_ref, gain_ref, dqkv_ref, wqkv_ref, ret_ref):
    order = onehot(position_order())
    gn = dot(dqkv_ref[...], wqkv_ref[...], 1, 1).astype(BF)
    gn = dot(order, gn, 0, 0)
    _, inv_rms, unit = normalise(recv_ref[:, 0].reshape(TOK, D))
    g = jnp.sum(gn * unit, axis=0, keepdims=True)
    dunit = gn * gain_ref[...]
    back = inv_rms * (dunit - unit * jnp.mean(dunit * unit, axis=-1, keepdims=True))
    gy = recv_ref[:, 1].reshape(TOK, D).astype(F32)
    grad = (gy + back).astype(BF)
    for l in range(6):
        ret_ref[:, l * 16 : l * 16 + 16] = grad[:, l * 128 : l * 128 + 128].reshape(32, 16, 128)
    k = lax.broadcasted_iota(jnp.int32, (32, 8, 128), 0) * 24
    lane = lax.broadcasted_iota(jnp.int32, (32, 8, 128), 2)
    own = jnp.zeros((32, 8, 128), F32)
    for l in range(6):
        f = lane + l * 128
        part = g[:, l * 128 : l * 128 + 128].reshape(1, 1, 128)
        own = own + jnp.where(jnp.logical_and(f >= k, f < k + 24), part, 0.0)
    high = own.astype(BF).astype(F32)
    mid = (own - high).astype(BF).astype(F32)
    row = lax.broadcasted_iota(jnp.int32, (32, 8, 128), 1)
    low = own - high - mid
    terms = jnp.where(row == 0, high, jnp.where(row == 1, mid, jnp.where(row == 2, low, 0.0)))
    ret_ref[:, 96:] = terms.astype(BF)


def mixed_kernel(recv_ref, attn_ref, wout_ref, grad_ref, ret_hbm, ret_ref, sems):
    store_g = pltpu.make_async_copy(grad_ref, ret_hbm.at[:, 96:], sems.at[0])
    store_g.start()
    attn = dot(onehot(position_order()), attn_ref[...], 0, 0).astype(BF)
    proj = dot(attn, wout_ref[...], 1, 0).astype(BF)
    mixed = (recv_ref[:, 0].reshape(TOK, D).astype(F32) + proj.astype(F32)).astype(BF)
    for l in range(6):
        ret_ref[:, l * 16 : l * 16 + 16] = mixed[:, l * 128 : l * 128 + 128].reshape(32, 16, 128)
    store_m = pltpu.make_async_copy(ret_ref, ret_hbm.at[:, :96], sems.at[1])
    store_m.start()
    store_g.wait()
    store_m.wait()


def pair_sum_kernel(a_ref, b_ref, o0, o1, o2, o3):
    for n, o in enumerate((o0, o1, o2, o3)):
        rows = slice(n * 96, n * 96 + 96)
        o[...] = (a_ref[rows].astype(F32) + b_ref[rows].astype(F32)).astype(BF)


def ring_sum_kernel(a, b, c, d, o, sum_ref, out_ref):
    sum_ref[...] = (a[...].astype(F32) + b[...].astype(F32)) + (
        c[...].astype(F32) + d[...].astype(F32)
    )
    for k in range(16):
        for l in range(24):
            out_ref[k, l * 6 : l * 6 + 6] = sum_ref[k * 6 : k * 6 + 6, l * 128 : l * 128 + 128]
    o[...] = out_ref[...].astype(BF)


def final_kernel(first_ref, in_ref, g0, g1, g2, g3, qkv_ref, out_ref, gain_ref, sum_ref):
    sum_ref[...] = jnp.sum(in_ref[...].astype(F32), axis=0)
    for l in range(24):
        v = sum_ref[l * 6 : l * 6 + 6]
        if l < 18:
            qkv_ref[:, l * 128 : l * 128 + 128] = v
        else:
            out_ref[:, (l - 18) * 128 : (l - 17) * 128] = v
    g = (g0[...] + g1[...]) + (g2[...] + g3[...])
    r = lax.broadcasted_iota(jnp.int32, (8, 128), 0)
    lane = lax.broadcasted_iota(jnp.int32, (8, 128), 1)
    mine = jnp.sum(
        jnp.where(lane == ((first_ref[0] + r) & 127), g, 0.0), axis=1, keepdims=True
    )
    gain_ref[...] = jnp.sum(jnp.where(lane == r, mine, 0.0), axis=0, keepdims=True)[:, :6]


def params(mb):
    return pltpu.CompilerParams(vmem_limit_bytes=mb * MB)


def cost(flops, nbytes):
    return pl.CostEstimate(flops=int(flops), bytes_accessed=int(nbytes), transcendentals=0)


def shape(*dims, dtype=BF):
    return jax.ShapeDtypeStruct(dims, dtype)


HBM = pl.BlockSpec(memory_space=pltpu.HBM)
VM = pl.BlockSpec(memory_space=pltpu.VMEM)
DMA = pltpu.SemaphoreType.DMA


def per_device(tokens, cotangent, lesion, w_qkv, w_out, norm_gain):
    gain = norm_gain.reshape(1, D)
    depth = lax.axis_index("depth")
    mod = lax.axis_index("mod")
    feat = lax.dynamic_slice(jnp.asarray(FEATURES), ((depth & 1) * 4 + (mod & 3), 0), (1, D))
    first = ((depth * 8 + mod) * 6).astype(jnp.int32).reshape(1)
    packed = pl.pallas_call(
        pack_kernel, out_shape=shape(32, 2, 16, D), in_specs=[HBM] * 3, out_specs=HBM,
        scratch_shapes=[
            pltpu.VMEM((4, 128, D), BF), pltpu.VMEM((4, 128, D), BF), pltpu.VMEM((4, 128), jnp.int32),
            pltpu.VMEM((2, 32, 16, D), BF), DMA((5,)),
        ],
        compiler_params=params(60), cost_estimate=cost(1e9, 4e6), name="pack",
    )(tokens, cotangent, lesion)
    recv = lax.all_to_all(packed, AXES, 0, 0, tiled=True, axis_index_groups=PLANE)
    keep, send, attn, dqkv = pl.pallas_call(
        main_kernel,
        out_shape=(shape(384, 4 * D), shape(384, 4 * D), shape(TOK, D), shape(TOK, 3 * D)),
        in_specs=[HBM, VM, VM, HBM, HBM],
        scratch_shapes=[
            pltpu.VMEM((32, 2, 16, D), BF), pltpu.VMEM((D, 3 * D), BF), pltpu.VMEM((D, D), BF),
            pltpu.VMEM((TOK, 3 * D), BF), pltpu.VMEM((TOK, D), BF), pltpu.VMEM((TOK, D), BF),
            pltpu.VMEM((TOK, D), BF), pltpu.VMEM((D, TOK), BF), DMA((3,)),
        ],
        compiler_params=params(MAIN_MB), cost_estimate=cost(1e10, 1.5e7), name="main",
    )(recv, gain, feat, w_qkv, w_out)
    got = lax.ppermute(send, AXES, CORE_SWAP)
    grads = pl.pallas_call(
        token_kernel, out_shape=shape(32, 104, 128),
        compiler_params=params(TOKEN_MB), cost_estimate=cost(2.8e9, 9e6), name="token_grads",
    )(recv, gain, dqkv, w_qkv)
    quarters = pl.pallas_call(
        pair_sum_kernel, out_shape=tuple(shape(96, 4 * D) for _ in range(4)),
        compiler_params=params(16), cost_estimate=cost(1e6, 7e6), name="pair_sum",
    )(keep, got)
    q0, q1, q2, q3, attn, grads = lax.optimization_barrier((*quarters, attn, grads))
    moved = [lax.ppermute(q, AXES, y_shift(s)) for s, q in ((1, q1), (2, q2), (3, q3))]
    ret = pl.pallas_call(
        mixed_kernel, out_shape=shape(32, 200, 128), out_specs=HBM,
        scratch_shapes=[pltpu.VMEM((32, 96, 128), BF), DMA((2,))],
        compiler_params=params(16), cost_estimate=cost(1e9, 5e6), name="mixed",
    )(recv, attn, w_out, grads)
    back = lax.all_to_all(ret, AXES, 0, 0, tiled=True, axis_index_groups=PLANE)
    mine = pl.pallas_call(
        ring_sum_kernel, out_shape=shape(16, 144, 128),
        scratch_shapes=[pltpu.VMEM((96, 4 * D), F32), pltpu.VMEM((16, 144, 128), F32)],
        compiler_params=params(16), cost_estimate=cost(1e6, 3e6), name="ring_sum",
    )(q0, *moved)
    mixed, grad_tokens, gain_part = pl.pallas_call(
        unpack_kernel,
        out_shape=(shape(4, 128, D), shape(4, 128, D), shape(8, 128, dtype=F32)),
        compiler_params=params(20), cost_estimate=cost(1e9, 4e6), name="unpack",
    )(back)
    last = lax.all_to_all(mine, AXES, 0, 0, tiled=True, axis_index_groups=CHIPS)
    gains = [gain_part] + [lax.ppermute(gain_part, AXES, y_shift(s)) for s in range(1, 4)]
    grad_qkv, grad_out, grad_gain = pl.pallas_call(
        final_kernel,
        out_shape=(shape(6, 3 * D, dtype=F32), shape(6, D, dtype=F32), shape(1, 6, dtype=F32)),
        in_specs=[pl.BlockSpec(memory_space=pltpu.SMEM)] + [VM] * 5,
        scratch_shapes=[pltpu.VMEM((144, 128), F32)],
        compiler_params=params(16), cost_estimate=cost(1e6, 1e6), name="final",
    )(first, last, *gains)
    return mixed, grad_tokens, grad_qkv, grad_out, grad_gain.reshape(6)


def solution(mesh):
    in_specs = (P("depth", "mod", None), P("depth", "mod", None), P("depth", "mod"), P(), P(), P())
    out_specs = (
        P("depth", "mod", None),
        P("depth", "mod", None),
        P(("depth", "mod"), None),
        P(("depth", "mod"), None),
        P(("depth", "mod")),
    )
    return jax.shard_map(
        per_device, mesh=mesh, in_specs=in_specs, out_specs=out_specs, check_vma=False
    )
```

```python
import jax
import jax.numpy as jnp
import numpy as np
from jax import lax
from jax.experimental import pallas as pl
from jax.experimental.pallas import tpu as pltpu
from jax.sharding import PartitionSpec as P

HEADS = 12
HEAD_DIM = 64
EPS = 1e-06
LESION_GAIN = 3.0
D = 768
TOK = 512
AXES = ("depth", "mod")
BF = jnp.bfloat16
F32 = jnp.float32
MB = 1024 * 1024
RING = 2e10
MAIN_MB = 42
TOKEN_MB = 20


def place(xlo, z, c, xhi, y):
    return (xlo * 8 + z * 2 + c) * 8 + xhi * 4 + y


def parts_of(i):
    d, m = divmod(i, 8)
    return d // 8, (d // 2) % 4, d % 2, m // 4, m % 4


PLANE = [
    [place(a, z, c, b, y) for a in range(2) for z in range(4) for c in range(2) for b in range(2)]
    for y in range(4)
]
CHIPS = [
    [place(a, z, c, b, y) for a in range(2) for z in range(4) for b in range(2)]
    for c in range(2)
    for y in range(4)
]
CORE_SWAP = [(i, i ^ 8) for i in range(128)]


def y_shift(s):
    out = []
    for i in range(128):
        a, z, c, b, y = parts_of(i)
        out.append((i, place(a, z, c, b, (y + s) % 4)))
    return out


def feature_table():
    table = np.zeros((8, D), np.int32)
    for c in range(2):
        for y in range(4):
            n = 0
            for rc in range(2):
                for ry in range(4):
                    for a in range(2):
                        for z in range(4):
                            for b in range(2):
                                i = place(a, z, c ^ rc, b, (y + ry) % 4)
                                for r in range(6):
                                    table[c * 4 + y, n] = 6 * i + r
                                    n += 1
    return table


FEATURES = feature_table()


def dot(a, b, ca, cb):
    return lax.dot_general(a, b, (((ca,), (cb,)), ((), ())), preferred_element_type=F32)


def send_order():
    i = lax.broadcasted_iota(jnp.int32, (TOK, TOK), 0)
    s = lax.broadcasted_iota(jnp.int32, (TOK, TOK), 1)
    src = ((i >> 2) & 3) * 128 + (i >> 4) * 4 + (i & 3)
    return s == src


def position_order():
    i = lax.broadcasted_iota(jnp.int32, (TOK, TOK), 0)
    s = lax.broadcasted_iota(jnp.int32, (TOK, TOK), 1)
    return s == (i & 127) * 4 + (i >> 7)


def onehot(mask):
    return jnp.where(mask, 1.0, 0.0).astype(BF)


def pack_kernel(tok_hbm, cot_hbm, les_hbm, out_hbm, tok_ref, cot_ref, les_ref, out_ref, sems):
    loads = [
        pltpu.make_async_copy(src, dst, sems.at[n])
        for n, (src, dst) in enumerate(
            ((les_hbm, les_ref), (tok_hbm, tok_ref), (cot_hbm, cot_ref))
        )
    ]
    for c in loads:
        c.start()
    mask = send_order()
    plain = onehot(mask)
    loads[0].wait()
    weight = 1.0 + LESION_GAIN * les_ref[...].astype(F32)
    row = jnp.concatenate([weight[d : d + 1, :] for d in range(4)], axis=1)
    scaled = jnp.where(mask, row, 0.0).astype(BF)
    loads[1].wait()
    t = dot(plain, tok_ref[...].reshape(TOK, D), 1, 0).astype(BF)
    out_ref[0] = t.reshape(32, 16, D)
    store_t = pltpu.make_async_copy(out_ref.at[0], out_hbm.at[:, 0], sems.at[3])
    store_t.start()
    loads[2].wait()
    g = dot(scaled, cot_ref[...].reshape(TOK, D), 1, 0).astype(BF)
    out_ref[1] = g.reshape(32, 16, D)
    store_g = pltpu.make_async_copy(out_ref.at[1], out_hbm.at[:, 1], sems.at[4])
    store_g.start()
    store_t.wait()
    store_g.wait()


def unpack_kernel(in_ref, mixed_ref, grad_ref, gain_ref):
    sel = onehot(send_order())
    for n, out in enumerate((mixed_ref, grad_ref)):
        base = n * 96
        x = jnp.concatenate(
            [in_ref[:, base + l * 16 : base + l * 16 + 16].reshape(TOK, 128) for l in range(6)],
            axis=1,
        )
        out[...] = dot(sel, x, 0, 0).astype(BF).reshape(4, 128, D)
    g = jnp.sum(in_ref[:, 192:].astype(F32), axis=0)
    gain_ref[...] = jnp.broadcast_to(jnp.sum(g, axis=0, keepdims=True), (8, 128))


def normalise(x):
    xf = x.astype(F32)
    inv_rms = lax.rsqrt(jnp.mean(xf * xf, axis=-1, keepdims=True) + EPS)
    return xf, inv_rms, xf * inv_rms


def main_kernel(
    recv_hbm, gain_ref, feat_ref, wqkv_hbm, wout_hbm,
    keep_ref, send_ref, attn_ref, dqkv_ref,
    recv_ref, wqkv_ref, wout_ref, qkv_ref, ga_ref, norm_ref, gy_ref, lhs_ref, sems,
):
    scale = float(HEAD_DIM) ** (-0.5)
    loads = [
        pltpu.make_async_copy(src, dst, sems.at[n])
        for n, (src, dst) in enumerate(
            ((recv_hbm, recv_ref), (wqkv_hbm, wqkv_ref), (wout_hbm, wout_ref))
        )
    ]
    for c in loads:
        c.start()
    order = onehot(position_order())
    loads[0].wait()
    _, _, unit = normalise(recv_ref[:, 0].reshape(TOK, D))
    normed = (unit * gain_ref[...]).astype(BF)
    norm_ref[...] = dot(order, normed, 1, 0).astype(BF)
    gy_ref[...] = dot(order, recv_ref[:, 1].reshape(TOK, D), 1, 0).astype(BF)
    loads[1].wait()

    def project(n, _):
        cols = pl.ds(pl.multiple_of(n * 768, 768), 768)
        qkv_ref[:, cols] = dot(norm_ref[...], wqkv_ref[:, cols], 1, 0).astype(BF)
        return 0

    lax.fori_loop(0, 3, project, 0)
    loads[2].wait()
    ga_ref[...] = dot(gy_ref[...], wout_ref[...], 1, 1).astype(BF)
    first = lax.broadcasted_iota(jnp.int32, (128, 128), 1) < 64

    def split(x):
        zero = jnp.zeros_like(x)
        return jnp.concatenate([jnp.where(first, x, zero), jnp.where(first, zero, x)], axis=0)

    def heads(hp, _):
        base = pl.multiple_of(hp * 128, 128)
        rows = [slice(p * 128, (p + 1) * 128) for p in range(4)]
        q = [qkv_ref[r, pl.ds(base, 128)] for r in rows]
        kb = [split(qkv_ref[r, pl.ds(base + D, 128)]) for r in rows]
        vb = [split(qkv_ref[r, pl.ds(base + 2 * D, 128)]) for r in rows]
        ga = [ga_ref[r, pl.ds(base, 128)] for r in rows]
        s = [dot(kb[p], q[p], 1, 1).reshape(2, 128, 128) for p in range(4)]
        dp = [dot(vb[p], ga[p], 1, 1).reshape(2, 128, 128) for p in range(4)]
        pb, ds = [], []
        for p in range(4):
            sp = s[p] * scale
            e = jnp.exp(sp - jnp.max(sp, axis=1, keepdims=True))
            probs = e * (1.0 / jnp.sum(e, axis=1, keepdims=True))
            delta = jnp.sum(probs * dp[p], axis=1, keepdims=True)
            ds.append((probs * (dp[p] - delta) * scale).astype(BF).reshape(256, 128))
            pb.append(probs.astype(BF).reshape(256, 128))
        for p in range(4):
            attn_ref[rows[p], pl.ds(base, 128)] = dot(pb[p], vb[p], 0, 0).astype(BF)
            dqkv_ref[rows[p], pl.ds(base, 128)] = dot(ds[p], kb[p], 0, 0).astype(BF)
            dk = dot(ds[p], q[p], 1, 0)
            dv = dot(pb[p], ga[p], 1, 0)
            dqkv_ref[rows[p], pl.ds(base + D, 128)] = jnp.where(first, dk[:128], dk[128:]).astype(BF)
            dqkv_ref[rows[p], pl.ds(base + 2 * D, 128)] = jnp.where(first, dv[:128], dv[128:]).astype(BF)
        return 0

    lax.fori_loop(0, HEADS // 2, heads, 0)
    pick = onehot(lax.broadcasted_iota(jnp.int32, (D, D), 0) == feat_ref[...])
    lhs_ref[...] = dot(pick, norm_ref[...], 0, 1).astype(BF)

    def weight_grad(n, _):
        cols = pl.ds(pl.multiple_of(n * 768, 768), 768)
        g = dot(lhs_ref[...], dqkv_ref[:, cols], 1, 0).astype(BF)
        keep_ref[:, cols] = g[:384]
        send_ref[:, cols] = g[384:]
        return 0

    lax.fori_loop(0, 3, weight_grad, 0)
    lhs_ref[...] = dot(pick, attn_ref[...], 0, 1).astype(BF)
    g = dot(lhs_ref[...], gy_ref[...], 1, 0).astype(BF)
    keep_ref[:, 3 * D :] = g[:384]
    send_ref[:, 3 * D :] = g[384:]


def token_kernel(recv_ref, gain_ref, dqkv_ref, wqkv_ref, ret_ref):
    order = onehot(position_order())
    gn = dot(dqkv_ref[...], wqkv_ref[...], 1, 1).astype(BF)
    gn = dot(order, gn, 0, 0)
    _, inv_rms, unit = normalise(recv_ref[:, 0].reshape(TOK, D))
    g = jnp.sum(gn * unit, axis=0, keepdims=True)
    dunit = gn * gain_ref[...]
    back = inv_rms * (dunit - unit * jnp.mean(dunit * unit, axis=-1, keepdims=True))
    gy = recv_ref[:, 1].reshape(TOK, D).astype(F32)
    grad = (gy + back).astype(BF)
    for l in range(6):
        ret_ref[:, l * 16 : l * 16 + 16] = grad[:, l * 128 : l * 128 + 128].reshape(32, 16, 128)
    k = lax.broadcasted_iota(jnp.int32, (32, 8, 128), 0) * 24
    lane = lax.broadcasted_iota(jnp.int32, (32, 8, 128), 2)
    own = jnp.zeros((32, 8, 128), F32)
    for l in range(6):
        f = lane + l * 128
        part = g[:, l * 128 : l * 128 + 128].reshape(1, 1, 128)
        own = own + jnp.where(jnp.logical_and(f >= k, f < k + 24), part, 0.0)
    high = own.astype(BF).astype(F32)
    mid = (own - high).astype(BF).astype(F32)
    row = lax.broadcasted_iota(jnp.int32, (32, 8, 128), 1)
    low = own - high - mid
    terms = jnp.where(row == 0, high, jnp.where(row == 1, mid, jnp.where(row == 2, low, 0.0)))
    ret_ref[:, 96:] = terms.astype(BF)


def mixed_kernel(recv_ref, attn_ref, wout_ref, grad_ref, ret_hbm, ret_ref, sems):
    store_g = pltpu.make_async_copy(grad_ref, ret_hbm.at[:, 96:], sems.at[0])
    store_g.start()
    attn = dot(onehot(position_order()), attn_ref[...], 0, 0).astype(BF)
    proj = dot(attn, wout_ref[...], 1, 0).astype(BF)
    mixed = (recv_ref[:, 0].reshape(TOK, D).astype(F32) + proj.astype(F32)).astype(BF)
    for l in range(6):
        ret_ref[:, l * 16 : l * 16 + 16] = mixed[:, l * 128 : l * 128 + 128].reshape(32, 16, 128)
    store_m = pltpu.make_async_copy(ret_ref, ret_hbm.at[:, :96], sems.at[1])
    store_m.start()
    store_g.wait()
    store_m.wait()


def pair_sum_kernel(a_ref, b_ref, o0, o1, o2, o3):
    for n, o in enumerate((o0, o1, o2, o3)):
        rows = slice(n * 96, n * 96 + 96)
        o[...] = (a_ref[rows].astype(F32) + b_ref[rows].astype(F32)).astype(BF)


def ring_sum_kernel(a, b, c, d, o, sum_ref, out_ref):
    sum_ref[...] = (a[...].astype(F32) + b[...].astype(F32)) + (
        c[...].astype(F32) + d[...].astype(F32)
    )
    for k in range(16):
        for l in range(24):
            out_ref[k, l * 6 : l * 6 + 6] = sum_ref[k * 6 : k * 6 + 6, l * 128 : l * 128 + 128]
    o[...] = out_ref[...].astype(BF)


def final_kernel(first_ref, in_ref, g0, g1, g2, g3, qkv_ref, out_ref, gain_ref, sum_ref):
    sum_ref[...] = jnp.sum(in_ref[...].astype(F32), axis=0)
    for l in range(24):
        v = sum_ref[l * 6 : l * 6 + 6]
        if l < 18:
            qkv_ref[:, l * 128 : l * 128 + 128] = v
        else:
            out_ref[:, (l - 18) * 128 : (l - 17) * 128] = v
    g = (g0[...] + g1[...]) + (g2[...] + g3[...])
    r = lax.broadcasted_iota(jnp.int32, (8, 128), 0)
    lane = lax.broadcasted_iota(jnp.int32, (8, 128), 1)
    mine = jnp.sum(
        jnp.where(lane == ((first_ref[0] + r) & 127), g, 0.0), axis=1, keepdims=True
    )
    gain_ref[...] = jnp.sum(jnp.where(lane == r, mine, 0.0), axis=0, keepdims=True)[:, :6]


def params(mb):
    return pltpu.CompilerParams(vmem_limit_bytes=mb * MB)


def cost(flops, nbytes):
    return pl.CostEstimate(flops=int(flops), bytes_accessed=int(nbytes), transcendentals=0)


def shape(*dims, dtype=BF):
    return jax.ShapeDtypeStruct(dims, dtype)


HBM = pl.BlockSpec(memory_space=pltpu.HBM)
VM = pl.BlockSpec(memory_space=pltpu.VMEM)
DMA = pltpu.SemaphoreType.DMA


def per_device(tokens, cotangent, lesion, w_qkv, w_out, norm_gain):
    gain = norm_gain.reshape(1, D)
    depth = lax.axis_index("depth")
    mod = lax.axis_index("mod")
    feat = lax.dynamic_slice(jnp.asarray(FEATURES), ((depth & 1) * 4 + (mod & 3), 0), (1, D))
    first = ((depth * 8 + mod) * 6).astype(jnp.int32).reshape(1)
    packed = pl.pallas_call(
        pack_kernel, out_shape=shape(32, 2, 16, D), in_specs=[HBM] * 3, out_specs=HBM,
        scratch_shapes=[
            pltpu.VMEM((4, 128, D), BF), pltpu.VMEM((4, 128, D), BF), pltpu.VMEM((4, 128), jnp.int32),
            pltpu.VMEM((2, 32, 16, D), BF), DMA((5,)),
        ],
        compiler_params=params(60), cost_estimate=cost(1e9, 4e6), name="pack",
    )(tokens, cotangent, lesion)
    recv = lax.all_to_all(packed, AXES, 0, 0, tiled=True, axis_index_groups=PLANE)
    keep, send, attn, dqkv = pl.pallas_call(
        main_kernel,
        out_shape=(shape(384, 4 * D), shape(384, 4 * D), shape(TOK, D), shape(TOK, 3 * D)),
        in_specs=[HBM, VM, VM, HBM, HBM],
        scratch_shapes=[
            pltpu.VMEM((32, 2, 16, D), BF), pltpu.VMEM((D, 3 * D), BF), pltpu.VMEM((D, D), BF),
            pltpu.VMEM((TOK, 3 * D), BF), pltpu.VMEM((TOK, D), BF), pltpu.VMEM((TOK, D), BF),
            pltpu.VMEM((TOK, D), BF), pltpu.VMEM((D, TOK), BF), DMA((3,)),
        ],
        compiler_params=params(MAIN_MB), cost_estimate=cost(1e10, 1.5e7), name="main",
    )(recv, gain, feat, w_qkv, w_out)
    got = lax.ppermute(send, AXES, CORE_SWAP)
    grads = pl.pallas_call(
        token_kernel, out_shape=shape(32, 104, 128),
        compiler_params=params(TOKEN_MB), cost_estimate=cost(2.8e9, 9e6), name="token_grads",
    )(recv, gain, dqkv, w_qkv)
    ret = pl.pallas_call(
        mixed_kernel, out_shape=shape(32, 200, 128), out_specs=HBM,
        scratch_shapes=[pltpu.VMEM((32, 96, 128), BF), DMA((2,))],
        compiler_params=params(16), cost_estimate=cost(1e9, 5e6), name="mixed",
    )(recv, attn, w_out, grads)
    quarters = pl.pallas_call(
        pair_sum_kernel, out_shape=tuple(shape(96, 4 * D) for _ in range(4)),
        compiler_params=params(16), cost_estimate=cost(1e6, 7e6), name="pair_sum",
    )(keep, got)
    q0, q1, q2, q3, ret = lax.optimization_barrier((*quarters, ret))
    moved = [lax.ppermute(q, AXES, y_shift(s)) for s, q in ((1, q1), (2, q2), (3, q3))]
    back = lax.all_to_all(ret, AXES, 0, 0, tiled=True, axis_index_groups=PLANE)
    mine = pl.pallas_call(
        ring_sum_kernel, out_shape=shape(16, 144, 128),
        scratch_shapes=[pltpu.VMEM((96, 4 * D), F32), pltpu.VMEM((16, 144, 128), F32)],
        compiler_params=params(16), cost_estimate=cost(RING, 3e6), name="ring_sum",
    )(q0, *moved)
    mixed, grad_tokens, gain_part = pl.pallas_call(
        unpack_kernel,
        out_shape=(shape(4, 128, D), shape(4, 128, D), shape(8, 128, dtype=F32)),
        compiler_params=params(20), cost_estimate=cost(1e9, 4e6), name="unpack",
    )(back)
    last = lax.all_to_all(mine, AXES, 0, 0, tiled=True, axis_index_groups=CHIPS)
    gains = [gain_part] + [lax.ppermute(gain_part, AXES, y_shift(s)) for s in range(1, 4)]
    grad_qkv, grad_out, grad_gain = pl.pallas_call(
        final_kernel,
        out_shape=(shape(6, 3 * D, dtype=F32), shape(6, D, dtype=F32), shape(1, 6, dtype=F32)),
        in_specs=[pl.BlockSpec(memory_space=pltpu.SMEM)] + [VM] * 5,
        scratch_shapes=[pltpu.VMEM((144, 128), F32)],
        compiler_params=params(16), cost_estimate=cost(1e6, 1e6), name="final",
    )(first, last, *gains)
    return mixed, grad_tokens, grad_qkv, grad_out, grad_gain.reshape(6)


def solution(mesh):
    in_specs = (P("depth", "mod", None), P("depth", "mod", None), P("depth", "mod"), P(), P(), P())
    out_specs = (
        P("depth", "mod", None),
        P("depth", "mod", None),
        P(("depth", "mod"), None),
        P(("depth", "mod"), None),
        P(("depth", "mod")),
    )
    return jax.shard_map(
        per_device, mesh=mesh, in_specs=in_specs, out_specs=out_specs, check_vma=False
    )
```

```python
import jax
import jax.numpy as jnp
import numpy as np
from jax import lax
from jax.experimental import pallas as pl
from jax.experimental.pallas import tpu as pltpu
from jax.sharding import PartitionSpec as P

HEADS = 12
HEAD_DIM = 64
EPS = 1e-06
LESION_GAIN = 3.0
D = 768
TOK = 512
AXES = ("depth", "mod")
BF = jnp.bfloat16
F32 = jnp.float32
MB = 1024 * 1024
RING = 2e10
MAIN_MB = 42
TOKEN_MB = 20


def place(xlo, z, c, xhi, y):
    return (xlo * 8 + z * 2 + c) * 8 + xhi * 4 + y


def parts_of(i):
    d, m = divmod(i, 8)
    return d // 8, (d // 2) % 4, d % 2, m // 4, m % 4


PLANE = [
    [place(a, z, c, b, y) for a in range(2) for z in range(4) for c in range(2) for b in range(2)]
    for y in range(4)
]
CHIPS = [
    [place(a, z, c, b, y) for a in range(2) for z in range(4) for b in range(2)]
    for c in range(2)
    for y in range(4)
]
CORE_SWAP = [(i, i ^ 8) for i in range(128)]


def y_shift(s):
    out = []
    for i in range(128):
        a, z, c, b, y = parts_of(i)
        out.append((i, place(a, z, c, b, (y + s) % 4)))
    return out


def feature_table():
    table = np.zeros((8, D), np.int32)
    for c in range(2):
        for y in range(4):
            n = 0
            for rc in range(2):
                for ry in range(4):
                    for a in range(2):
                        for z in range(4):
                            for b in range(2):
                                i = place(a, z, c ^ rc, b, (y + ry) % 4)
                                for r in range(6):
                                    table[c * 4 + y, n] = 6 * i + r
                                    n += 1
    return table


FEATURES = feature_table()


def dot(a, b, ca, cb):
    return lax.dot_general(a, b, (((ca,), (cb,)), ((), ())), preferred_element_type=F32)


def onehot(mask):
    return jnp.where(mask, 1.0, 0.0).astype(BF)


def rows_and_columns():
    i = lax.broadcasted_iota(jnp.int32, (128, 128), 0)
    return i, lax.broadcasted_iota(jnp.int32, (128, 128), 1)


def send_order():
    i, s = rows_and_columns()
    return s == ((i >> 2) & 3) * 32 + (i >> 4) * 4 + (i & 3)


def position_order():
    i, s = rows_and_columns()
    return onehot(s == ((i >> 2) & 7) * 16 + (i & 3) * 4 + (i >> 5))


def by_position(x):
    order = position_order()
    parts = [dot(order, x[n * 128 : n * 128 + 128], 1, 0).astype(BF) for n in range(4)]
    return jnp.concatenate(
        [parts[n][p * 32 : p * 32 + 32] for p in range(4) for n in range(4)], axis=0
    )


def by_source(x):
    order = position_order()
    parts = [
        jnp.concatenate([x[p * 128 + n * 32 : p * 128 + n * 32 + 32] for p in range(4)], axis=0)
        for n in range(4)
    ]
    return jnp.concatenate([dot(order, part, 0, 0).astype(BF) for part in parts], axis=0)


def pack_kernel(tok_hbm, cot_hbm, les_hbm, out_hbm, tok_ref, cot_ref, les_ref, out_ref, sems):
    loads = [
        pltpu.make_async_copy(src, dst, sems.at[n])
        for n, (src, dst) in enumerate(
            ((les_hbm, les_ref), (tok_hbm, tok_ref), (cot_hbm, cot_ref))
        )
    ]
    for c in loads:
        c.start()
    mask = send_order()
    plain = onehot(mask)

    def block(ref, n):
        return jnp.concatenate([ref[d, n * 32 : n * 32 + 32] for d in range(4)], axis=0)

    loads[1].wait()
    for n in range(4):
        t = dot(plain, block(tok_ref, n), 1, 0).astype(BF)
        out_ref[0, n * 8 : n * 8 + 8] = t.reshape(8, 16, D)
    store_t = pltpu.make_async_copy(out_ref.at[0], out_hbm.at[:, 0], sems.at[3])
    store_t.start()
    loads[0].wait()
    weight = 1.0 + LESION_GAIN * les_ref[...].astype(F32)
    loads[2].wait()
    for n in range(4):
        row = jnp.concatenate([weight[d : d + 1, n * 32 : n * 32 + 32] for d in range(4)], axis=1)
        scaled = jnp.where(mask, row, 0.0).astype(BF)
        g = dot(scaled, block(cot_ref, n), 1, 0).astype(BF)
        out_ref[1, n * 8 : n * 8 + 8] = g.reshape(8, 16, D)
    store_g = pltpu.make_async_copy(out_ref.at[1], out_hbm.at[:, 1], sems.at[4])
    store_g.start()
    store_t.wait()
    store_g.wait()


def unpack_kernel(in_ref, mixed_ref, grad_ref, gain_ref):
    sel = onehot(send_order())
    for n, out in enumerate((mixed_ref, grad_ref)):
        base = n * 96
        x = jnp.concatenate(
            [in_ref[:, base + l * 16 : base + l * 16 + 16].reshape(TOK, 128) for l in range(6)],
            axis=1,
        )
        for b in range(4):
            y = dot(sel, x[b * 128 : b * 128 + 128], 0, 0).astype(BF)
            for d in range(4):
                out[d, b * 32 : b * 32 + 32] = y[d * 32 : d * 32 + 32]
    g = jnp.sum(in_ref[:, 192:].astype(F32), axis=0)
    gain_ref[...] = jnp.broadcast_to(jnp.sum(g, axis=0, keepdims=True), (8, 128))


def normalise(x):
    xf = x.astype(F32)
    inv_rms = lax.rsqrt(jnp.mean(xf * xf, axis=-1, keepdims=True) + EPS)
    return xf, inv_rms, xf * inv_rms


def main_kernel(
    recv_hbm, gain_ref, feat_ref, wqkv_hbm, wout_hbm,
    keep_ref, send_ref, attn_ref, dqkv_ref,
    recv_ref, wqkv_ref, wout_ref, qkv_ref, ga_ref, norm_ref, gy_ref, lhs_ref, sems,
):
    scale = float(HEAD_DIM) ** (-0.5)
    loads = [
        pltpu.make_async_copy(src, dst, sems.at[n])
        for n, (src, dst) in enumerate(
            ((recv_hbm, recv_ref), (wout_hbm, wout_ref), (wqkv_hbm, wqkv_ref))
        )
    ]
    for c in loads:
        c.start()
    loads[0].wait()
    _, _, unit = normalise(recv_ref[:, 0].reshape(TOK, D))
    normed = (unit * gain_ref[...]).astype(BF)
    norm_ref[...] = by_position(normed)
    gy_ref[...] = by_position(recv_ref[:, 1].reshape(TOK, D))
    loads[1].wait()
    ga_ref[...] = dot(gy_ref[...], wout_ref[...], 1, 1).astype(BF)
    loads[2].wait()

    def project(n, _):
        cols = pl.ds(pl.multiple_of(n * 768, 768), 768)
        qkv_ref[:, cols] = dot(norm_ref[...], wqkv_ref[:, cols], 1, 0).astype(BF)
        return 0

    lax.fori_loop(0, 3, project, 0, unroll=True)
    first = lax.broadcasted_iota(jnp.int32, (128, 128), 1) < 64

    def split(x):
        zero = jnp.zeros_like(x)
        return jnp.concatenate([jnp.where(first, x, zero), jnp.where(first, zero, x)], axis=0)

    def stack(x):
        return jnp.concatenate([x[:, :128], x[:, 128:]], axis=0)

    def heads(hp, _):
        base = pl.multiple_of(hp * 128, 128)
        rows = [slice(p * 128, (p + 1) * 128) for p in range(4)]
        q = [qkv_ref[r, pl.ds(base, 128)] for r in rows]
        k = [qkv_ref[r, pl.ds(base + D, 128)] for r in rows]
        v = [qkv_ref[r, pl.ds(base + 2 * D, 128)] for r in rows]
        qb = [split(x) for x in q]
        gb = [split(ga_ref[r, pl.ds(base, 128)]) for r in rows]
        s = [dot(k[p], qb[p], 1, 1) for p in range(4)]
        dp = [dot(v[p], gb[p], 1, 1) for p in range(4)]
        pb, ds = [], []
        for p in range(4):
            sp = s[p] * scale
            e = jnp.exp(sp - jnp.max(sp, axis=0, keepdims=True))
            probs = e * (1.0 / jnp.sum(e, axis=0, keepdims=True))
            delta = jnp.sum(probs * dp[p], axis=0, keepdims=True)
            ds.append((probs * (dp[p] - delta) * scale).astype(BF))
            pb.append(probs.astype(BF))
        for p in range(4):
            attn_ref[rows[p], pl.ds(base, 128)] = dot(stack(pb[p]), split(v[p]), 0, 0).astype(BF)
            dqkv_ref[rows[p], pl.ds(base, 128)] = dot(stack(ds[p]), split(k[p]), 0, 0).astype(BF)
            dqkv_ref[rows[p], pl.ds(base + D, 128)] = dot(ds[p], qb[p], 1, 0).astype(BF)
            dqkv_ref[rows[p], pl.ds(base + 2 * D, 128)] = dot(pb[p], gb[p], 1, 0).astype(BF)
        return 0

    lax.fori_loop(0, HEADS // 2, heads, 0, unroll=True)
    pick = onehot(lax.broadcasted_iota(jnp.int32, (D, D), 0) == feat_ref[...])
    lhs_ref[...] = dot(pick, norm_ref[...], 0, 1).astype(BF)

    def weight_grad(n, _):
        cols = pl.ds(pl.multiple_of(n * 768, 768), 768)
        g = dot(lhs_ref[...], dqkv_ref[:, cols], 1, 0).astype(BF)
        keep_ref[:, cols] = g[:384]
        send_ref[:, cols] = g[384:]
        return 0

    lax.fori_loop(0, 3, weight_grad, 0, unroll=True)
    lhs_ref[...] = dot(pick, attn_ref[...], 0, 1).astype(BF)
    g = dot(lhs_ref[...], gy_ref[...], 1, 0).astype(BF)
    keep_ref[:, 3 * D :] = g[:384]
    send_ref[:, 3 * D :] = g[384:]


def token_kernel(recv_ref, gain_ref, dqkv_ref, wqkv_ref, ret_ref):
    gn = dot(dqkv_ref[...], wqkv_ref[...], 1, 1).astype(BF)
    gn = by_source(gn).astype(F32)
    _, inv_rms, unit = normalise(recv_ref[:, 0].reshape(TOK, D))
    g = jnp.sum(gn * unit, axis=0, keepdims=True)
    dunit = gn * gain_ref[...]
    back = inv_rms * (dunit - unit * jnp.mean(dunit * unit, axis=-1, keepdims=True))
    gy = recv_ref[:, 1].reshape(TOK, D).astype(F32)
    grad = (gy + back).astype(BF)
    for l in range(6):
        ret_ref[:, l * 16 : l * 16 + 16] = grad[:, l * 128 : l * 128 + 128].reshape(32, 16, 128)
    k = lax.broadcasted_iota(jnp.int32, (32, 8, 128), 0) * 24
    lane = lax.broadcasted_iota(jnp.int32, (32, 8, 128), 2)
    own = jnp.zeros((32, 8, 128), F32)
    for l in range(6):
        f = lane + l * 128
        part = g[:, l * 128 : l * 128 + 128].reshape(1, 1, 128)
        own = own + jnp.where(jnp.logical_and(f >= k, f < k + 24), part, 0.0)
    high = own.astype(BF).astype(F32)
    mid = (own - high).astype(BF).astype(F32)
    row = lax.broadcasted_iota(jnp.int32, (32, 8, 128), 1)
    low = own - high - mid
    terms = jnp.where(row == 0, high, jnp.where(row == 1, mid, jnp.where(row == 2, low, 0.0)))
    ret_ref[:, 96:] = terms.astype(BF)


def mixed_kernel(recv_ref, attn_ref, wout_ref, grad_ref, ret_hbm, ret_ref, sems):
    store_g = pltpu.make_async_copy(grad_ref, ret_hbm.at[:, 96:], sems.at[0])
    store_g.start()
    attn = by_source(attn_ref[...])
    proj = dot(attn, wout_ref[...], 1, 0).astype(BF)
    mixed = (recv_ref[:, 0].reshape(TOK, D).astype(F32) + proj.astype(F32)).astype(BF)
    for l in range(6):
        ret_ref[:, l * 16 : l * 16 + 16] = mixed[:, l * 128 : l * 128 + 128].reshape(32, 16, 128)
    store_m = pltpu.make_async_copy(ret_ref, ret_hbm.at[:, :96], sems.at[1])
    store_m.start()
    store_g.wait()
    store_m.wait()


def pair_sum_kernel(a_ref, b_ref, o0, o1, o2, o3):
    for n, o in enumerate((o0, o1, o2, o3)):
        rows = slice(n * 96, n * 96 + 96)
        o[...] = (a_ref[rows].astype(F32) + b_ref[rows].astype(F32)).astype(BF)


def ring_sum_kernel(a, b, c, d, o, sum_ref, out_ref):
    sum_ref[...] = (a[...].astype(F32) + b[...].astype(F32)) + (
        c[...].astype(F32) + d[...].astype(F32)
    )
    for k in range(16):
        for l in range(24):
            out_ref[k, l * 6 : l * 6 + 6] = sum_ref[k * 6 : k * 6 + 6, l * 128 : l * 128 + 128]
    o[...] = out_ref[...].astype(BF)


def final_kernel(first_ref, in_ref, g0, g1, g2, g3, qkv_ref, out_ref, gain_ref, sum_ref):
    sum_ref[...] = jnp.sum(in_ref[...].astype(F32), axis=0)
    for l in range(24):
        v = sum_ref[l * 6 : l * 6 + 6]
        if l < 18:
            qkv_ref[:, l * 128 : l * 128 + 128] = v
        else:
            out_ref[:, (l - 18) * 128 : (l - 17) * 128] = v
    g = (g0[...] + g1[...]) + (g2[...] + g3[...])
    r = lax.broadcasted_iota(jnp.int32, (8, 128), 0)
    lane = lax.broadcasted_iota(jnp.int32, (8, 128), 1)
    mine = jnp.sum(
        jnp.where(lane == ((first_ref[0] + r) & 127), g, 0.0), axis=1, keepdims=True
    )
    gain_ref[...] = jnp.sum(jnp.where(lane == r, mine, 0.0), axis=0, keepdims=True)[:, :6]


def params(mb):
    return pltpu.CompilerParams(vmem_limit_bytes=mb * MB)


def cost(flops, nbytes):
    return pl.CostEstimate(flops=int(flops), bytes_accessed=int(nbytes), transcendentals=0)


def shape(*dims, dtype=BF):
    return jax.ShapeDtypeStruct(dims, dtype)


HBM = pl.BlockSpec(memory_space=pltpu.HBM)
VM = pl.BlockSpec(memory_space=pltpu.VMEM)
DMA = pltpu.SemaphoreType.DMA


def per_device(tokens, cotangent, lesion, w_qkv, w_out, norm_gain):
    gain = norm_gain.reshape(1, D)
    depth = lax.axis_index("depth")
    mod = lax.axis_index("mod")
    feat = lax.dynamic_slice(jnp.asarray(FEATURES), ((depth & 1) * 4 + (mod & 3), 0), (1, D))
    first = ((depth * 8 + mod) * 6).astype(jnp.int32).reshape(1)
    packed = pl.pallas_call(
        pack_kernel, out_shape=shape(32, 2, 16, D), in_specs=[HBM] * 3, out_specs=HBM,
        scratch_shapes=[
            pltpu.VMEM((4, 128, D), BF), pltpu.VMEM((4, 128, D), BF), pltpu.VMEM((4, 128), jnp.int32),
            pltpu.VMEM((2, 32, 16, D), BF), DMA((5,)),
        ],
        compiler_params=params(60), cost_estimate=cost(1e9, 4e6), name="pack",
    )(tokens, cotangent, lesion)
    recv = lax.all_to_all(packed, AXES, 0, 0, tiled=True, axis_index_groups=PLANE)
    keep, send, attn, dqkv = pl.pallas_call(
        main_kernel,
        out_shape=(shape(384, 4 * D), shape(384, 4 * D), shape(TOK, D), shape(TOK, 3 * D)),
        in_specs=[HBM, VM, VM, HBM, HBM],
        scratch_shapes=[
            pltpu.VMEM((32, 2, 16, D), BF), pltpu.VMEM((D, 3 * D), BF), pltpu.VMEM((D, D), BF),
            pltpu.VMEM((TOK, 3 * D), BF), pltpu.VMEM((TOK, D), BF), pltpu.VMEM((TOK, D), BF),
            pltpu.VMEM((TOK, D), BF), pltpu.VMEM((D, TOK), BF), DMA((3,)),
        ],
        compiler_params=params(MAIN_MB), cost_estimate=cost(1e10, 1.5e7), name="main",
    )(recv, gain, feat, w_qkv, w_out)
    got = lax.ppermute(send, AXES, CORE_SWAP)
    grads = pl.pallas_call(
        token_kernel, out_shape=shape(32, 104, 128),
        compiler_params=params(TOKEN_MB), cost_estimate=cost(2.8e9, 9e6), name="token_grads",
    )(recv, gain, dqkv, w_qkv)
    ret = pl.pallas_call(
        mixed_kernel, out_shape=shape(32, 200, 128), out_specs=HBM,
        scratch_shapes=[pltpu.VMEM((32, 96, 128), BF), DMA((2,))],
        compiler_params=params(16), cost_estimate=cost(1e9, 5e6), name="mixed",
    )(recv, attn, w_out, grads)
    quarters = pl.pallas_call(
        pair_sum_kernel, out_shape=tuple(shape(96, 4 * D) for _ in range(4)),
        compiler_params=params(16), cost_estimate=cost(1e6, 7e6), name="pair_sum",
    )(keep, got)
    q0, q1, q2, q3, ret = lax.optimization_barrier((*quarters, ret))
    moved = [lax.ppermute(q, AXES, y_shift(s)) for s, q in ((1, q1), (2, q2), (3, q3))]
    back = lax.all_to_all(ret, AXES, 0, 0, tiled=True, axis_index_groups=PLANE)
    mine = pl.pallas_call(
        ring_sum_kernel, out_shape=shape(16, 144, 128),
        scratch_shapes=[pltpu.VMEM((96, 4 * D), F32), pltpu.VMEM((16, 144, 128), F32)],
        compiler_params=params(16), cost_estimate=cost(RING, 3e6), name="ring_sum",
    )(q0, *moved)
    mixed, grad_tokens, gain_part = pl.pallas_call(
        unpack_kernel,
        out_shape=(shape(4, 128, D), shape(4, 128, D), shape(8, 128, dtype=F32)),
        compiler_params=params(20), cost_estimate=cost(1e9, 4e6), name="unpack",
    )(back)
    last = lax.all_to_all(mine, AXES, 0, 0, tiled=True, axis_index_groups=CHIPS)
    gains = [gain_part] + [lax.ppermute(gain_part, AXES, y_shift(s)) for s in range(1, 4)]
    grad_qkv, grad_out, grad_gain = pl.pallas_call(
        final_kernel,
        out_shape=(shape(6, 3 * D, dtype=F32), shape(6, D, dtype=F32), shape(1, 6, dtype=F32)),
        in_specs=[pl.BlockSpec(memory_space=pltpu.SMEM)] + [VM] * 5,
        scratch_shapes=[pltpu.VMEM((144, 128), F32)],
        compiler_params=params(16), cost_estimate=cost(1e6, 1e6), name="final",
    )(first, last, *gains)
    return mixed, grad_tokens, grad_qkv, grad_out, grad_gain.reshape(6)


def solution(mesh):
    in_specs = (P("depth", "mod", None), P("depth", "mod", None), P("depth", "mod"), P(), P(), P())
    out_specs = (
        P("depth", "mod", None),
        P("depth", "mod", None),
        P(("depth", "mod"), None),
        P(("depth", "mod"), None),
        P(("depth", "mod")),
    )
    return jax.shard_map(
        per_device, mesh=mesh, in_specs=in_specs, out_specs=out_specs, check_vma=False
    )
```

```python
import jax
import jax.numpy as jnp
import numpy as np
from jax import lax
from jax.experimental import pallas as pl
from jax.experimental.pallas import tpu as pltpu
from jax.sharding import PartitionSpec as P

HEADS = 12
HEAD_DIM = 64
EPS = 1e-06
LESION_GAIN = 3.0
D = 768
TOK = 512
AXES = ("depth", "mod")
BF = jnp.bfloat16
F32 = jnp.float32
MB = 1024 * 1024
PASS = 1e6
RING = 1e10
MAIN_MB = 42
TOKEN_MB = 14


def place(xlo, z, c, xhi, y):
    return (xlo * 8 + z * 2 + c) * 8 + xhi * 4 + y


def parts_of(i):
    d, m = divmod(i, 8)
    return d // 8, (d // 2) % 4, d % 2, m // 4, m % 4


PLANE = [
    [place(a, z, c, b, y) for a in range(2) for z in range(4) for c in range(2) for b in range(2)]
    for y in range(4)
]
CHIPS = [
    [place(a, z, c, b, y) for a in range(2) for z in range(4) for b in range(2)]
    for c in range(2)
    for y in range(4)
]
CORE_SWAP = [(i, i ^ 8) for i in range(128)]


def y_shift(s):
    out = []
    for i in range(128):
        a, z, c, b, y = parts_of(i)
        out.append((i, place(a, z, c, b, (y + s) % 4)))
    return out


def feature_table():
    table = np.zeros((8, D), np.int32)
    for c in range(2):
        for y in range(4):
            n = 0
            for rc in range(2):
                for ry in range(4):
                    for a in range(2):
                        for z in range(4):
                            for b in range(2):
                                i = place(a, z, c ^ rc, b, (y + ry) % 4)
                                for r in range(6):
                                    table[c * 4 + y, n] = 6 * i + r
                                    n += 1
    return table


FEATURES = feature_table()


def dot(a, b, ca, cb):
    return lax.dot_general(a, b, (((ca,), (cb,)), ((), ())), preferred_element_type=F32)


def onehot(mask):
    return jnp.where(mask, 1.0, 0.0).astype(BF)


def rows_and_columns():
    i = lax.broadcasted_iota(jnp.int32, (128, 128), 0)
    return i, lax.broadcasted_iota(jnp.int32, (128, 128), 1)


def send_order():
    i, s = rows_and_columns()
    return s == ((i >> 2) & 3) * 32 + (i >> 4) * 4 + (i & 3)


def position_order():
    i, s = rows_and_columns()
    return onehot(s == ((i >> 2) & 7) * 16 + (i & 3) * 4 + (i >> 5))


def by_position(x):
    order = position_order()
    parts = [dot(order, x[n * 128 : n * 128 + 128], 1, 0).astype(BF) for n in range(4)]
    return jnp.concatenate(
        [parts[n][p * 32 : p * 32 + 32] for p in range(4) for n in range(4)], axis=0
    )


def by_source(x):
    order = position_order()
    parts = [
        jnp.concatenate([x[p * 128 + n * 32 : p * 128 + n * 32 + 32] for p in range(4)], axis=0)
        for n in range(4)
    ]
    return jnp.concatenate([dot(order, part, 0, 0).astype(BF) for part in parts], axis=0)


def pack_kernel(tok_hbm, cot_hbm, les_hbm, out_hbm, tok_ref, cot_ref, les_ref, out_ref, sems):
    loads = [
        pltpu.make_async_copy(src, dst, sems.at[n])
        for n, (src, dst) in enumerate(
            ((les_hbm, les_ref), (tok_hbm, tok_ref), (cot_hbm, cot_ref))
        )
    ]
    for c in loads:
        c.start()
    mask = send_order()
    plain = onehot(mask)

    def block(ref, n):
        return jnp.concatenate([ref[d, n * 32 : n * 32 + 32] for d in range(4)], axis=0)

    loads[1].wait()
    for n in range(4):
        t = dot(plain, block(tok_ref, n), 1, 0).astype(BF)
        out_ref[0, n * 8 : n * 8 + 8] = t.reshape(8, 16, D)
    store_t = pltpu.make_async_copy(out_ref.at[0], out_hbm.at[:, 0], sems.at[3])
    store_t.start()
    loads[0].wait()
    weight = 1.0 + LESION_GAIN * les_ref[...].astype(F32)
    loads[2].wait()
    for n in range(4):
        row = jnp.concatenate([weight[d : d + 1, n * 32 : n * 32 + 32] for d in range(4)], axis=1)
        scaled = jnp.where(mask, row, 0.0).astype(BF)
        g = dot(scaled, block(cot_ref, n), 1, 0).astype(BF)
        out_ref[1, n * 8 : n * 8 + 8] = g.reshape(8, 16, D)
    store_g = pltpu.make_async_copy(out_ref.at[1], out_hbm.at[:, 1], sems.at[4])
    store_g.start()
    store_t.wait()
    store_g.wait()


def unpack_kernel(in_ref, mixed_ref, grad_ref, gain_ref):
    sel = onehot(send_order())
    for n, out in enumerate((mixed_ref, grad_ref)):
        base = n * 96
        x = jnp.concatenate(
            [in_ref[:, base + l * 16 : base + l * 16 + 16].reshape(TOK, 128) for l in range(6)],
            axis=1,
        )
        for b in range(4):
            y = dot(sel, x[b * 128 : b * 128 + 128], 0, 0).astype(BF)
            for d in range(4):
                out[d, b * 32 : b * 32 + 32] = y[d * 32 : d * 32 + 32]
    g = jnp.sum(in_ref[:, 192:].astype(F32), axis=0)
    gain_ref[...] = jnp.broadcast_to(jnp.sum(g, axis=0, keepdims=True), (8, 128))


def normalise(x):
    xf = x.astype(F32)
    inv_rms = lax.rsqrt(jnp.mean(xf * xf, axis=-1, keepdims=True) + EPS)
    return xf, inv_rms, xf * inv_rms


def main_kernel(
    recv_hbm, gain_ref, feat_ref, wqkv_hbm, wout_hbm,
    keep_ref, send_ref, attn_ref, dqkv_ref,
    recv_ref, wqkv_ref, wout_ref, qkv_ref, ga_ref, norm_ref, gy_ref, lhs_ref, sems,
):
    scale = float(HEAD_DIM) ** (-0.5)
    loads = [
        pltpu.make_async_copy(src, dst, sems.at[n])
        for n, (src, dst) in enumerate(
            ((recv_hbm, recv_ref), (wout_hbm, wout_ref), (wqkv_hbm, wqkv_ref))
        )
    ]
    for c in loads:
        c.start()
    loads[0].wait()
    _, _, unit = normalise(recv_ref[:, 0].reshape(TOK, D))
    normed = (unit * gain_ref[...]).astype(BF)
    norm_ref[...] = by_position(normed)
    gy_ref[...] = by_position(recv_ref[:, 1].reshape(TOK, D))
    loads[1].wait()
    ga_ref[...] = dot(gy_ref[...], wout_ref[...], 1, 1).astype(BF)
    loads[2].wait()

    def project(n, _):
        cols = pl.ds(pl.multiple_of(n * 768, 768), 768)
        qkv_ref[:, cols] = dot(norm_ref[...], wqkv_ref[:, cols], 1, 0).astype(BF)
        return 0

    lax.fori_loop(0, 3, project, 0, unroll=True)
    first = lax.broadcasted_iota(jnp.int32, (128, 128), 1) < 64

    def split(x):
        zero = jnp.zeros_like(x)
        return jnp.concatenate([jnp.where(first, x, zero), jnp.where(first, zero, x)], axis=0)

    def stack(x):
        return jnp.concatenate([x[:, :128], x[:, 128:]], axis=0)

    def heads(hp, _):
        base = pl.multiple_of(hp * 128, 128)
        rows = [slice(p * 128, (p + 1) * 128) for p in range(4)]
        q = [qkv_ref[r, pl.ds(base, 128)] for r in rows]
        k = [qkv_ref[r, pl.ds(base + D, 128)] for r in rows]
        v = [qkv_ref[r, pl.ds(base + 2 * D, 128)] for r in rows]
        qb = [split(x) for x in q]
        gb = [split(ga_ref[r, pl.ds(base, 128)]) for r in rows]
        s = [dot(k[p], qb[p], 1, 1) for p in range(4)]
        dp = [dot(v[p], gb[p], 1, 1) for p in range(4)]
        pb, ds = [], []
        for p in range(4):
            sp = s[p] * scale
            e = jnp.exp(sp - jnp.max(sp, axis=0, keepdims=True))
            probs = e * (1.0 / jnp.sum(e, axis=0, keepdims=True))
            delta = jnp.sum(probs * dp[p], axis=0, keepdims=True)
            ds.append((probs * (dp[p] - delta) * scale).astype(BF))
            pb.append(probs.astype(BF))
        for p in range(4):
            attn_ref[rows[p], pl.ds(base, 128)] = dot(stack(pb[p]), split(v[p]), 0, 0).astype(BF)
            dqkv_ref[rows[p], pl.ds(base, 128)] = dot(stack(ds[p]), split(k[p]), 0, 0).astype(BF)
            dqkv_ref[rows[p], pl.ds(base + D, 128)] = dot(ds[p], qb[p], 1, 0).astype(BF)
            dqkv_ref[rows[p], pl.ds(base + 2 * D, 128)] = dot(pb[p], gb[p], 1, 0).astype(BF)
        return 0

    lax.fori_loop(0, HEADS // 2, heads, 0, unroll=True)
    pick = onehot(lax.broadcasted_iota(jnp.int32, (D, D), 0) == feat_ref[...])
    lhs_ref[...] = dot(pick, norm_ref[...], 0, 1).astype(BF)

    def weight_grad(n, _):
        cols = pl.ds(pl.multiple_of(n * 768, 768), 768)
        g = dot(lhs_ref[...], dqkv_ref[:, cols], 1, 0).astype(BF)
        keep_ref[:, cols] = g[:384]
        send_ref[:, cols] = g[384:]
        return 0

    lax.fori_loop(0, 3, weight_grad, 0, unroll=True)
    lhs_ref[...] = dot(pick, attn_ref[...], 0, 1).astype(BF)
    g = dot(lhs_ref[...], gy_ref[...], 1, 0).astype(BF)
    keep_ref[:, 3 * D :] = g[:384]
    send_ref[:, 3 * D :] = g[384:]


def token_kernel(recv_ref, gain_ref, dqkv_ref, wqkv_ref, ret_ref):
    gn = dot(dqkv_ref[...], wqkv_ref[...], 1, 1).astype(BF)
    gn = by_source(gn).astype(F32)
    _, inv_rms, unit = normalise(recv_ref[:, 0].reshape(TOK, D))
    g = jnp.sum(gn * unit, axis=0, keepdims=True)
    dunit = gn * gain_ref[...]
    back = inv_rms * (dunit - unit * jnp.mean(dunit * unit, axis=-1, keepdims=True))
    gy = recv_ref[:, 1].reshape(TOK, D).astype(F32)
    grad = (gy + back).astype(BF)
    for l in range(6):
        ret_ref[:, l * 16 : l * 16 + 16] = grad[:, l * 128 : l * 128 + 128].reshape(32, 16, 128)
    k = lax.broadcasted_iota(jnp.int32, (32, 8, 128), 0) * 24
    lane = lax.broadcasted_iota(jnp.int32, (32, 8, 128), 2)
    own = jnp.zeros((32, 8, 128), F32)
    for l in range(6):
        f = lane + l * 128
        part = g[:, l * 128 : l * 128 + 128].reshape(1, 1, 128)
        own = own + jnp.where(jnp.logical_and(f >= k, f < k + 24), part, 0.0)
    high = own.astype(BF).astype(F32)
    mid = (own - high).astype(BF).astype(F32)
    row = lax.broadcasted_iota(jnp.int32, (32, 8, 128), 1)
    low = own - high - mid
    terms = jnp.where(row == 0, high, jnp.where(row == 1, mid, jnp.where(row == 2, low, 0.0)))
    ret_ref[:, 96:] = terms.astype(BF)


def mixed_kernel(recv_ref, attn_ref, wout_ref, grad_ref, ret_hbm, ret_ref, sems):
    store_g = pltpu.make_async_copy(grad_ref, ret_hbm.at[:, 96:], sems.at[0])
    store_g.start()
    attn = by_source(attn_ref[...])
    proj = dot(attn, wout_ref[...], 1, 0).astype(BF)
    mixed = (recv_ref[:, 0].reshape(TOK, D).astype(F32) + proj.astype(F32)).astype(BF)
    for l in range(6):
        ret_ref[:, l * 16 : l * 16 + 16] = mixed[:, l * 128 : l * 128 + 128].reshape(32, 16, 128)
    store_m = pltpu.make_async_copy(ret_ref, ret_hbm.at[:, :96], sems.at[1])
    store_m.start()
    store_g.wait()
    store_m.wait()


HALF = 2 * D


def pair_sum_kernel(a_ref, b_ref, own, up, down, hold):
    def block(n, cols):
        rows = slice(n * 96, n * 96 + 96)
        return (a_ref[rows, cols].astype(F32) + b_ref[rows, cols].astype(F32)).astype(BF)

    left, right = slice(0, HALF), slice(HALF, 2 * HALF)
    up[:, left] = block(2, left)
    up[:, right] = block(1, right)
    down[:, left] = block(3, left)
    down[:, right] = block(2, right)
    own[:, left] = block(0, left)
    own[:, right] = block(0, right)
    hold[:, left] = block(1, left)
    hold[:, right] = block(3, right)


def pass_on_kernel(hold, up, down, up_out, down_out):
    left, right = slice(0, HALF), slice(HALF, 2 * HALF)
    up_out[...] = (hold[:, left].astype(F32) + up[:, left].astype(F32)).astype(BF)
    down_out[...] = (hold[:, right].astype(F32) + down[:, right].astype(F32)).astype(BF)


def ring_sum_kernel(own, up, down, up_far, down_far, o):
    left, right = slice(0, HALF), slice(HALF, 2 * HALF)
    for q in range(4):
        r = slice(q * 24, q * 24 + 24)
        x = own[r, left].astype(F32) + down[r, left].astype(F32) + up_far[r].astype(F32)
        y = own[r, right].astype(F32) + up[r, right].astype(F32) + down_far[r].astype(F32)
        for k in range(4):
            pieces = [
                v[k * 6 : k * 6 + 6, l * 128 : l * 128 + 128] for v in (x, y) for l in range(12)
            ]
            o[q * 4 + k] = jnp.concatenate(pieces, axis=0).astype(BF)


def final_kernel(first_ref, in_ref, g0, g1, g2, g3, qkv_ref, out_ref, gain_ref, sum_ref):
    sum_ref[...] = jnp.sum(in_ref[...].astype(F32), axis=0)
    for l in range(24):
        v = sum_ref[l * 6 : l * 6 + 6]
        if l < 18:
            qkv_ref[:, l * 128 : l * 128 + 128] = v
        else:
            out_ref[:, (l - 18) * 128 : (l - 17) * 128] = v
    g = (g0[...] + g1[...]) + (g2[...] + g3[...])
    r = lax.broadcasted_iota(jnp.int32, (8, 128), 0)
    lane = lax.broadcasted_iota(jnp.int32, (8, 128), 1)
    mine = jnp.sum(
        jnp.where(lane == ((first_ref[0] + r) & 127), g, 0.0), axis=1, keepdims=True
    )
    gain_ref[...] = jnp.sum(jnp.where(lane == r, mine, 0.0), axis=0, keepdims=True)[:, :6]


def params(mb):
    return pltpu.CompilerParams(vmem_limit_bytes=mb * MB)


def cost(flops, nbytes):
    return pl.CostEstimate(flops=int(flops), bytes_accessed=int(nbytes), transcendentals=0)


def shape(*dims, dtype=BF):
    return jax.ShapeDtypeStruct(dims, dtype)


HBM = pl.BlockSpec(memory_space=pltpu.HBM)
VM = pl.BlockSpec(memory_space=pltpu.VMEM)
DMA = pltpu.SemaphoreType.DMA


def per_device(tokens, cotangent, lesion, w_qkv, w_out, norm_gain):
    gain = norm_gain.reshape(1, D)
    depth = lax.axis_index("depth")
    mod = lax.axis_index("mod")
    feat = lax.dynamic_slice(jnp.asarray(FEATURES), ((depth & 1) * 4 + (mod & 3), 0), (1, D))
    first = ((depth * 8 + mod) * 6).astype(jnp.int32).reshape(1)
    packed = pl.pallas_call(
        pack_kernel, out_shape=shape(32, 2, 16, D), in_specs=[HBM] * 3, out_specs=HBM,
        scratch_shapes=[
            pltpu.VMEM((4, 128, D), BF), pltpu.VMEM((4, 128, D), BF), pltpu.VMEM((4, 128), jnp.int32),
            pltpu.VMEM((2, 32, 16, D), BF), DMA((5,)),
        ],
        compiler_params=params(60), cost_estimate=cost(1e9, 4e6), name="pack",
    )(tokens, cotangent, lesion)
    recv = lax.all_to_all(packed, AXES, 0, 0, tiled=True, axis_index_groups=PLANE)
    keep, send, attn, dqkv = pl.pallas_call(
        main_kernel,
        out_shape=(shape(384, 4 * D), shape(384, 4 * D), shape(TOK, D), shape(TOK, 3 * D)),
        in_specs=[HBM, VM, VM, HBM, HBM],
        scratch_shapes=[
            pltpu.VMEM((32, 2, 16, D), BF), pltpu.VMEM((D, 3 * D), BF), pltpu.VMEM((D, D), BF),
            pltpu.VMEM((TOK, 3 * D), BF), pltpu.VMEM((TOK, D), BF), pltpu.VMEM((TOK, D), BF),
            pltpu.VMEM((TOK, D), BF), pltpu.VMEM((D, TOK), BF), DMA((3,)),
        ],
        compiler_params=params(MAIN_MB), cost_estimate=cost(1e10, 1.5e7), name="main",
    )(recv, gain, feat, w_qkv, w_out)
    got = lax.ppermute(send, AXES, CORE_SWAP)
    grads = pl.pallas_call(
        token_kernel, out_shape=shape(32, 104, 128),
        compiler_params=params(TOKEN_MB), cost_estimate=cost(2.8e9, 9e6), name="token_grads",
    )(recv, gain, dqkv, w_qkv)
    ret = pl.pallas_call(
        mixed_kernel, out_shape=shape(32, 200, 128), out_specs=HBM,
        scratch_shapes=[pltpu.VMEM((32, 96, 128), BF), DMA((2,))],
        compiler_params=params(14), cost_estimate=cost(1e9, 5e6), name="mixed",
    )(recv, attn, w_out, grads)
    quarters = pl.pallas_call(
        pair_sum_kernel, out_shape=tuple(shape(96, 4 * D) for _ in range(4)),
        compiler_params=params(6), cost_estimate=cost(1e6, 7e6), name="pair_sum",
    )(keep, got)
    own, up, down, hold, ret = lax.optimization_barrier((*quarters, ret))
    up = lax.ppermute(up, AXES, y_shift(1))
    down = lax.ppermute(down, AXES, y_shift(3))
    up_far, down_far = pl.pallas_call(
        pass_on_kernel, out_shape=(shape(96, HALF), shape(96, HALF)),
        compiler_params=params(6), cost_estimate=cost(PASS, 3e6), name="pass_on",
    )(hold, up, down)
    up_far = lax.ppermute(up_far, AXES, y_shift(1))
    down_far = lax.ppermute(down_far, AXES, y_shift(3))
    back = lax.all_to_all(ret, AXES, 0, 0, tiled=True, axis_index_groups=PLANE)
    mine = pl.pallas_call(
        ring_sum_kernel, out_shape=shape(16, 144, 128),
        compiler_params=params(6), cost_estimate=cost(RING, 3e6), name="ring_sum",
    )(own, up, down, up_far, down_far)
    mixed, grad_tokens, gain_part = pl.pallas_call(
        unpack_kernel,
        out_shape=(shape(4, 128, D), shape(4, 128, D), shape(8, 128, dtype=F32)),
        compiler_params=params(14), cost_estimate=cost(1e9, 4e6), name="unpack",
    )(back)
    last = lax.all_to_all(mine, AXES, 0, 0, tiled=True, axis_index_groups=CHIPS)
    gains = [gain_part] + [lax.ppermute(gain_part, AXES, y_shift(s)) for s in range(1, 4)]
    grad_qkv, grad_out, grad_gain = pl.pallas_call(
        final_kernel,
        out_shape=(shape(6, 3 * D, dtype=F32), shape(6, D, dtype=F32), shape(1, 6, dtype=F32)),
        in_specs=[pl.BlockSpec(memory_space=pltpu.SMEM)] + [VM] * 5,
        scratch_shapes=[pltpu.VMEM((144, 128), F32)],
        compiler_params=params(6), cost_estimate=cost(1e6, 1e6), name="final",
    )(first, last, *gains)
    return mixed, grad_tokens, grad_qkv, grad_out, grad_gain.reshape(6)


def solution(mesh):
    in_specs = (P("depth", "mod", None), P("depth", "mod", None), P("depth", "mod"), P(), P(), P())
    out_specs = (
        P("depth", "mod", None),
        P("depth", "mod", None),
        P(("depth", "mod"), None),
        P(("depth", "mod"), None),
        P(("depth", "mod")),
    )
    return jax.shard_map(
        per_device, mesh=mesh, in_specs=in_specs, out_specs=out_specs, check_vma=False
    )
```

```python
import jax
import jax.numpy as jnp
import numpy as np
from jax import lax
from jax.experimental import pallas as pl
from jax.experimental.pallas import tpu as pltpu
from jax.sharding import PartitionSpec as P

HEADS = 12
HEAD_DIM = 64
EPS = 1e-06
LESION_GAIN = 3.0
D = 768
TOK = 512
AXES = ("depth", "mod")
BF = jnp.bfloat16
F32 = jnp.float32
MB = 1024 * 1024
PASS = 1e6
RING = 1e10
MAIN_MB = 42
TOKEN_MB = 20


def place(xlo, z, c, xhi, y):
    return (xlo * 8 + z * 2 + c) * 8 + xhi * 4 + y


def parts_of(i):
    d, m = divmod(i, 8)
    return d // 8, (d // 2) % 4, d % 2, m // 4, m % 4


PLANE = [
    [place(a, z, c, b, y) for a in range(2) for z in range(4) for c in range(2) for b in range(2)]
    for y in range(4)
]
CHIPS = [
    [place(a, z, c, b, y) for a in range(2) for z in range(4) for b in range(2)]
    for c in range(2)
    for y in range(4)
]
CORE_SWAP = [(i, i ^ 8) for i in range(128)]


def y_shift(s):
    out = []
    for i in range(128):
        a, z, c, b, y = parts_of(i)
        out.append((i, place(a, z, c, b, (y + s) % 4)))
    return out


def feature_table():
    table = np.zeros((8, D), np.int32)
    for c in range(2):
        for y in range(4):
            n = 0
            for rc in range(2):
                for ry in range(4):
                    for a in range(2):
                        for z in range(4):
                            for b in range(2):
                                i = place(a, z, c ^ rc, b, (y + ry) % 4)
                                for r in range(6):
                                    table[c * 4 + y, n] = 6 * i + r
                                    n += 1
    return table


FEATURES = feature_table()


def dot(a, b, ca, cb):
    return lax.dot_general(a, b, (((ca,), (cb,)), ((), ())), preferred_element_type=F32)


def onehot(mask):
    return jnp.where(mask, 1.0, 0.0).astype(BF)


def rows_and_columns():
    i = lax.broadcasted_iota(jnp.int32, (128, 128), 0)
    return i, lax.broadcasted_iota(jnp.int32, (128, 128), 1)


def send_order():
    i, s = rows_and_columns()
    return s == ((i >> 2) & 3) * 32 + (i >> 4) * 4 + (i & 3)


def position_order():
    i, s = rows_and_columns()
    return onehot(s == ((i >> 2) & 7) * 16 + (i & 3) * 4 + (i >> 5))


def by_position(x):
    order = position_order()
    parts = [dot(order, x[n * 128 : n * 128 + 128], 1, 0).astype(BF) for n in range(4)]
    return jnp.concatenate(
        [parts[n][p * 32 : p * 32 + 32] for p in range(4) for n in range(4)], axis=0
    )


def by_source(x):
    order = position_order()
    parts = [
        jnp.concatenate([x[p * 128 + n * 32 : p * 128 + n * 32 + 32] for p in range(4)], axis=0)
        for n in range(4)
    ]
    return jnp.concatenate([dot(order, part, 0, 0).astype(BF) for part in parts], axis=0)


def pack_kernel(tok_hbm, cot_hbm, les_hbm, out_hbm, tok_ref, cot_ref, les_ref, out_ref, sems):
    loads = [
        pltpu.make_async_copy(src, dst, sems.at[n])
        for n, (src, dst) in enumerate(
            ((les_hbm, les_ref), (tok_hbm, tok_ref), (cot_hbm, cot_ref))
        )
    ]
    for c in loads:
        c.start()
    mask = send_order()
    plain = onehot(mask)

    def block(ref, n):
        return jnp.concatenate([ref[d, n * 32 : n * 32 + 32] for d in range(4)], axis=0)

    loads[1].wait()
    for n in range(4):
        t = dot(plain, block(tok_ref, n), 1, 0).astype(BF)
        out_ref[0, n * 8 : n * 8 + 8] = t.reshape(8, 16, D)
    store_t = pltpu.make_async_copy(out_ref.at[0], out_hbm.at[:, 0], sems.at[3])
    store_t.start()
    loads[0].wait()
    weight = 1.0 + LESION_GAIN * les_ref[...].astype(F32)
    loads[2].wait()
    for n in range(4):
        row = jnp.concatenate([weight[d : d + 1, n * 32 : n * 32 + 32] for d in range(4)], axis=1)
        scaled = jnp.where(mask, row, 0.0).astype(BF)
        g = dot(scaled, block(cot_ref, n), 1, 0).astype(BF)
        out_ref[1, n * 8 : n * 8 + 8] = g.reshape(8, 16, D)
    store_g = pltpu.make_async_copy(out_ref.at[1], out_hbm.at[:, 1], sems.at[4])
    store_g.start()
    store_t.wait()
    store_g.wait()


def unpack_kernel(in_ref, mixed_ref, grad_ref, gain_ref):
    sel = onehot(send_order())
    for n, out in enumerate((mixed_ref, grad_ref)):
        base = n * 96
        x = jnp.concatenate(
            [in_ref[:, base + l * 16 : base + l * 16 + 16].reshape(TOK, 128) for l in range(6)],
            axis=1,
        )
        for b in range(4):
            y = dot(sel, x[b * 128 : b * 128 + 128], 0, 0).astype(BF)
            for d in range(4):
                out[d, b * 32 : b * 32 + 32] = y[d * 32 : d * 32 + 32]
    g = jnp.sum(in_ref[:, 192:].astype(F32), axis=0)
    gain_ref[...] = jnp.broadcast_to(jnp.sum(g, axis=0, keepdims=True), (8, 128))


def normalise(x):
    xf = x.astype(F32)
    inv_rms = lax.rsqrt(jnp.mean(xf * xf, axis=-1, keepdims=True) + EPS)
    return xf, inv_rms, xf * inv_rms


def main_kernel(
    recv_ref, gain_ref, feat_ref, wqkv_hbm, wout_hbm,
    keep_ref, send_ref, attn_ref, dqkv_ref,
    wqkv_ref, wout_ref, qkv_ref, ga_ref, norm_ref, gy_ref, lhs_ref, sems,
):
    scale = float(HEAD_DIM) ** (-0.5)
    loads = [
        pltpu.make_async_copy(src, dst, sems.at[n])
        for n, (src, dst) in enumerate(
            ((wout_hbm, wout_ref), (wqkv_hbm, wqkv_ref))
        )
    ]
    for c in loads:
        c.start()
    _, _, unit = normalise(recv_ref[:, 0].reshape(TOK, D))
    normed = (unit * gain_ref[...]).astype(BF)
    norm_ref[...] = by_position(normed)
    gy_ref[...] = by_position(recv_ref[:, 1].reshape(TOK, D))
    loads[0].wait()
    ga_ref[...] = dot(gy_ref[...], wout_ref[...], 1, 1).astype(BF)
    loads[1].wait()

    def project(n, _):
        cols = pl.ds(pl.multiple_of(n * 768, 768), 768)
        qkv_ref[:, cols] = dot(norm_ref[...], wqkv_ref[:, cols], 1, 0).astype(BF)
        return 0

    lax.fori_loop(0, 3, project, 0, unroll=True)
    first = lax.broadcasted_iota(jnp.int32, (128, 128), 1) < 64

    def split(x):
        zero = jnp.zeros_like(x)
        return jnp.concatenate([jnp.where(first, x, zero), jnp.where(first, zero, x)], axis=0)

    def stack(x):
        return jnp.concatenate([x[:, :128], x[:, 128:]], axis=0)

    def heads(hp, _):
        base = pl.multiple_of(hp * 128, 128)
        rows = [slice(p * 128, (p + 1) * 128) for p in range(4)]
        q = [qkv_ref[r, pl.ds(base, 128)] for r in rows]
        k = [qkv_ref[r, pl.ds(base + D, 128)] for r in rows]
        v = [qkv_ref[r, pl.ds(base + 2 * D, 128)] for r in rows]
        qb = [split(x) for x in q]
        gb = [split(ga_ref[r, pl.ds(base, 128)]) for r in rows]
        s = [dot(k[p], qb[p], 1, 1) for p in range(4)]
        dp = [dot(v[p], gb[p], 1, 1) for p in range(4)]
        pb, ds = [], []
        for p in range(4):
            sp = s[p] * scale
            e = jnp.exp(sp - jnp.max(sp, axis=0, keepdims=True))
            probs = e * (1.0 / jnp.sum(e, axis=0, keepdims=True))
            delta = jnp.sum(probs * dp[p], axis=0, keepdims=True)
            ds.append((probs * (dp[p] - delta) * scale).astype(BF))
            pb.append(probs.astype(BF))
        for p in range(4):
            attn_ref[rows[p], pl.ds(base, 128)] = dot(stack(pb[p]), split(v[p]), 0, 0).astype(BF)
            dqkv_ref[rows[p], pl.ds(base, 128)] = dot(stack(ds[p]), split(k[p]), 0, 0).astype(BF)
            dqkv_ref[rows[p], pl.ds(base + D, 128)] = dot(ds[p], qb[p], 1, 0).astype(BF)
            dqkv_ref[rows[p], pl.ds(base + 2 * D, 128)] = dot(pb[p], gb[p], 1, 0).astype(BF)
        return 0

    lax.fori_loop(0, HEADS // 2, heads, 0, unroll=True)
    pick = onehot(lax.broadcasted_iota(jnp.int32, (D, D), 0) == feat_ref[...])
    lhs_ref[...] = dot(pick, norm_ref[...], 0, 1).astype(BF)

    def weight_grad(n, _):
        cols = pl.ds(pl.multiple_of(n * 768, 768), 768)
        g = dot(lhs_ref[...], dqkv_ref[:, cols], 1, 0).astype(BF)
        keep_ref[:, cols] = g[:384]
        send_ref[:, cols] = g[384:]
        return 0

    lax.fori_loop(0, 3, weight_grad, 0, unroll=True)
    lhs_ref[...] = dot(pick, attn_ref[...], 0, 1).astype(BF)
    g = dot(lhs_ref[...], gy_ref[...], 1, 0).astype(BF)
    keep_ref[:, 3 * D :] = g[:384]
    send_ref[:, 3 * D :] = g[384:]


def token_kernel(
    recv_ref, gain_ref, attn_ref, dqkv_ref, wqkv_ref, wout_ref, ret_hbm, ret_ref, sems
):
    gn = dot(dqkv_ref[...], wqkv_ref[...], 1, 1).astype(BF)
    gn = by_source(gn).astype(F32)
    xf, inv_rms, unit = normalise(recv_ref[:, 0].reshape(TOK, D))
    g = jnp.sum(gn * unit, axis=0, keepdims=True)
    dunit = gn * gain_ref[...]
    back = inv_rms * (dunit - unit * jnp.mean(dunit * unit, axis=-1, keepdims=True))
    gy = recv_ref[:, 1].reshape(TOK, D).astype(F32)
    grad = (gy + back).astype(BF)
    for l in range(6):
        ret_ref[:, 96 + l * 16 : 112 + l * 16] = grad[:, l * 128 : l * 128 + 128].reshape(32, 16, 128)
    k = lax.broadcasted_iota(jnp.int32, (32, 8, 128), 0) * 24
    lane = lax.broadcasted_iota(jnp.int32, (32, 8, 128), 2)
    own = jnp.zeros((32, 8, 128), F32)
    for l in range(6):
        f = lane + l * 128
        part = g[:, l * 128 : l * 128 + 128].reshape(1, 1, 128)
        own = own + jnp.where(jnp.logical_and(f >= k, f < k + 24), part, 0.0)
    high = own.astype(BF).astype(F32)
    mid = (own - high).astype(BF).astype(F32)
    row = lax.broadcasted_iota(jnp.int32, (32, 8, 128), 1)
    low = own - high - mid
    terms = jnp.where(row == 0, high, jnp.where(row == 1, mid, jnp.where(row == 2, low, 0.0)))
    ret_ref[:, 192:] = terms.astype(BF)
    store_g = pltpu.make_async_copy(ret_ref.at[:, 96:], ret_hbm.at[:, 96:], sems.at[0])
    store_g.start()
    attn = by_source(attn_ref[...])
    proj = dot(attn, wout_ref[...], 1, 0).astype(BF)
    mixed = (xf + proj.astype(F32)).astype(BF)
    for l in range(6):
        ret_ref[:, l * 16 : l * 16 + 16] = mixed[:, l * 128 : l * 128 + 128].reshape(32, 16, 128)
    store_m = pltpu.make_async_copy(ret_ref.at[:, :96], ret_hbm.at[:, :96], sems.at[1])
    store_m.start()
    store_g.wait()
    store_m.wait()


HALF = 2 * D


def pair_sum_kernel(a_ref, b_ref, own, up, down, hold):
    def block(n, cols):
        rows = slice(n * 96, n * 96 + 96)
        return (a_ref[rows, cols].astype(F32) + b_ref[rows, cols].astype(F32)).astype(BF)

    left, right = slice(0, HALF), slice(HALF, 2 * HALF)
    up[:, left] = block(2, left)
    up[:, right] = block(1, right)
    down[:, left] = block(3, left)
    down[:, right] = block(2, right)
    own[:, left] = block(0, left)
    own[:, right] = block(0, right)
    hold[:, left] = block(1, left)
    hold[:, right] = block(3, right)


def pass_on_kernel(hold, up, down, own, up_out, down_out, sum_out):
    left, right = slice(0, HALF), slice(HALF, 2 * HALF)
    up_out[...] = (hold[:, left].astype(F32) + up[:, left].astype(F32)).astype(BF)
    down_out[...] = (hold[:, right].astype(F32) + down[:, right].astype(F32)).astype(BF)
    sum_out[:, left] = own[:, left].astype(F32) + down[:, left].astype(F32)
    sum_out[:, right] = own[:, right].astype(F32) + up[:, right].astype(F32)


def ring_sum_kernel(near, up_far, down_far, o):
    for q in range(4):
        r = slice(q * 24, q * 24 + 24)
        x = near[r, :HALF] + up_far[r].astype(F32)
        y = near[r, HALF:] + down_far[r].astype(F32)
        for k in range(4):
            pieces = [
                v[k * 6 : k * 6 + 6, l * 128 : l * 128 + 128] for v in (x, y) for l in range(12)
            ]
            o[q * 4 + k] = jnp.concatenate(pieces, axis=0).astype(BF)


def final_kernel(first_ref, in_ref, g0, g1, g2, g3, qkv_ref, out_ref, gain_ref, sum_ref):
    sum_ref[...] = jnp.sum(in_ref[...].astype(F32), axis=0)
    for l in range(24):
        v = sum_ref[l * 6 : l * 6 + 6]
        if l < 18:
            qkv_ref[:, l * 128 : l * 128 + 128] = v
        else:
            out_ref[:, (l - 18) * 128 : (l - 17) * 128] = v
    g = (g0[...] + g1[...]) + (g2[...] + g3[...])
    r = lax.broadcasted_iota(jnp.int32, (8, 128), 0)
    lane = lax.broadcasted_iota(jnp.int32, (8, 128), 1)
    mine = jnp.sum(
        jnp.where(lane == ((first_ref[0] + r) & 127), g, 0.0), axis=1, keepdims=True
    )
    gain_ref[...] = jnp.sum(jnp.where(lane == r, mine, 0.0), axis=0, keepdims=True)[:, :6]


def params(mb):
    return pltpu.CompilerParams(vmem_limit_bytes=int(mb * MB))


def cost(flops, nbytes):
    return pl.CostEstimate(flops=int(flops), bytes_accessed=int(nbytes), transcendentals=0)


def shape(*dims, dtype=BF):
    return jax.ShapeDtypeStruct(dims, dtype)


HBM = pl.BlockSpec(memory_space=pltpu.HBM)
VM = pl.BlockSpec(memory_space=pltpu.VMEM)
DMA = pltpu.SemaphoreType.DMA


def per_device(tokens, cotangent, lesion, w_qkv, w_out, norm_gain):
    gain = norm_gain.reshape(1, D)
    depth = lax.axis_index("depth")
    mod = lax.axis_index("mod")
    feat = lax.dynamic_slice(jnp.asarray(FEATURES), ((depth & 1) * 4 + (mod & 3), 0), (1, D))
    first = ((depth * 8 + mod) * 6).astype(jnp.int32).reshape(1)
    packed = pl.pallas_call(
        pack_kernel, out_shape=shape(32, 2, 16, D), in_specs=[HBM] * 3, out_specs=HBM,
        scratch_shapes=[
            pltpu.VMEM((4, 128, D), BF), pltpu.VMEM((4, 128, D), BF), pltpu.VMEM((4, 128), jnp.int32),
            pltpu.VMEM((2, 32, 16, D), BF), DMA((5,)),
        ],
        compiler_params=params(60), cost_estimate=cost(1e9, 4e6), name="pack",
    )(tokens, cotangent, lesion)
    recv = lax.all_to_all(packed, AXES, 0, 0, tiled=True, axis_index_groups=PLANE)
    keep, send, attn, dqkv = pl.pallas_call(
        main_kernel,
        out_shape=(shape(384, 4 * D), shape(384, 4 * D), shape(TOK, D), shape(TOK, 3 * D)),
        in_specs=[VM, VM, VM, HBM, HBM],
        scratch_shapes=[
            pltpu.VMEM((D, 3 * D), BF), pltpu.VMEM((D, D), BF),
            pltpu.VMEM((TOK, 3 * D), BF), pltpu.VMEM((TOK, D), BF), pltpu.VMEM((TOK, D), BF),
            pltpu.VMEM((TOK, D), BF), pltpu.VMEM((D, TOK), BF), DMA((2,)),
        ],
        compiler_params=params(MAIN_MB), cost_estimate=cost(1e10, 1.5e7), name="main",
    )(recv, gain, feat, w_qkv, w_out)
    got = lax.ppermute(send, AXES, CORE_SWAP)
    ret = pl.pallas_call(
        token_kernel, out_shape=shape(32, 200, 128), out_specs=HBM,
        scratch_shapes=[pltpu.VMEM((32, 200, 128), BF), DMA((2,))],
        compiler_params=params(TOKEN_MB), cost_estimate=cost(3.5e9, 1.2e7), name="token_grads",
    )(recv, gain, attn, dqkv, w_qkv, w_out)
    quarters = pl.pallas_call(
        pair_sum_kernel, out_shape=tuple(shape(96, 4 * D) for _ in range(4)),
        compiler_params=params(6), cost_estimate=cost(1e6, 7e6), name="pair_sum",
    )(keep, got)
    own, up, down, hold, ret = lax.optimization_barrier((*quarters, ret))
    up = lax.ppermute(up, AXES, y_shift(1))
    down = lax.ppermute(down, AXES, y_shift(3))
    up_far, down_far, near = pl.pallas_call(
        pass_on_kernel,
        out_shape=(shape(96, HALF), shape(96, HALF), shape(96, 4 * D, dtype=F32)),
        compiler_params=params(6), cost_estimate=cost(PASS, 3e6), name="pass_on",
    )(hold, up, down, own)
    up_far = lax.ppermute(up_far, AXES, y_shift(1))
    down_far = lax.ppermute(down_far, AXES, y_shift(3))
    back = lax.all_to_all(ret, AXES, 0, 0, tiled=True, axis_index_groups=PLANE)
    mine = pl.pallas_call(
        ring_sum_kernel, out_shape=shape(16, 144, 128),
        compiler_params=params(6), cost_estimate=cost(RING, 3e6), name="ring_sum",
    )(near, up_far, down_far)
    mixed, grad_tokens, gain_part = pl.pallas_call(
        unpack_kernel,
        out_shape=(shape(4, 128, D), shape(4, 128, D), shape(8, 128, dtype=F32)),
        compiler_params=params(14), cost_estimate=cost(1e9, 4e6), name="unpack",
    )(back)
    last = lax.all_to_all(mine, AXES, 0, 0, tiled=True, axis_index_groups=CHIPS)
    gains = [gain_part] + [lax.ppermute(gain_part, AXES, y_shift(s)) for s in range(1, 4)]
    grad_qkv, grad_out, grad_gain = pl.pallas_call(
        final_kernel,
        out_shape=(shape(6, 3 * D, dtype=F32), shape(6, D, dtype=F32), shape(1, 6, dtype=F32)),
        in_specs=[pl.BlockSpec(memory_space=pltpu.SMEM)] + [VM] * 5,
        scratch_shapes=[pltpu.VMEM((144, 128), F32)],
        compiler_params=params(6), cost_estimate=cost(1e6, 1e6), name="final",
    )(first, last, *gains)
    return mixed, grad_tokens, grad_qkv, grad_out, grad_gain.reshape(6)


def solution(mesh):
    in_specs = (P("depth", "mod", None), P("depth", "mod", None), P("depth", "mod"), P(), P(), P())
    out_specs = (
        P("depth", "mod", None),
        P("depth", "mod", None),
        P(("depth", "mod"), None),
        P(("depth", "mod"), None),
        P(("depth", "mod")),
    )
    return jax.shard_map(
        per_device, mesh=mesh, in_specs=in_specs, out_specs=out_specs, check_vma=False
    )
```

```python
import jax
import jax.numpy as jnp
import numpy as np
from jax import lax
from jax.experimental import pallas as pl
from jax.experimental.pallas import tpu as pltpu
from jax.sharding import PartitionSpec as P

HEADS = 12
HEAD_DIM = 64
EPS = 1e-06
LESION_GAIN = 3.0
D = 768
TOK = 512
AXES = ("depth", "mod")
BF = jnp.bfloat16
F32 = jnp.float32
MB = 1024 * 1024
PASS = 1e6
RING = 1e10
MAIN_MB = 42
TOKEN_MB = 14


def place(xlo, z, c, xhi, y):
    return (xlo * 8 + z * 2 + c) * 8 + xhi * 4 + y


def parts_of(i):
    d, m = divmod(i, 8)
    return d // 8, (d // 2) % 4, d % 2, m // 4, m % 4


PLANE = [
    [place(a, z, c, b, y) for a in range(2) for z in range(4) for c in range(2) for b in range(2)]
    for y in range(4)
]
CHIPS = [
    [place(a, z, c, b, y) for a in range(2) for z in range(4) for b in range(2)]
    for c in range(2)
    for y in range(4)
]
CORE_SWAP = [(i, i ^ 8) for i in range(128)]


def y_shift(s):
    out = []
    for i in range(128):
        a, z, c, b, y = parts_of(i)
        out.append((i, place(a, z, c, b, (y + s) % 4)))
    return out


def feature_table():
    table = np.zeros((8, D), np.int32)
    for c in range(2):
        for y in range(4):
            n = 0
            for rc in range(2):
                for ry in range(4):
                    for a in range(2):
                        for z in range(4):
                            for b in range(2):
                                i = place(a, z, c ^ rc, b, (y + ry) % 4)
                                for r in range(6):
                                    table[c * 4 + y, n] = 6 * i + r
                                    n += 1
    return table


FEATURES = feature_table()


def dot(a, b, ca, cb):
    return lax.dot_general(a, b, (((ca,), (cb,)), ((), ())), preferred_element_type=F32)


def onehot(mask):
    return jnp.where(mask, 1.0, 0.0).astype(BF)


def rows_and_columns():
    i = lax.broadcasted_iota(jnp.int32, (128, 128), 0)
    return i, lax.broadcasted_iota(jnp.int32, (128, 128), 1)


def send_order():
    i, s = rows_and_columns()
    return s == ((i >> 2) & 3) * 32 + (i >> 4) * 4 + (i & 3)


def position_order():
    i, s = rows_and_columns()
    return onehot(s == ((i >> 2) & 7) * 16 + (i & 3) * 4 + (i >> 5))


def by_position(x):
    order = position_order()
    parts = [dot(order, x[n * 128 : n * 128 + 128], 1, 0).astype(BF) for n in range(4)]
    return jnp.concatenate(
        [parts[n][p * 32 : p * 32 + 32] for p in range(4) for n in range(4)], axis=0
    )


def by_source(x):
    order = position_order()
    parts = [
        jnp.concatenate([x[p * 128 + n * 32 : p * 128 + n * 32 + 32] for p in range(4)], axis=0)
        for n in range(4)
    ]
    return jnp.concatenate([dot(order, part, 0, 0).astype(BF) for part in parts], axis=0)


def pack_kernel(tok_hbm, cot_hbm, les_hbm, out_hbm, tok_ref, cot_ref, les_ref, out_ref, sems):
    loads = [
        pltpu.make_async_copy(src, dst, sems.at[n])
        for n, (src, dst) in enumerate(
            ((les_hbm, les_ref), (tok_hbm, tok_ref), (cot_hbm, cot_ref))
        )
    ]
    for c in loads:
        c.start()
    mask = send_order()
    plain = onehot(mask)

    def block(ref, n):
        return jnp.concatenate([ref[d, n * 32 : n * 32 + 32] for d in range(4)], axis=0)

    loads[1].wait()
    for n in range(4):
        t = dot(plain, block(tok_ref, n), 1, 0).astype(BF)
        out_ref[0, n * 8 : n * 8 + 8] = t.reshape(8, 16, D)
    store_t = pltpu.make_async_copy(out_ref.at[0], out_hbm.at[:, 0], sems.at[3])
    store_t.start()
    loads[0].wait()
    weight = 1.0 + LESION_GAIN * les_ref[...].astype(F32)
    loads[2].wait()
    for n in range(4):
        row = jnp.concatenate([weight[d : d + 1, n * 32 : n * 32 + 32] for d in range(4)], axis=1)
        scaled = jnp.where(mask, row, 0.0).astype(BF)
        g = dot(scaled, block(cot_ref, n), 1, 0).astype(BF)
        out_ref[1, n * 8 : n * 8 + 8] = g.reshape(8, 16, D)
    store_g = pltpu.make_async_copy(out_ref.at[1], out_hbm.at[:, 1], sems.at[4])
    store_g.start()
    store_t.wait()
    store_g.wait()


def unpack_kernel(in_ref, mixed_ref, grad_ref, gain_ref):
    sel = onehot(send_order())
    for n, out in enumerate((mixed_ref, grad_ref)):
        base = n * 96
        x = jnp.concatenate(
            [in_ref[:, base + l * 16 : base + l * 16 + 16].reshape(TOK, 128) for l in range(6)],
            axis=1,
        )
        for b in range(4):
            y = dot(sel, x[b * 128 : b * 128 + 128], 0, 0).astype(BF)
            for d in range(4):
                out[d, b * 32 : b * 32 + 32] = y[d * 32 : d * 32 + 32]
    g = jnp.sum(in_ref[:, 192:].astype(F32), axis=0)
    gain_ref[...] = jnp.broadcast_to(jnp.sum(g, axis=0, keepdims=True), (8, 128))


def normalise(x):
    xf = x.astype(F32)
    inv_rms = lax.rsqrt(jnp.mean(xf * xf, axis=-1, keepdims=True) + EPS)
    return xf, inv_rms, xf * inv_rms


def main_kernel(
    recv_hbm, gain_ref, feat_ref, wqkv_hbm, wout_hbm,
    keep1_ref, keep2_ref, send1_ref, send2_ref, dqkv_ref, mixed_ref,
    attn_ref, recv_ref, wqkv_ref, wout_ref, qkv_ref, ga_ref, norm_ref, gy_ref, lhs_ref, sems,
):
    scale = float(HEAD_DIM) ** (-0.5)
    loads = [
        pltpu.make_async_copy(src, dst, sems.at[n])
        for n, (src, dst) in enumerate(
            ((recv_hbm, recv_ref), (wout_hbm, wout_ref), (wqkv_hbm, wqkv_ref))
        )
    ]
    for c in loads:
        c.start()
    loads[0].wait()
    _, _, unit = normalise(recv_ref[:, 0].reshape(TOK, D))
    normed = (unit * gain_ref[...]).astype(BF)
    norm_ref[...] = by_position(normed)
    gy_ref[...] = by_position(recv_ref[:, 1].reshape(TOK, D))
    loads[1].wait()
    ga_ref[...] = dot(gy_ref[...], wout_ref[...], 1, 1).astype(BF)
    loads[2].wait()

    def project(n, _):
        cols = pl.ds(pl.multiple_of(n * 768, 768), 768)
        qkv_ref[:, cols] = dot(norm_ref[...], wqkv_ref[:, cols], 1, 0).astype(BF)
        return 0

    lax.fori_loop(0, 3, project, 0, unroll=True)
    first = lax.broadcasted_iota(jnp.int32, (128, 128), 1) < 64

    def split(x):
        zero = jnp.zeros_like(x)
        return jnp.concatenate([jnp.where(first, x, zero), jnp.where(first, zero, x)], axis=0)

    def stack(x):
        return jnp.concatenate([x[:, :128], x[:, 128:]], axis=0)

    def heads(hp, _):
        base = pl.multiple_of(hp * 128, 128)
        rows = [slice(p * 128, (p + 1) * 128) for p in range(4)]
        q = [qkv_ref[r, pl.ds(base, 128)] for r in rows]
        k = [qkv_ref[r, pl.ds(base + D, 128)] for r in rows]
        v = [qkv_ref[r, pl.ds(base + 2 * D, 128)] for r in rows]
        qb = [split(x) for x in q]
        gb = [split(ga_ref[r, pl.ds(base, 128)]) for r in rows]
        s = [dot(k[p], qb[p], 1, 1) for p in range(4)]
        dp = [dot(v[p], gb[p], 1, 1) for p in range(4)]
        pb, ds = [], []
        for p in range(4):
            sp = s[p] * scale
            e = jnp.exp(sp - jnp.max(sp, axis=0, keepdims=True))
            probs = e * (1.0 / jnp.sum(e, axis=0, keepdims=True))
            delta = jnp.sum(probs * dp[p], axis=0, keepdims=True)
            ds.append((probs * (dp[p] - delta) * scale).astype(BF))
            pb.append(probs.astype(BF))
        for p in range(4):
            attn_ref[rows[p], pl.ds(base, 128)] = dot(stack(pb[p]), split(v[p]), 0, 0).astype(BF)
            dqkv_ref[rows[p], pl.ds(base, 128)] = dot(stack(ds[p]), split(k[p]), 0, 0).astype(BF)
            dqkv_ref[rows[p], pl.ds(base + D, 128)] = dot(ds[p], qb[p], 1, 0).astype(BF)
            dqkv_ref[rows[p], pl.ds(base + 2 * D, 128)] = dot(pb[p], gb[p], 1, 0).astype(BF)
        return 0

    lax.fori_loop(0, HEADS // 2, heads, 0, unroll=True)
    pick = onehot(lax.broadcasted_iota(jnp.int32, (D, D), 0) == feat_ref[...])
    lhs_ref[...] = dot(pick, norm_ref[...], 0, 1).astype(BF)

    def place_rows(g, n):
        cols = slice(n * D, n * D + D)
        for r, (first, second) in ((0, (keep1_ref, keep2_ref)), (384, (send1_ref, send2_ref))):
            own, one, two, three = (g[r + k * 96 : r + k * 96 + 96] for k in range(4))
            up, down, hold = (two, three, one) if n < 2 else (one, two, three)
            first[:96, cols] = up
            first[96:, cols] = down
            second[:96, cols] = own
            second[96:, cols] = hold

    for n in range(3):
        place_rows(dot(lhs_ref[...], dqkv_ref[:, n * D : n * D + D], 1, 0).astype(BF), n)
    lhs_ref[...] = dot(pick, attn_ref[...], 0, 1).astype(BF)
    place_rows(dot(lhs_ref[...], gy_ref[...], 1, 0).astype(BF), 3)
    proj = dot(by_source(attn_ref[...]), wout_ref[...], 1, 0).astype(BF)
    mixed = (recv_ref[:, 0].reshape(TOK, D).astype(F32) + proj.astype(F32)).astype(BF)
    for l in range(6):
        mixed_ref[:, l * 16 : l * 16 + 16] = mixed[:, l * 128 : l * 128 + 128].reshape(32, 16, 128)


def token_kernel(
    recv_ref, gain_ref, dqkv_ref, wqkv_ref, mixed_ref, ret_hbm, ret_ref, sems
):
    store_m = pltpu.make_async_copy(mixed_ref, ret_hbm.at[:, :96], sems.at[1])
    store_m.start()
    gn = dot(dqkv_ref[...], wqkv_ref[...], 1, 1).astype(BF)
    gn = by_source(gn).astype(F32)
    _, inv_rms, unit = normalise(recv_ref[:, 0].reshape(TOK, D))
    g = jnp.sum(gn * unit, axis=0, keepdims=True)
    dunit = gn * gain_ref[...]
    back = inv_rms * (dunit - unit * jnp.mean(dunit * unit, axis=-1, keepdims=True))
    gy = recv_ref[:, 1].reshape(TOK, D).astype(F32)
    grad = (gy + back).astype(BF)
    for l in range(6):
        ret_ref[:, l * 16 : l * 16 + 16] = grad[:, l * 128 : l * 128 + 128].reshape(32, 16, 128)
    k = lax.broadcasted_iota(jnp.int32, (32, 8, 128), 0) * 24
    lane = lax.broadcasted_iota(jnp.int32, (32, 8, 128), 2)
    own = jnp.zeros((32, 8, 128), F32)
    for l in range(6):
        f = lane + l * 128
        part = g[:, l * 128 : l * 128 + 128].reshape(1, 1, 128)
        own = own + jnp.where(jnp.logical_and(f >= k, f < k + 24), part, 0.0)
    high = own.astype(BF).astype(F32)
    mid = (own - high).astype(BF).astype(F32)
    row = lax.broadcasted_iota(jnp.int32, (32, 8, 128), 1)
    low = own - high - mid
    terms = jnp.where(row == 0, high, jnp.where(row == 1, mid, jnp.where(row == 2, low, 0.0)))
    ret_ref[:, 96:] = terms.astype(BF)
    store_g = pltpu.make_async_copy(ret_ref, ret_hbm.at[:, 96:], sems.at[0])
    store_g.start()
    store_m.wait()
    store_g.wait()


HALF = 2 * D


def pair_sum_kernel(a_ref, b_ref, up, down):
    up[...] = (a_ref[:96].astype(F32) + b_ref[:96].astype(F32)).astype(BF)
    down[...] = (a_ref[96:].astype(F32) + b_ref[96:].astype(F32)).astype(BF)


def pass_on_kernel(a_ref, b_ref, up, down, up_out, down_out, sum_out):
    left, right = slice(0, HALF), slice(HALF, 2 * HALF)

    def pair(rows, cols):
        return a_ref[rows, cols].astype(F32) + b_ref[rows, cols].astype(F32)

    own, hold = slice(0, 96), slice(96, 192)
    up_out[...] = (pair(hold, left) + up[:, left].astype(F32)).astype(BF)
    down_out[...] = (pair(hold, right) + down[:, right].astype(F32)).astype(BF)
    sum_out[:, left] = pair(own, left) + down[:, left].astype(F32)
    sum_out[:, right] = pair(own, right) + up[:, right].astype(F32)


def ring_sum_kernel(near, up_far, down_far, o):
    for q in range(4):
        r = slice(q * 24, q * 24 + 24)
        x = near[r, :HALF] + up_far[r].astype(F32)
        y = near[r, HALF:] + down_far[r].astype(F32)
        for k in range(4):
            pieces = [
                v[k * 6 : k * 6 + 6, l * 128 : l * 128 + 128] for v in (x, y) for l in range(12)
            ]
            o[q * 4 + k] = jnp.concatenate(pieces, axis=0).astype(BF)


def final_kernel(first_ref, in_ref, g0, g1, g2, g3, qkv_ref, out_ref, gain_ref, sum_ref):
    sum_ref[...] = jnp.sum(in_ref[...].astype(F32), axis=0)
    for l in range(24):
        v = sum_ref[l * 6 : l * 6 + 6]
        if l < 18:
            qkv_ref[:, l * 128 : l * 128 + 128] = v
        else:
            out_ref[:, (l - 18) * 128 : (l - 17) * 128] = v
    g = (g0[...] + g1[...]) + (g2[...] + g3[...])
    r = lax.broadcasted_iota(jnp.int32, (8, 128), 0)
    lane = lax.broadcasted_iota(jnp.int32, (8, 128), 1)
    mine = jnp.sum(
        jnp.where(lane == ((first_ref[0] + r) & 127), g, 0.0), axis=1, keepdims=True
    )
    gain_ref[...] = jnp.sum(jnp.where(lane == r, mine, 0.0), axis=0, keepdims=True)[:, :6]


def params(mb):
    return pltpu.CompilerParams(vmem_limit_bytes=int(mb * MB))


def cost(flops, nbytes):
    return pl.CostEstimate(flops=int(flops), bytes_accessed=int(nbytes), transcendentals=0)


def shape(*dims, dtype=BF):
    return jax.ShapeDtypeStruct(dims, dtype)


HBM = pl.BlockSpec(memory_space=pltpu.HBM)
VM = pl.BlockSpec(memory_space=pltpu.VMEM)
DMA = pltpu.SemaphoreType.DMA


def per_device(tokens, cotangent, lesion, w_qkv, w_out, norm_gain):
    gain = norm_gain.reshape(1, D)
    depth = lax.axis_index("depth")
    mod = lax.axis_index("mod")
    feat = lax.dynamic_slice(jnp.asarray(FEATURES), ((depth & 1) * 4 + (mod & 3), 0), (1, D))
    first = ((depth * 8 + mod) * 6).astype(jnp.int32).reshape(1)
    packed = pl.pallas_call(
        pack_kernel, out_shape=shape(32, 2, 16, D), in_specs=[HBM] * 3, out_specs=HBM,
        scratch_shapes=[
            pltpu.VMEM((4, 128, D), BF), pltpu.VMEM((4, 128, D), BF), pltpu.VMEM((4, 128), jnp.int32),
            pltpu.VMEM((2, 32, 16, D), BF), DMA((5,)),
        ],
        compiler_params=params(60), cost_estimate=cost(1e9, 4e6), name="pack",
    )(tokens, cotangent, lesion)
    recv = lax.all_to_all(packed, AXES, 0, 0, tiled=True, axis_index_groups=PLANE)
    keep1, keep2, send1, send2, dqkv, mixed_rows = pl.pallas_call(
        main_kernel,
        out_shape=(*(shape(192, 4 * D) for _ in range(4)), shape(TOK, 3 * D), shape(32, 96, 128)),
        in_specs=[HBM, VM, VM, HBM, HBM],
        scratch_shapes=[
            pltpu.VMEM((TOK, D), BF), pltpu.VMEM((32, 2, 16, D), BF), pltpu.VMEM((D, 3 * D), BF), pltpu.VMEM((D, D), BF),
            pltpu.VMEM((TOK, 3 * D), BF), pltpu.VMEM((TOK, D), BF), pltpu.VMEM((TOK, D), BF),
            pltpu.VMEM((TOK, D), BF), pltpu.VMEM((D, TOK), BF), DMA((3,)),
        ],
        compiler_params=params(MAIN_MB), cost_estimate=cost(1e10, 1.5e7), name="main",
    )(recv, gain, feat, w_qkv, w_out)
    got1 = lax.ppermute(send1, AXES, CORE_SWAP)
    got2 = lax.ppermute(send2, AXES, CORE_SWAP)
    ret = pl.pallas_call(
        token_kernel, out_shape=shape(32, 200, 128), out_specs=HBM,
        scratch_shapes=[pltpu.VMEM((32, 104, 128), BF), DMA((2,))],
        compiler_params=params(TOKEN_MB), cost_estimate=cost(2.8e9, 1e7), name="token_grads",
    )(recv, gain, dqkv, w_qkv, mixed_rows)
    up, down = pl.pallas_call(
        pair_sum_kernel, out_shape=(shape(96, 4 * D), shape(96, 4 * D)),
        compiler_params=params(6), cost_estimate=cost(1e6, 3e6), name="pair_sum",
    )(keep1, got1)
    up, down, ret = lax.optimization_barrier((up, down, ret))
    up = lax.ppermute(up, AXES, y_shift(1))
    down = lax.ppermute(down, AXES, y_shift(3))
    up_far, down_far, near = pl.pallas_call(
        pass_on_kernel,
        out_shape=(shape(96, HALF), shape(96, HALF), shape(96, 4 * D, dtype=F32)),
        compiler_params=params(6), cost_estimate=cost(PASS, 3e6), name="pass_on",
    )(keep2, got2, up, down)
    up_far = lax.ppermute(up_far, AXES, y_shift(1))
    down_far = lax.ppermute(down_far, AXES, y_shift(3))
    back = lax.all_to_all(ret, AXES, 0, 0, tiled=True, axis_index_groups=PLANE)
    mine = pl.pallas_call(
        ring_sum_kernel, out_shape=shape(16, 144, 128),
        compiler_params=params(6), cost_estimate=cost(RING, 3e6), name="ring_sum",
    )(near, up_far, down_far)
    mixed, grad_tokens, gain_part = pl.pallas_call(
        unpack_kernel,
        out_shape=(shape(4, 128, D), shape(4, 128, D), shape(8, 128, dtype=F32)),
        compiler_params=params(14), cost_estimate=cost(1e9, 4e6), name="unpack",
    )(back)
    last = lax.all_to_all(mine, AXES, 0, 0, tiled=True, axis_index_groups=CHIPS)
    gains = [gain_part] + [lax.ppermute(gain_part, AXES, y_shift(s)) for s in range(1, 4)]
    grad_qkv, grad_out, grad_gain = pl.pallas_call(
        final_kernel,
        out_shape=(shape(6, 3 * D, dtype=F32), shape(6, D, dtype=F32), shape(1, 6, dtype=F32)),
        in_specs=[pl.BlockSpec(memory_space=pltpu.SMEM)] + [VM] * 5,
        scratch_shapes=[pltpu.VMEM((144, 128), F32)],
        compiler_params=params(6), cost_estimate=cost(1e6, 1e6), name="final",
    )(first, last, *gains)
    return mixed, grad_tokens, grad_qkv, grad_out, grad_gain.reshape(6)


def solution(mesh):
    in_specs = (P("depth", "mod", None), P("depth", "mod", None), P("depth", "mod"), P(), P(), P())
    out_specs = (
        P("depth", "mod", None),
        P("depth", "mod", None),
        P(("depth", "mod"), None),
        P(("depth", "mod"), None),
        P(("depth", "mod")),
    )
    return jax.shard_map(
        per_device, mesh=mesh, in_specs=in_specs, out_specs=out_specs, check_vma=False
    )
```

```python
import jax
import jax.numpy as jnp
import numpy as np
from jax import lax
from jax.experimental import pallas as pl
from jax.experimental.pallas import tpu as pltpu
from jax.sharding import PartitionSpec as P

HEADS = 12
HEAD_DIM = 64
EPS = 1e-06
LESION_GAIN = 3.0
D = 768
TOK = 512
AXES = ("depth", "mod")
BF = jnp.bfloat16
F32 = jnp.float32
MB = 1024 * 1024
PASS = 1e6
RING = 1e10
MAIN_MB = 42
TOKEN_MB = 14


def place(xlo, z, c, xhi, y):
    return (xlo * 8 + z * 2 + c) * 8 + xhi * 4 + y


def parts_of(i):
    d, m = divmod(i, 8)
    return d // 8, (d // 2) % 4, d % 2, m // 4, m % 4


PLANE = [
    [place(a, z, c, b, y) for a in range(2) for z in range(4) for c in range(2) for b in range(2)]
    for y in range(4)
]
CHIPS = [
    [place(a, z, c, b, y) for a in range(2) for z in range(4) for b in range(2)]
    for c in range(2)
    for y in range(4)
]
CORE_SWAP = [(i, i ^ 8) for i in range(128)]


def y_shift(s):
    out = []
    for i in range(128):
        a, z, c, b, y = parts_of(i)
        out.append((i, place(a, z, c, b, (y + s) % 4)))
    return out


def feature_table():
    table = np.zeros((8, D), np.int32)
    for c in range(2):
        for y in range(4):
            n = 0
            for rc in range(2):
                for ry in range(4):
                    for a in range(2):
                        for z in range(4):
                            for b in range(2):
                                i = place(a, z, c ^ rc, b, (y + ry) % 4)
                                for r in range(6):
                                    table[c * 4 + y, n] = 6 * i + r
                                    n += 1
    return table


FEATURES = feature_table()


def dot(a, b, ca, cb):
    return lax.dot_general(a, b, (((ca,), (cb,)), ((), ())), preferred_element_type=F32)


def onehot(mask):
    return jnp.where(mask, 1.0, 0.0).astype(BF)


def rows_and_columns():
    i = lax.broadcasted_iota(jnp.int32, (128, 128), 0)
    return i, lax.broadcasted_iota(jnp.int32, (128, 128), 1)


def send_order():
    i, s = rows_and_columns()
    return s == ((i >> 2) & 3) * 32 + (i >> 4) * 4 + (i & 3)


def position_order():
    i, s = rows_and_columns()
    return onehot(s == ((i >> 2) & 7) * 16 + (i & 3) * 4 + (i >> 5))


def by_position(x):
    order = position_order()
    parts = [dot(order, x[n * 128 : n * 128 + 128], 1, 0).astype(BF) for n in range(4)]
    return jnp.concatenate(
        [parts[n][p * 32 : p * 32 + 32] for p in range(4) for n in range(4)], axis=0
    )


def by_source(x):
    order = position_order()
    parts = [
        jnp.concatenate([x[p * 128 + n * 32 : p * 128 + n * 32 + 32] for p in range(4)], axis=0)
        for n in range(4)
    ]
    return jnp.concatenate([dot(order, part, 0, 0).astype(BF) for part in parts], axis=0)


def pack_kernel(tok_hbm, cot_hbm, les_hbm, out_hbm, tok_ref, cot_ref, les_ref, out_ref, sems):
    loads = [
        pltpu.make_async_copy(src, dst, sems.at[n])
        for n, (src, dst) in enumerate(
            ((les_hbm, les_ref), (tok_hbm, tok_ref), (cot_hbm, cot_ref))
        )
    ]
    for c in loads:
        c.start()
    mask = send_order()
    plain = onehot(mask)

    def block(ref, n):
        return jnp.concatenate([ref[d, n * 32 : n * 32 + 32] for d in range(4)], axis=0)

    stores = []

    def put(which, n, x):
        out_ref[which, n * 8 : n * 8 + 8] = x.reshape(8, 16, D)
        store = pltpu.make_async_copy(
            out_ref.at[which, pl.ds(n * 8, 8)],
            out_hbm.at[pl.ds(n * 8, 8), which],
            sems.at[3 + which * 4 + n],
        )
        store.start()
        stores.append(store)

    loads[1].wait()
    for n in range(4):
        t = dot(plain, block(tok_ref, n), 1, 0).astype(BF)
        put(0, n, t)
    loads[0].wait()
    weight = 1.0 + LESION_GAIN * les_ref[...].astype(F32)
    loads[2].wait()
    for n in range(4):
        row = jnp.concatenate([weight[d : d + 1, n * 32 : n * 32 + 32] for d in range(4)], axis=1)
        scaled = jnp.where(mask, row, 0.0).astype(BF)
        g = dot(scaled, block(cot_ref, n), 1, 0).astype(BF)
        put(1, n, g)
    for c in stores:
        c.wait()


def unpack_kernel(in_ref, mixed_ref, grad_ref, gain_ref):
    sel = onehot(send_order())
    for n, out in enumerate((mixed_ref, grad_ref)):
        base = n * 96
        x = jnp.concatenate(
            [in_ref[:, base + l * 16 : base + l * 16 + 16].reshape(TOK, 128) for l in range(6)],
            axis=1,
        )
        for b in range(4):
            y = dot(sel, x[b * 128 : b * 128 + 128], 0, 0).astype(BF)
            for d in range(4):
                out[d, b * 32 : b * 32 + 32] = y[d * 32 : d * 32 + 32]
    g = jnp.sum(in_ref[:, 192:].astype(F32), axis=0)
    gain_ref[...] = jnp.broadcast_to(jnp.sum(g, axis=0, keepdims=True), (8, 128))


def normalise(x):
    xf = x.astype(F32)
    inv_rms = lax.rsqrt(jnp.mean(xf * xf, axis=-1, keepdims=True) + EPS)
    return xf, inv_rms, xf * inv_rms


def order_kernel(feat_ref, wout_ref, out_ref):
    out_ref[...] = feat_ref[...]


def main_kernel(
    recv_hbm, gain_ref, feat_ref, wqkv_hbm, wout_hbm,
    keep1_ref, keep2_ref, send1_ref, send2_ref, attn_ref, dqkv_ref,
    recv_ref, wqkv_ref, wout_ref, qkv_ref, ga_ref, norm_ref, gy_ref, lhs_ref, sems,
):
    scale = float(HEAD_DIM) ** (-0.5)
    loads = [
        pltpu.make_async_copy(src, dst, sems.at[n])
        for n, (src, dst) in enumerate(
            ((recv_hbm, recv_ref), (wout_hbm, wout_ref), (wqkv_hbm, wqkv_ref))
        )
    ]
    for c in loads:
        c.start()
    loads[0].wait()
    _, _, unit = normalise(recv_ref[:, 0].reshape(TOK, D))
    normed = (unit * gain_ref[...]).astype(BF)
    norm_ref[...] = by_position(normed)
    gy_ref[...] = by_position(recv_ref[:, 1].reshape(TOK, D))
    loads[1].wait()
    ga_ref[...] = dot(gy_ref[...], wout_ref[...], 1, 1).astype(BF)
    loads[2].wait()

    def project(n, _):
        cols = pl.ds(pl.multiple_of(n * 768, 768), 768)
        qkv_ref[:, cols] = dot(norm_ref[...], wqkv_ref[:, cols], 1, 0).astype(BF)
        return 0

    lax.fori_loop(0, 3, project, 0, unroll=True)
    first = lax.broadcasted_iota(jnp.int32, (128, 128), 1) < 64

    def split(x):
        zero = jnp.zeros_like(x)
        return jnp.concatenate([jnp.where(first, x, zero), jnp.where(first, zero, x)], axis=0)

    def stack(x):
        return jnp.concatenate([x[:, :128], x[:, 128:]], axis=0)

    def heads(hp, _):
        base = pl.multiple_of(hp * 128, 128)
        rows = [slice(p * 128, (p + 1) * 128) for p in range(4)]
        q = [qkv_ref[r, pl.ds(base, 128)] for r in rows]
        k = [qkv_ref[r, pl.ds(base + D, 128)] for r in rows]
        v = [qkv_ref[r, pl.ds(base + 2 * D, 128)] for r in rows]
        qb = [split(x) for x in q]
        gb = [split(ga_ref[r, pl.ds(base, 128)]) for r in rows]
        s = [dot(k[p], qb[p], 1, 1) for p in range(4)]
        dp = [dot(v[p], gb[p], 1, 1) for p in range(4)]
        pb, ds = [], []
        for p in range(4):
            sp = s[p] * scale
            e = jnp.exp(sp - jnp.max(sp, axis=0, keepdims=True))
            probs = e * (1.0 / jnp.sum(e, axis=0, keepdims=True))
            delta = jnp.sum(probs * dp[p], axis=0, keepdims=True)
            ds.append((probs * (dp[p] - delta) * scale).astype(BF))
            pb.append(probs.astype(BF))
        for p in range(4):
            attn_ref[rows[p], pl.ds(base, 128)] = dot(stack(pb[p]), split(v[p]), 0, 0).astype(BF)
            dqkv_ref[rows[p], pl.ds(base, 128)] = dot(stack(ds[p]), split(k[p]), 0, 0).astype(BF)
            dqkv_ref[rows[p], pl.ds(base + D, 128)] = dot(ds[p], qb[p], 1, 0).astype(BF)
            dqkv_ref[rows[p], pl.ds(base + 2 * D, 128)] = dot(pb[p], gb[p], 1, 0).astype(BF)
        return 0

    lax.fori_loop(0, HEADS // 2, heads, 0, unroll=True)
    pick = onehot(lax.broadcasted_iota(jnp.int32, (D, D), 0) == feat_ref[...])
    lhs_ref[...] = dot(pick, norm_ref[...], 0, 1).astype(BF)

    def place_rows(g, n):
        cols = slice(n * D, n * D + D)
        for r, (first, second) in ((0, (keep1_ref, keep2_ref)), (384, (send1_ref, send2_ref))):
            own, one, two, three = (g[r + k * 96 : r + k * 96 + 96] for k in range(4))
            up, down, hold = (two, three, one) if n < 2 else (one, two, three)
            first[:96, cols] = up
            first[96:, cols] = down
            second[:96, cols] = own
            second[96:, cols] = hold

    for n in range(3):
        place_rows(dot(lhs_ref[...], dqkv_ref[:, n * D : n * D + D], 1, 0).astype(BF), n)
    lhs_ref[...] = dot(pick, attn_ref[...], 0, 1).astype(BF)
    place_rows(dot(lhs_ref[...], gy_ref[...], 1, 0).astype(BF), 3)


def token_kernel(recv_ref, gain_ref, dqkv_ref, wqkv_ref, ret_ref):
    gn = dot(dqkv_ref[...], wqkv_ref[...], 1, 1).astype(BF)
    gn = by_source(gn).astype(F32)
    _, inv_rms, unit = normalise(recv_ref[:, 0].reshape(TOK, D))
    g = jnp.sum(gn * unit, axis=0, keepdims=True)
    dunit = gn * gain_ref[...]
    back = inv_rms * (dunit - unit * jnp.mean(dunit * unit, axis=-1, keepdims=True))
    gy = recv_ref[:, 1].reshape(TOK, D).astype(F32)
    grad = (gy + back).astype(BF)
    for l in range(6):
        ret_ref[:, l * 16 : l * 16 + 16] = grad[:, l * 128 : l * 128 + 128].reshape(32, 16, 128)
    k = lax.broadcasted_iota(jnp.int32, (32, 8, 128), 0) * 24
    lane = lax.broadcasted_iota(jnp.int32, (32, 8, 128), 2)
    own = jnp.zeros((32, 8, 128), F32)
    for l in range(6):
        f = lane + l * 128
        part = g[:, l * 128 : l * 128 + 128].reshape(1, 1, 128)
        own = own + jnp.where(jnp.logical_and(f >= k, f < k + 24), part, 0.0)
    high = own.astype(BF).astype(F32)
    mid = (own - high).astype(BF).astype(F32)
    row = lax.broadcasted_iota(jnp.int32, (32, 8, 128), 1)
    low = own - high - mid
    terms = jnp.where(row == 0, high, jnp.where(row == 1, mid, jnp.where(row == 2, low, 0.0)))
    ret_ref[:, 96:] = terms.astype(BF)


def mixed_kernel(recv_ref, attn_ref, wout_ref, grad_ref, ret_hbm, ret_ref, sems):
    store_g = pltpu.make_async_copy(grad_ref, ret_hbm.at[:, 96:], sems.at[0])
    store_g.start()
    attn = by_source(attn_ref[...])
    proj = dot(attn, wout_ref[...], 1, 0).astype(BF)
    mixed = (recv_ref[:, 0].reshape(TOK, D).astype(F32) + proj.astype(F32)).astype(BF)
    for l in range(6):
        ret_ref[:, l * 16 : l * 16 + 16] = mixed[:, l * 128 : l * 128 + 128].reshape(32, 16, 128)
    store_m = pltpu.make_async_copy(ret_ref, ret_hbm.at[:, :96], sems.at[1])
    store_m.start()
    store_g.wait()
    store_m.wait()


HALF = 2 * D


def pair_sum_kernel(a_ref, b_ref, up, down):
    up[...] = (a_ref[:96].astype(F32) + b_ref[:96].astype(F32)).astype(BF)
    down[...] = (a_ref[96:].astype(F32) + b_ref[96:].astype(F32)).astype(BF)


def pass_on_kernel(a_ref, b_ref, up, down, up_out, down_out, sum_out):
    left, right = slice(0, HALF), slice(HALF, 2 * HALF)

    def pair(rows, cols):
        return a_ref[rows, cols].astype(F32) + b_ref[rows, cols].astype(F32)

    own, hold = slice(0, 96), slice(96, 192)
    up_out[...] = (pair(hold, left) + up[:, left].astype(F32)).astype(BF)
    down_out[...] = (pair(hold, right) + down[:, right].astype(F32)).astype(BF)
    sum_out[:, left] = pair(own, left) + down[:, left].astype(F32)
    sum_out[:, right] = pair(own, right) + up[:, right].astype(F32)


def ring_sum_kernel(near, up_far, down_far, o):
    for q in range(4):
        r = slice(q * 24, q * 24 + 24)
        x = near[r, :HALF] + up_far[r].astype(F32)
        y = near[r, HALF:] + down_far[r].astype(F32)
        for k in range(4):
            pieces = [
                v[k * 6 : k * 6 + 6, l * 128 : l * 128 + 128] for v in (x, y) for l in range(12)
            ]
            o[q * 4 + k] = jnp.concatenate(pieces, axis=0).astype(BF)


def final_kernel(first_ref, in_ref, g0, g1, g2, g3, qkv_ref, out_ref, gain_ref, sum_ref):
    sum_ref[...] = jnp.sum(in_ref[...].astype(F32), axis=0)
    for l in range(24):
        v = sum_ref[l * 6 : l * 6 + 6]
        if l < 18:
            qkv_ref[:, l * 128 : l * 128 + 128] = v
        else:
            out_ref[:, (l - 18) * 128 : (l - 17) * 128] = v
    g = (g0[...] + g1[...]) + (g2[...] + g3[...])
    r = lax.broadcasted_iota(jnp.int32, (8, 128), 0)
    lane = lax.broadcasted_iota(jnp.int32, (8, 128), 1)
    mine = jnp.sum(
        jnp.where(lane == ((first_ref[0] + r) & 127), g, 0.0), axis=1, keepdims=True
    )
    gain_ref[...] = jnp.sum(jnp.where(lane == r, mine, 0.0), axis=0, keepdims=True)[:, :6]


def params(mb):
    return pltpu.CompilerParams(vmem_limit_bytes=int(mb * MB))


def cost(flops, nbytes):
    return pl.CostEstimate(flops=int(flops), bytes_accessed=int(nbytes), transcendentals=0)


def shape(*dims, dtype=BF):
    return jax.ShapeDtypeStruct(dims, dtype)


HBM = pl.BlockSpec(memory_space=pltpu.HBM)
VM = pl.BlockSpec(memory_space=pltpu.VMEM)
DMA = pltpu.SemaphoreType.DMA


def per_device(tokens, cotangent, lesion, w_qkv, w_out, norm_gain):
    gain = norm_gain.reshape(1, D)
    depth = lax.axis_index("depth")
    mod = lax.axis_index("mod")
    feat = lax.dynamic_slice(jnp.asarray(FEATURES), ((depth & 1) * 4 + (mod & 3), 0), (1, D))
    first = ((depth * 8 + mod) * 6).astype(jnp.int32).reshape(1)
    packed = pl.pallas_call(
        pack_kernel, out_shape=shape(32, 2, 16, D), in_specs=[HBM] * 3, out_specs=HBM,
        scratch_shapes=[
            pltpu.VMEM((4, 128, D), BF), pltpu.VMEM((4, 128, D), BF), pltpu.VMEM((4, 128), jnp.int32),
            pltpu.VMEM((2, 32, 16, D), BF), DMA((11,)),
        ],
        compiler_params=params(60), cost_estimate=cost(1e9, 4e6), name="pack",
    )(tokens, cotangent, lesion)
    feat = pl.pallas_call(
        order_kernel, out_shape=shape(1, D, dtype=jnp.int32), compiler_params=params(2),
        cost_estimate=cost(1e6, 1e6), name="order",
    )(feat, w_out)
    recv = lax.all_to_all(packed, AXES, 0, 0, tiled=True, axis_index_groups=PLANE)
    keep1, keep2, send1, send2, attn, dqkv = pl.pallas_call(
        main_kernel,
        out_shape=(*(shape(192, 4 * D) for _ in range(4)), shape(TOK, D), shape(TOK, 3 * D)),
        in_specs=[HBM, VM, VM, HBM, HBM],
        scratch_shapes=[
            pltpu.VMEM((32, 2, 16, D), BF), pltpu.VMEM((D, 3 * D), BF), pltpu.VMEM((D, D), BF),
            pltpu.VMEM((TOK, 3 * D), BF), pltpu.VMEM((TOK, D), BF), pltpu.VMEM((TOK, D), BF),
            pltpu.VMEM((TOK, D), BF), pltpu.VMEM((D, TOK), BF), DMA((3,)),
        ],
        compiler_params=params(MAIN_MB), cost_estimate=cost(1e10, 1.5e7), name="main",
    )(recv, gain, feat, w_qkv, w_out)
    got1 = lax.ppermute(send1, AXES, CORE_SWAP)
    got2 = lax.ppermute(send2, AXES, CORE_SWAP)
    grads = pl.pallas_call(
        token_kernel, out_shape=shape(32, 104, 128),
        compiler_params=params(TOKEN_MB), cost_estimate=cost(2.8e9, 9e6), name="token_grads",
    )(recv, gain, dqkv, w_qkv)
    up, down = pl.pallas_call(
        pair_sum_kernel, out_shape=(shape(96, 4 * D), shape(96, 4 * D)),
        compiler_params=params(6), cost_estimate=cost(1e6, 3e6), name="pair_sum",
    )(keep1, got1)
    up, down, attn, grads = lax.optimization_barrier((up, down, attn, grads))
    ret = pl.pallas_call(
        mixed_kernel, out_shape=shape(32, 200, 128), out_specs=HBM,
        scratch_shapes=[pltpu.VMEM((32, 96, 128), BF), DMA((2,))],
        compiler_params=params(14), cost_estimate=cost(1e9, 5e6), name="mixed",
    )(recv, attn, w_out, grads)
    up = lax.ppermute(up, AXES, y_shift(1))
    down = lax.ppermute(down, AXES, y_shift(3))
    up_far, down_far, near = pl.pallas_call(
        pass_on_kernel,
        out_shape=(shape(96, HALF), shape(96, HALF), shape(96, 4 * D, dtype=F32)),
        compiler_params=params(6), cost_estimate=cost(PASS, 3e6), name="pass_on",
    )(keep2, got2, up, down)
    up_far = lax.ppermute(up_far, AXES, y_shift(1))
    down_far = lax.ppermute(down_far, AXES, y_shift(3))
    back = lax.all_to_all(ret, AXES, 0, 0, tiled=True, axis_index_groups=PLANE)
    mine = pl.pallas_call(
        ring_sum_kernel, out_shape=shape(16, 144, 128),
        compiler_params=params(6), cost_estimate=cost(RING, 3e6), name="ring_sum",
    )(near, up_far, down_far)
    mixed, grad_tokens, gain_part = pl.pallas_call(
        unpack_kernel,
        out_shape=(shape(4, 128, D), shape(4, 128, D), shape(8, 128, dtype=F32)),
        compiler_params=params(14), cost_estimate=cost(1e9, 4e6), name="unpack",
    )(back)
    last = lax.all_to_all(mine, AXES, 0, 0, tiled=True, axis_index_groups=CHIPS)
    gains = [gain_part] + [lax.ppermute(gain_part, AXES, y_shift(s)) for s in range(1, 4)]
    grad_qkv, grad_out, grad_gain = pl.pallas_call(
        final_kernel,
        out_shape=(shape(6, 3 * D, dtype=F32), shape(6, D, dtype=F32), shape(1, 6, dtype=F32)),
        in_specs=[pl.BlockSpec(memory_space=pltpu.SMEM)] + [VM] * 5,
        scratch_shapes=[pltpu.VMEM((144, 128), F32)],
        compiler_params=params(6), cost_estimate=cost(1e6, 1e6), name="final",
    )(first, last, *gains)
    return mixed, grad_tokens, grad_qkv, grad_out, grad_gain.reshape(6)


def solution(mesh):
    in_specs = (P("depth", "mod", None), P("depth", "mod", None), P("depth", "mod"), P(), P(), P())
    out_specs = (
        P("depth", "mod", None),
        P("depth", "mod", None),
        P(("depth", "mod"), None),
        P(("depth", "mod"), None),
        P(("depth", "mod")),
    )
    return jax.shard_map(
        per_device, mesh=mesh, in_specs=in_specs, out_specs=out_specs, check_vma=False
    )
```

```python
import jax
import jax.numpy as jnp
import numpy as np
from jax import lax
from jax.experimental import pallas as pl
from jax.experimental.pallas import tpu as pltpu
from jax.sharding import PartitionSpec as P

HEADS = 12
HEAD_DIM = 64
EPS = 1e-06
LESION_GAIN = 3.0
D = 768
TOK = 512
AXES = ("depth", "mod")
BF = jnp.bfloat16
F32 = jnp.float32
MB = 1024 * 1024
PASS = 1e6
RING = 1e10
MAIN_MB = 42
TOKEN_MB = 14


def place(xlo, z, c, xhi, y):
    return (xlo * 8 + z * 2 + c) * 8 + xhi * 4 + y


def parts_of(i):
    d, m = divmod(i, 8)
    return d // 8, (d // 2) % 4, d % 2, m // 4, m % 4


PLANE = [
    [place(a, z, c, b, y) for a in range(2) for z in range(4) for c in range(2) for b in range(2)]
    for y in range(4)
]
CHIPS = [
    [place(a, z, c, b, y) for a in range(2) for z in range(4) for b in range(2)]
    for c in range(2)
    for y in range(4)
]
CORE_SWAP = [(i, i ^ 8) for i in range(128)]


def y_shift(s):
    out = []
    for i in range(128):
        a, z, c, b, y = parts_of(i)
        out.append((i, place(a, z, c, b, (y + s) % 4)))
    return out


def feature_table():
    table = np.zeros((8, D), np.int32)
    for c in range(2):
        for y in range(4):
            n = 0
            for rc in range(2):
                for ry in range(4):
                    for a in range(2):
                        for z in range(4):
                            for b in range(2):
                                i = place(a, z, c ^ rc, b, (y + ry) % 4)
                                for r in range(6):
                                    table[c * 4 + y, n] = 6 * i + r
                                    n += 1
    return table


FEATURES = feature_table()


def dot(a, b, ca, cb):
    return lax.dot_general(a, b, (((ca,), (cb,)), ((), ())), preferred_element_type=F32)


def onehot(mask):
    return jnp.where(mask, 1.0, 0.0).astype(BF)


def rows_and_columns():
    i = lax.broadcasted_iota(jnp.int32, (128, 128), 0)
    return i, lax.broadcasted_iota(jnp.int32, (128, 128), 1)


def send_order():
    i, s = rows_and_columns()
    return s == ((i >> 2) & 3) * 32 + (i >> 4) * 4 + (i & 3)


def position_order():
    i, s = rows_and_columns()
    return onehot(s == ((i >> 2) & 7) * 16 + (i & 3) * 4 + (i >> 5))


def by_position(x):
    order = position_order()
    parts = [dot(order, x[n * 128 : n * 128 + 128], 1, 0).astype(BF) for n in range(4)]
    return jnp.concatenate(
        [parts[n][p * 32 : p * 32 + 32] for p in range(4) for n in range(4)], axis=0
    )


def by_source(x):
    order = position_order()
    parts = [
        jnp.concatenate([x[p * 128 + n * 32 : p * 128 + n * 32 + 32] for p in range(4)], axis=0)
        for n in range(4)
    ]
    return jnp.concatenate([dot(order, part, 0, 0).astype(BF) for part in parts], axis=0)


def pack_kernel(tok_hbm, cot_hbm, les_hbm, out_hbm, tok_ref, cot_ref, les_ref, out_ref, sems):
    loads = [
        pltpu.make_async_copy(src, dst, sems.at[n])
        for n, (src, dst) in enumerate(
            ((les_hbm, les_ref), (tok_hbm, tok_ref), (cot_hbm, cot_ref))
        )
    ]
    for c in loads:
        c.start()
    mask = send_order()
    plain = onehot(mask)

    def block(ref, n):
        return jnp.concatenate([ref[d, n * 32 : n * 32 + 32] for d in range(4)], axis=0)

    stores = []

    def put(which, n, x):
        out_ref[which, n * 8 : n * 8 + 8] = x.reshape(8, 16, D)
        store = pltpu.make_async_copy(
            out_ref.at[which, pl.ds(n * 8, 8)],
            out_hbm.at[pl.ds(n * 8, 8), which],
            sems.at[3 + which * 4 + n],
        )
        store.start()
        stores.append(store)

    loads[1].wait()
    for n in range(4):
        t = dot(plain, block(tok_ref, n), 1, 0).astype(BF)
        put(0, n, t)
    loads[0].wait()
    weight = 1.0 + LESION_GAIN * les_ref[...].astype(F32)
    loads[2].wait()
    for n in range(4):
        row = jnp.concatenate([weight[d : d + 1, n * 32 : n * 32 + 32] for d in range(4)], axis=1)
        scaled = jnp.where(mask, row, 0.0).astype(BF)
        g = dot(scaled, block(cot_ref, n), 1, 0).astype(BF)
        put(1, n, g)
    for c in stores:
        c.wait()


def unpack_kernel(in_ref, mixed_ref, grad_ref, gain_ref):
    sel = onehot(send_order())
    for n, out in enumerate((mixed_ref, grad_ref)):
        base = n * 96
        x = jnp.concatenate(
            [in_ref[:, base + l * 16 : base + l * 16 + 16].reshape(TOK, 128) for l in range(6)],
            axis=1,
        )
        for b in range(4):
            y = dot(sel, x[b * 128 : b * 128 + 128], 0, 0).astype(BF)
            for d in range(4):
                out[d, b * 32 : b * 32 + 32] = y[d * 32 : d * 32 + 32]
    g = jnp.sum(in_ref[:, 192:].astype(F32), axis=0)
    gain_ref[...] = jnp.broadcast_to(jnp.sum(g, axis=0, keepdims=True), (8, 128))


def normalise(x):
    xf = x.astype(F32)
    inv_rms = lax.rsqrt(jnp.mean(xf * xf, axis=-1, keepdims=True) + EPS)
    return xf, inv_rms, xf * inv_rms


def main_kernel(
    recv_hbm, gain_ref, feat_ref, wqkv_hbm, wout_hbm,
    keep_ref, send_ref, attn_ref, dqkv_ref,
    recv_ref, wqkv_ref, wout_ref, qkv_ref, ga_ref, norm_ref, gy_ref, lhs_ref, sems,
):
    scale = float(HEAD_DIM) ** (-0.5)
    loads = [
        pltpu.make_async_copy(src, dst, sems.at[n])
        for n, (src, dst) in enumerate(
            ((recv_hbm, recv_ref), (wout_hbm, wout_ref), (wqkv_hbm, wqkv_ref))
        )
    ]
    for c in loads:
        c.start()
    loads[0].wait()
    _, _, unit = normalise(recv_ref[:, 0].reshape(TOK, D))
    normed = (unit * gain_ref[...]).astype(BF)
    norm_ref[...] = by_position(normed)
    gy_ref[...] = by_position(recv_ref[:, 1].reshape(TOK, D))
    loads[1].wait()
    ga_ref[...] = dot(gy_ref[...], wout_ref[...], 1, 1).astype(BF)
    loads[2].wait()

    def project(n, _):
        cols = pl.ds(pl.multiple_of(n * 768, 768), 768)
        qkv_ref[:, cols] = dot(norm_ref[...], wqkv_ref[:, cols], 1, 0).astype(BF)
        return 0

    lax.fori_loop(0, 3, project, 0, unroll=True)
    first = lax.broadcasted_iota(jnp.int32, (128, 128), 1) < 64

    def split(x):
        zero = jnp.zeros_like(x)
        return jnp.concatenate([jnp.where(first, x, zero), jnp.where(first, zero, x)], axis=0)

    def stack(x):
        return jnp.concatenate([x[:, :128], x[:, 128:]], axis=0)

    def heads(hp, _):
        base = pl.multiple_of(hp * 128, 128)
        rows = [slice(p * 128, (p + 1) * 128) for p in range(4)]
        q = [qkv_ref[r, pl.ds(base, 128)] for r in rows]
        k = [qkv_ref[r, pl.ds(base + D, 128)] for r in rows]
        v = [qkv_ref[r, pl.ds(base + 2 * D, 128)] for r in rows]
        qb = [split(x) for x in q]
        gb = [split(ga_ref[r, pl.ds(base, 128)]) for r in rows]
        s = [dot(k[p], qb[p], 1, 1) for p in range(4)]
        dp = [dot(v[p], gb[p], 1, 1) for p in range(4)]
        pb, ds = [], []
        for p in range(4):
            sp = s[p] * scale
            e = jnp.exp(sp - jnp.max(sp, axis=0, keepdims=True))
            probs = e * (1.0 / jnp.sum(e, axis=0, keepdims=True))
            delta = jnp.sum(probs * dp[p], axis=0, keepdims=True)
            ds.append((probs * (dp[p] - delta) * scale).astype(BF))
            pb.append(probs.astype(BF))
        for p in range(4):
            attn_ref[rows[p], pl.ds(base, 128)] = dot(stack(pb[p]), split(v[p]), 0, 0).astype(BF)
            dqkv_ref[rows[p], pl.ds(base, 128)] = dot(stack(ds[p]), split(k[p]), 0, 0).astype(BF)
            dqkv_ref[rows[p], pl.ds(base + D, 128)] = dot(ds[p], qb[p], 1, 0).astype(BF)
            dqkv_ref[rows[p], pl.ds(base + 2 * D, 128)] = dot(pb[p], gb[p], 1, 0).astype(BF)
        return 0

    lax.fori_loop(0, HEADS // 2, heads, 0, unroll=True)
    pick = onehot(lax.broadcasted_iota(jnp.int32, (D, D), 0) == feat_ref[...])
    lhs_ref[...] = dot(pick, norm_ref[...], 0, 1).astype(BF)

    def weight_grad(n, _):
        cols = pl.ds(pl.multiple_of(n * 768, 768), 768)
        g = dot(lhs_ref[...], dqkv_ref[:, cols], 1, 0).astype(BF)
        keep_ref[:, cols] = g[:384]
        send_ref[:, cols] = g[384:]
        return 0

    lax.fori_loop(0, 3, weight_grad, 0, unroll=True)
    lhs_ref[...] = dot(pick, attn_ref[...], 0, 1).astype(BF)
    g = dot(lhs_ref[...], gy_ref[...], 1, 0).astype(BF)
    keep_ref[:, 3 * D :] = g[:384]
    send_ref[:, 3 * D :] = g[384:]


def token_kernel(recv_ref, gain_ref, dqkv_ref, wqkv_ref, ret_ref):
    gn = dot(dqkv_ref[...], wqkv_ref[...], 1, 1).astype(BF)
    gn = by_source(gn).astype(F32)
    _, inv_rms, unit = normalise(recv_ref[:, 0].reshape(TOK, D))
    g = jnp.sum(gn * unit, axis=0, keepdims=True)
    dunit = gn * gain_ref[...]
    back = inv_rms * (dunit - unit * jnp.mean(dunit * unit, axis=-1, keepdims=True))
    gy = recv_ref[:, 1].reshape(TOK, D).astype(F32)
    grad = (gy + back).astype(BF)
    for l in range(6):
        ret_ref[:, l * 16 : l * 16 + 16] = grad[:, l * 128 : l * 128 + 128].reshape(32, 16, 128)
    k = lax.broadcasted_iota(jnp.int32, (32, 8, 128), 0) * 24
    lane = lax.broadcasted_iota(jnp.int32, (32, 8, 128), 2)
    own = jnp.zeros((32, 8, 128), F32)
    for l in range(6):
        f = lane + l * 128
        part = g[:, l * 128 : l * 128 + 128].reshape(1, 1, 128)
        own = own + jnp.where(jnp.logical_and(f >= k, f < k + 24), part, 0.0)
    high = own.astype(BF).astype(F32)
    mid = (own - high).astype(BF).astype(F32)
    row = lax.broadcasted_iota(jnp.int32, (32, 8, 128), 1)
    low = own - high - mid
    terms = jnp.where(row == 0, high, jnp.where(row == 1, mid, jnp.where(row == 2, low, 0.0)))
    ret_ref[:, 96:] = terms.astype(BF)


def mixed_kernel(recv_ref, attn_ref, wout_ref, grad_ref, ret_hbm, ret_ref, sems):
    store_g = pltpu.make_async_copy(grad_ref, ret_hbm.at[:, 96:], sems.at[0])
    store_g.start()
    attn = by_source(attn_ref[...])
    stores = [store_g]
    for n in range(2):
        proj = dot(attn[n * 256 : n * 256 + 256], wout_ref[...], 1, 0).astype(BF)
        x = recv_ref[n * 16 : n * 16 + 16, 0].reshape(256, D).astype(F32)
        mixed = (x + proj.astype(F32)).astype(BF)
        for l in range(6):
            ret_ref[n * 16 : n * 16 + 16, l * 16 : l * 16 + 16] = mixed[
                :, l * 128 : l * 128 + 128
            ].reshape(16, 16, 128)
        part = pl.ds(n * 16, 16)
        store = pltpu.make_async_copy(ret_ref.at[part], ret_hbm.at[part, :96], sems.at[1 + n])
        store.start()
        stores.append(store)
    for c in stores:
        c.wait()


HALF = 2 * D


def pair_sum_kernel(a_ref, b_ref, own, up_hbm, down_hbm, hold, up, down, sems):
    def block(n, cols):
        rows = slice(n * 96, n * 96 + 96)
        return (a_ref[rows, cols].astype(F32) + b_ref[rows, cols].astype(F32)).astype(BF)

    left, right = slice(0, HALF), slice(HALF, 2 * HALF)
    up[:, left] = block(2, left)
    up[:, right] = block(1, right)
    store_up = pltpu.make_async_copy(up, up_hbm, sems.at[0])
    store_up.start()
    down[:, left] = block(3, left)
    down[:, right] = block(2, right)
    store_down = pltpu.make_async_copy(down, down_hbm, sems.at[1])
    store_down.start()
    own[:, left] = block(0, left)
    own[:, right] = block(0, right)
    hold[:, left] = block(1, left)
    hold[:, right] = block(3, right)
    store_up.wait()
    store_down.wait()


def pass_on_kernel(hold, up, down, own, up_out, down_out, sum_out):
    left, right = slice(0, HALF), slice(HALF, 2 * HALF)
    up_out[...] = (hold[:, left].astype(F32) + up[:, left].astype(F32)).astype(BF)
    down_out[...] = (hold[:, right].astype(F32) + down[:, right].astype(F32)).astype(BF)
    sum_out[:, left] = own[:, left].astype(F32) + down[:, left].astype(F32)
    sum_out[:, right] = own[:, right].astype(F32) + up[:, right].astype(F32)


def ring_sum_kernel(near, up_far, down_far, o):
    for q in range(4):
        r = slice(q * 24, q * 24 + 24)
        x = near[r, :HALF] + up_far[r].astype(F32)
        y = near[r, HALF:] + down_far[r].astype(F32)
        for k in range(4):
            pieces = [
                v[k * 6 : k * 6 + 6, l * 128 : l * 128 + 128] for v in (x, y) for l in range(12)
            ]
            o[q * 4 + k] = jnp.concatenate(pieces, axis=0).astype(BF)


def final_kernel(first_ref, in_ref, g0, g1, g2, g3, qkv_ref, out_ref, gain_ref, sum_ref):
    sum_ref[...] = jnp.sum(in_ref[...].astype(F32), axis=0)
    for l in range(24):
        v = sum_ref[l * 6 : l * 6 + 6]
        if l < 18:
            qkv_ref[:, l * 128 : l * 128 + 128] = v
        else:
            out_ref[:, (l - 18) * 128 : (l - 17) * 128] = v
    g = (g0[...] + g1[...]) + (g2[...] + g3[...])
    r = lax.broadcasted_iota(jnp.int32, (8, 128), 0)
    lane = lax.broadcasted_iota(jnp.int32, (8, 128), 1)
    mine = jnp.sum(
        jnp.where(lane == ((first_ref[0] + r) & 127), g, 0.0), axis=1, keepdims=True
    )
    gain_ref[...] = jnp.sum(jnp.where(lane == r, mine, 0.0), axis=0, keepdims=True)[:, :6]


def params(mb):
    return pltpu.CompilerParams(vmem_limit_bytes=int(mb * MB))


def cost(flops, nbytes):
    return pl.CostEstimate(flops=int(flops), bytes_accessed=int(nbytes), transcendentals=0)


def shape(*dims, dtype=BF):
    return jax.ShapeDtypeStruct(dims, dtype)


HBM = pl.BlockSpec(memory_space=pltpu.HBM)
VM = pl.BlockSpec(memory_space=pltpu.VMEM)
DMA = pltpu.SemaphoreType.DMA


def per_device(tokens, cotangent, lesion, w_qkv, w_out, norm_gain):
    gain = norm_gain.reshape(1, D)
    depth = lax.axis_index("depth")
    mod = lax.axis_index("mod")
    feat = lax.dynamic_slice(jnp.asarray(FEATURES), ((depth & 1) * 4 + (mod & 3), 0), (1, D))
    first = ((depth * 8 + mod) * 6).astype(jnp.int32).reshape(1)
    packed = pl.pallas_call(
        pack_kernel, out_shape=shape(32, 2, 16, D), in_specs=[HBM] * 3, out_specs=HBM,
        scratch_shapes=[
            pltpu.VMEM((4, 128, D), BF), pltpu.VMEM((4, 128, D), BF), pltpu.VMEM((4, 128), jnp.int32),
            pltpu.VMEM((2, 32, 16, D), BF), DMA((11,)),
        ],
        compiler_params=params(60), cost_estimate=cost(1e9, 4e6), name="pack",
    )(tokens, cotangent, lesion)
    recv = lax.all_to_all(packed, AXES, 0, 0, tiled=True, axis_index_groups=PLANE)
    keep, send, attn, dqkv = pl.pallas_call(
        main_kernel,
        out_shape=(shape(384, 4 * D), shape(384, 4 * D), shape(TOK, D), shape(TOK, 3 * D)),
        in_specs=[HBM, VM, VM, HBM, HBM],
        scratch_shapes=[
            pltpu.VMEM((32, 2, 16, D), BF), pltpu.VMEM((D, 3 * D), BF), pltpu.VMEM((D, D), BF),
            pltpu.VMEM((TOK, 3 * D), BF), pltpu.VMEM((TOK, D), BF), pltpu.VMEM((TOK, D), BF),
            pltpu.VMEM((TOK, D), BF), pltpu.VMEM((D, TOK), BF), DMA((3,)),
        ],
        compiler_params=params(MAIN_MB), cost_estimate=cost(1e10, 1.5e7), name="main",
    )(recv, gain, feat, w_qkv, w_out)
    got = lax.ppermute(send, AXES, CORE_SWAP)
    grads = pl.pallas_call(
        token_kernel, out_shape=shape(32, 104, 128),
        compiler_params=params(TOKEN_MB), cost_estimate=cost(2.8e9, 9e6), name="token_grads",
    )(recv, gain, dqkv, w_qkv)
    ret = pl.pallas_call(
        mixed_kernel, out_shape=shape(32, 200, 128), out_specs=HBM,
        scratch_shapes=[pltpu.VMEM((32, 96, 128), BF), DMA((3,))],
        compiler_params=params(14), cost_estimate=cost(1e9, 5e6), name="mixed",
    )(recv, attn, w_out, grads)
    quarters = pl.pallas_call(
        pair_sum_kernel, out_shape=tuple(shape(96, 4 * D) for _ in range(4)),
        out_specs=(VM, HBM, HBM, VM),
        scratch_shapes=[pltpu.VMEM((96, 4 * D), BF), pltpu.VMEM((96, 4 * D), BF), DMA((2,))],
        compiler_params=params(6), cost_estimate=cost(1e6, 7e6), name="pair_sum",
    )(keep, got)
    own, up, down, hold, ret = lax.optimization_barrier((*quarters, ret))
    up = lax.ppermute(up, AXES, y_shift(1))
    down = lax.ppermute(down, AXES, y_shift(3))
    up_far, down_far, near = pl.pallas_call(
        pass_on_kernel,
        out_shape=(shape(96, HALF), shape(96, HALF), shape(96, 4 * D, dtype=F32)),
        compiler_params=params(6), cost_estimate=cost(PASS, 3e6), name="pass_on",
    )(hold, up, down, own)
    up_far = lax.ppermute(up_far, AXES, y_shift(1))
    down_far = lax.ppermute(down_far, AXES, y_shift(3))
    back = lax.all_to_all(ret, AXES, 0, 0, tiled=True, axis_index_groups=PLANE)
    mine = pl.pallas_call(
        ring_sum_kernel, out_shape=shape(16, 144, 128),
        compiler_params=params(6), cost_estimate=cost(RING, 3e6), name="ring_sum",
    )(near, up_far, down_far)
    mixed, grad_tokens, gain_part = pl.pallas_call(
        unpack_kernel,
        out_shape=(shape(4, 128, D), shape(4, 128, D), shape(8, 128, dtype=F32)),
        compiler_params=params(14), cost_estimate=cost(1e9, 4e6), name="unpack",
    )(back)
    last = lax.all_to_all(mine, AXES, 0, 0, tiled=True, axis_index_groups=CHIPS)
    gains = [gain_part] + [lax.ppermute(gain_part, AXES, y_shift(s)) for s in range(1, 4)]
    grad_qkv, grad_out, grad_gain = pl.pallas_call(
        final_kernel,
        out_shape=(shape(6, 3 * D, dtype=F32), shape(6, D, dtype=F32), shape(1, 6, dtype=F32)),
        in_specs=[pl.BlockSpec(memory_space=pltpu.SMEM)] + [VM] * 5,
        scratch_shapes=[pltpu.VMEM((144, 128), F32)],
        compiler_params=params(6), cost_estimate=cost(1e6, 1e6), name="final",
    )(first, last, *gains)
    return mixed, grad_tokens, grad_qkv, grad_out, grad_gain.reshape(6)


def solution(mesh):
    in_specs = (P("depth", "mod", None), P("depth", "mod", None), P("depth", "mod"), P(), P(), P())
    out_specs = (
        P("depth", "mod", None),
        P("depth", "mod", None),
        P(("depth", "mod"), None),
        P(("depth", "mod"), None),
        P(("depth", "mod")),
    )
    return jax.shard_map(
        per_device, mesh=mesh, in_specs=in_specs, out_specs=out_specs, check_vma=False
    )
```

```python
import jax
import jax.numpy as jnp
import numpy as np
from jax import lax
from jax.experimental import pallas as pl
from jax.experimental.pallas import tpu as pltpu
from jax.sharding import PartitionSpec as P

HEADS = 12
HEAD_DIM = 64
EPS = 1e-06
LESION_GAIN = 3.0
D = 768
TOK = 512
AXES = ("depth", "mod")
BF = jnp.bfloat16
F32 = jnp.float32
MB = 1024 * 1024
PASS = 1e6
RING = 1e10
MAIN_MB = 42
TOKEN_MB = 14


def place(xlo, z, c, xhi, y):
    return (xlo * 8 + z * 2 + c) * 8 + xhi * 4 + y


def parts_of(i):
    d, m = divmod(i, 8)
    return d // 8, (d // 2) % 4, d % 2, m // 4, m % 4


PLANE = [
    [place(a, z, c, b, y) for a in range(2) for z in range(4) for c in range(2) for b in range(2)]
    for y in range(4)
]
CHIPS = [
    [place(a, z, c, b, y) for a in range(2) for z in range(4) for b in range(2)]
    for c in range(2)
    for y in range(4)
]
CORE_SWAP = [(i, i ^ 8) for i in range(128)]


def y_shift(s):
    out = []
    for i in range(128):
        a, z, c, b, y = parts_of(i)
        out.append((i, place(a, z, c, b, (y + s) % 4)))
    return out


def place_table():
    table = np.zeros((8, D), np.int32)
    for c in range(2):
        for y in range(4):
            n = 0
            for rc in range(2):
                for ry in range(4):
                    for a in range(2):
                        for z in range(4):
                            for b in range(2):
                                i = place(a, z, c ^ rc, b, (y + ry) % 4)
                                for r in range(6):
                                    table[c * 4 + y, 6 * i + r] = n
                                    n += 1
    return table


PLACES = place_table()


def dot(a, b, ca, cb):
    return lax.dot_general(a, b, (((ca,), (cb,)), ((), ())), preferred_element_type=F32)


def onehot(mask):
    return jnp.where(mask, 1.0, 0.0).astype(BF)


def rows_and_columns():
    i = lax.broadcasted_iota(jnp.int32, (128, 128), 0)
    return i, lax.broadcasted_iota(jnp.int32, (128, 128), 1)


def send_order():
    i, s = rows_and_columns()
    return s == ((i >> 2) & 3) * 32 + (i >> 4) * 4 + (i & 3)


def position_order():
    i, s = rows_and_columns()
    return onehot(s == ((i >> 2) & 7) * 16 + (i & 3) * 4 + (i >> 5))


def by_position(x):
    order = position_order()
    parts = [dot(order, x[n * 128 : n * 128 + 128], 1, 0).astype(BF) for n in range(4)]
    return jnp.concatenate(
        [parts[n][p * 32 : p * 32 + 32] for p in range(4) for n in range(4)], axis=0
    )


def by_source(x):
    order = position_order()
    parts = [
        jnp.concatenate([x[p * 128 + n * 32 : p * 128 + n * 32 + 32] for p in range(4)], axis=0)
        for n in range(4)
    ]
    return jnp.concatenate([dot(order, part, 0, 0).astype(BF) for part in parts], axis=0)


def pack_kernel(tok_hbm, cot_hbm, les_hbm, out_hbm, tok_ref, cot_ref, les_ref, out_ref, sems):
    loads = [
        pltpu.make_async_copy(src, dst, sems.at[n])
        for n, (src, dst) in enumerate(
            ((les_hbm, les_ref), (tok_hbm, tok_ref), (cot_hbm, cot_ref))
        )
    ]
    for c in loads:
        c.start()
    mask = send_order()
    plain = onehot(mask)

    def block(ref, n):
        return jnp.concatenate([ref[d, n * 32 : n * 32 + 32] for d in range(4)], axis=0)

    stores = []

    def put(which, n, x):
        out_ref[which, n * 8 : n * 8 + 8] = x.reshape(8, 16, D)
        store = pltpu.make_async_copy(
            out_ref.at[which, pl.ds(n * 8, 8)],
            out_hbm.at[pl.ds(n * 8, 8), which],
            sems.at[3 + which * 4 + n],
        )
        store.start()
        stores.append(store)

    loads[1].wait()
    for n in range(4):
        t = dot(plain, block(tok_ref, n), 1, 0).astype(BF)
        put(0, n, t)
    loads[0].wait()
    weight = 1.0 + LESION_GAIN * les_ref[...].astype(F32)
    loads[2].wait()
    for n in range(4):
        row = jnp.concatenate([weight[d : d + 1, n * 32 : n * 32 + 32] for d in range(4)], axis=1)
        scaled = jnp.where(mask, row, 0.0).astype(BF)
        g = dot(scaled, block(cot_ref, n), 1, 0).astype(BF)
        put(1, n, g)
    for c in stores:
        c.wait()


def unpack_kernel(in_ref, mixed_ref, grad_ref, gain_ref):
    sel = onehot(send_order())
    for n, out in enumerate((mixed_ref, grad_ref)):
        base = n * 96
        x = jnp.concatenate(
            [in_ref[:, base + l * 16 : base + l * 16 + 16].reshape(TOK, 128) for l in range(6)],
            axis=1,
        )
        for b in range(4):
            y = dot(sel, x[b * 128 : b * 128 + 128], 0, 0).astype(BF)
            for d in range(4):
                out[d, b * 32 : b * 32 + 32] = y[d * 32 : d * 32 + 32]
    g = jnp.sum(in_ref[:, 192:].astype(F32), axis=0)
    gain_ref[...] = jnp.broadcast_to(jnp.sum(g, axis=0, keepdims=True), (8, 128))


def normalise(x):
    xf = x.astype(F32)
    inv_rms = lax.rsqrt(jnp.mean(xf * xf, axis=-1, keepdims=True) + EPS)
    return xf, inv_rms, xf * inv_rms


def main_kernel(
    recv_hbm, gain_ref, place_ref, wqkv_hbm, wout_hbm,
    keep_ref, send_ref, attn_ref, dqkv_ref,
    recv_ref, wqkv_ref, wout_ref, qkv_ref, ga_ref, norm_ref, gy_ref, lhs_ref, sems,
):
    scale = float(HEAD_DIM) ** (-0.5)
    loads = [
        pltpu.make_async_copy(src, dst, sems.at[n])
        for n, (src, dst) in enumerate(
            ((recv_hbm, recv_ref), (wout_hbm, wout_ref), (wqkv_hbm, wqkv_ref))
        )
    ]
    for c in loads:
        c.start()
    loads[0].wait()
    _, _, unit = normalise(recv_ref[:, 0].reshape(TOK, D))
    normed = (unit * gain_ref[...]).astype(BF)
    norm_ref[...] = by_position(normed)
    gy_ref[...] = by_position(recv_ref[:, 1].reshape(TOK, D))
    loads[1].wait()
    ga_ref[...] = dot(gy_ref[...], wout_ref[...], 1, 1).astype(BF)
    loads[2].wait()

    def span(n, part):
        return slice(part * D + n * 256, part * D + n * 256 + 256)

    def project(n):
        for part in range(3):
            cols = span(n, part)
            qkv_ref[:, cols] = dot(norm_ref[...], wqkv_ref[:, cols], 1, 0).astype(BF)

    def weight_grad(n, parts):
        for part in parts:
            cols = span(n, part)
            g = dot(lhs_ref[...], dqkv_ref[:, cols], 1, 0).astype(BF)
            keep_ref[:, cols] = g[:384]
            send_ref[:, cols] = g[384:]

    pick = onehot(lax.broadcasted_iota(jnp.int32, (D, D), 0) == place_ref[...])

    def turn():
        lhs_ref[...] = dot(pick, norm_ref[...], 1, 1).astype(BF)

    beside = {
        0: lambda: project(1),
        1: lambda: project(2),
        2: turn,
        3: lambda: weight_grad(0, (0, 1, 2)),
        4: lambda: weight_grad(1, (0, 1)),
        5: lambda: weight_grad(1, (2,)),
    }
    project(0)
    first = lax.broadcasted_iota(jnp.int32, (128, 128), 1) < 64

    def split(x):
        zero = jnp.zeros_like(x)
        return jnp.concatenate([jnp.where(first, x, zero), jnp.where(first, zero, x)], axis=0)

    def stack(x):
        return jnp.concatenate([x[:, :128], x[:, 128:]], axis=0)

    def heads(hp):
        base = hp * 128
        rows = [slice(p * 128, (p + 1) * 128) for p in range(4)]
        q = [qkv_ref[r, pl.ds(base, 128)] for r in rows]
        k = [qkv_ref[r, pl.ds(base + D, 128)] for r in rows]
        v = [qkv_ref[r, pl.ds(base + 2 * D, 128)] for r in rows]
        qb = [split(x) for x in q]
        gb = [split(ga_ref[r, pl.ds(base, 128)]) for r in rows]
        s = [dot(k[p], qb[p], 1, 1) for p in range(4)]
        dp = [dot(v[p], gb[p], 1, 1) for p in range(4)]
        beside[hp]()
        pb, ds = [], []
        for p in range(4):
            sp = s[p] * scale
            e = jnp.exp(sp - jnp.max(sp, axis=0, keepdims=True))
            probs = e * (1.0 / jnp.sum(e, axis=0, keepdims=True))
            delta = jnp.sum(probs * dp[p], axis=0, keepdims=True)
            ds.append((probs * (dp[p] - delta) * scale).astype(BF))
            pb.append(probs.astype(BF))
        for p in range(4):
            attn_ref[rows[p], pl.ds(base, 128)] = dot(stack(pb[p]), split(v[p]), 0, 0).astype(BF)
            dqkv_ref[rows[p], pl.ds(base, 128)] = dot(stack(ds[p]), split(k[p]), 0, 0).astype(BF)
            dqkv_ref[rows[p], pl.ds(base + D, 128)] = dot(ds[p], qb[p], 1, 0).astype(BF)
            dqkv_ref[rows[p], pl.ds(base + 2 * D, 128)] = dot(pb[p], gb[p], 1, 0).astype(BF)

    for hp in range(HEADS // 2):
        heads(hp)
    weight_grad(2, (0, 1, 2))
    lhs_ref[...] = dot(pick, attn_ref[...], 1, 1).astype(BF)
    g = dot(lhs_ref[...], gy_ref[...], 1, 0).astype(BF)
    keep_ref[:, 3 * D :] = g[:384]
    send_ref[:, 3 * D :] = g[384:]


def token_kernel(recv_ref, gain_ref, dqkv_ref, wqkv_ref, ret_ref):
    gn = dot(dqkv_ref[...], wqkv_ref[...], 1, 1).astype(BF)
    gn = by_source(gn).astype(F32)
    _, inv_rms, unit = normalise(recv_ref[:, 0].reshape(TOK, D))
    g = jnp.sum(gn * unit, axis=0, keepdims=True)
    dunit = gn * gain_ref[...]
    back = inv_rms * (dunit - unit * jnp.mean(dunit * unit, axis=-1, keepdims=True))
    gy = recv_ref[:, 1].reshape(TOK, D).astype(F32)
    grad = (gy + back).astype(BF)
    for l in range(6):
        ret_ref[:, l * 16 : l * 16 + 16] = grad[:, l * 128 : l * 128 + 128].reshape(32, 16, 128)
    k = lax.broadcasted_iota(jnp.int32, (32, 8, 128), 0) * 24
    lane = lax.broadcasted_iota(jnp.int32, (32, 8, 128), 2)
    own = jnp.zeros((32, 8, 128), F32)
    for l in range(6):
        f = lane + l * 128
        part = g[:, l * 128 : l * 128 + 128].reshape(1, 1, 128)
        own = own + jnp.where(jnp.logical_and(f >= k, f < k + 24), part, 0.0)
    high = own.astype(BF).astype(F32)
    mid = (own - high).astype(BF).astype(F32)
    row = lax.broadcasted_iota(jnp.int32, (32, 8, 128), 1)
    low = own - high - mid
    terms = jnp.where(row == 0, high, jnp.where(row == 1, mid, jnp.where(row == 2, low, 0.0)))
    ret_ref[:, 96:] = terms.astype(BF)


def mixed_kernel(recv_ref, attn_ref, wout_ref, grad_ref, ret_hbm, ret_ref, sems):
    store_g = pltpu.make_async_copy(grad_ref, ret_hbm.at[:, 96:], sems.at[0])
    store_g.start()
    attn = by_source(attn_ref[...])
    stores = [store_g]
    for n in range(2):
        proj = dot(attn[n * 256 : n * 256 + 256], wout_ref[...], 1, 0).astype(BF)
        x = recv_ref[n * 16 : n * 16 + 16, 0].reshape(256, D).astype(F32)
        mixed = (x + proj.astype(F32)).astype(BF)
        for l in range(6):
            ret_ref[n * 16 : n * 16 + 16, l * 16 : l * 16 + 16] = mixed[
                :, l * 128 : l * 128 + 128
            ].reshape(16, 16, 128)
        part = pl.ds(n * 16, 16)
        store = pltpu.make_async_copy(ret_ref.at[part], ret_hbm.at[part, :96], sems.at[1 + n])
        store.start()
        stores.append(store)
    for c in stores:
        c.wait()


HALF = 2 * D


def pair_sum_kernel(a_ref, b_ref, own, up_hbm, down_hbm, hold, up, down, sems):
    def block(n, cols):
        rows = slice(n * 96, n * 96 + 96)
        return (a_ref[rows, cols].astype(F32) + b_ref[rows, cols].astype(F32)).astype(BF)

    left, right = slice(0, HALF), slice(HALF, 2 * HALF)
    up[:, left] = block(2, left)
    up[:, right] = block(1, right)
    store_up = pltpu.make_async_copy(up, up_hbm, sems.at[0])
    store_up.start()
    down[:, left] = block(3, left)
    down[:, right] = block(2, right)
    store_down = pltpu.make_async_copy(down, down_hbm, sems.at[1])
    store_down.start()
    own[:, left] = block(0, left)
    own[:, right] = block(0, right)
    hold[:, left] = block(1, left)
    hold[:, right] = block(3, right)
    store_up.wait()
    store_down.wait()


def pass_on_kernel(hold, up, down, own, up_out, down_out, sum_out):
    left, right = slice(0, HALF), slice(HALF, 2 * HALF)
    up_out[...] = (hold[:, left].astype(F32) + up[:, left].astype(F32)).astype(BF)
    down_out[...] = (hold[:, right].astype(F32) + down[:, right].astype(F32)).astype(BF)
    sum_out[:, left] = own[:, left].astype(F32) + down[:, left].astype(F32)
    sum_out[:, right] = own[:, right].astype(F32) + up[:, right].astype(F32)


def ring_sum_kernel(near, up_far, down_far, o):
    for q in range(4):
        r = slice(q * 24, q * 24 + 24)
        x = near[r, :HALF] + up_far[r].astype(F32)
        y = near[r, HALF:] + down_far[r].astype(F32)
        for k in range(4):
            pieces = [
                v[k * 6 : k * 6 + 6, l * 128 : l * 128 + 128] for v in (x, y) for l in range(12)
            ]
            o[q * 4 + k] = jnp.concatenate(pieces, axis=0).astype(BF)


def final_kernel(first_ref, in_ref, g0, g1, g2, g3, qkv_ref, out_ref, gain_ref, sum_ref):
    sum_ref[...] = jnp.sum(in_ref[...].astype(F32), axis=0)
    for l in range(24):
        v = sum_ref[l * 6 : l * 6 + 6]
        if l < 18:
            qkv_ref[:, l * 128 : l * 128 + 128] = v
        else:
            out_ref[:, (l - 18) * 128 : (l - 17) * 128] = v
    g = (g0[...] + g1[...]) + (g2[...] + g3[...])
    r = lax.broadcasted_iota(jnp.int32, (8, 128), 0)
    lane = lax.broadcasted_iota(jnp.int32, (8, 128), 1)
    mine = jnp.sum(
        jnp.where(lane == ((first_ref[0] + r) & 127), g, 0.0), axis=1, keepdims=True
    )
    gain_ref[...] = jnp.sum(jnp.where(lane == r, mine, 0.0), axis=0, keepdims=True)[:, :6]


def params(mb):
    return pltpu.CompilerParams(vmem_limit_bytes=int(mb * MB))


def cost(flops, nbytes):
    return pl.CostEstimate(flops=int(flops), bytes_accessed=int(nbytes), transcendentals=0)


def shape(*dims, dtype=BF):
    return jax.ShapeDtypeStruct(dims, dtype)


HBM = pl.BlockSpec(memory_space=pltpu.HBM)
VM = pl.BlockSpec(memory_space=pltpu.VMEM)
DMA = pltpu.SemaphoreType.DMA


def per_device(tokens, cotangent, lesion, w_qkv, w_out, norm_gain):
    gain = norm_gain.reshape(1, D)
    depth = lax.axis_index("depth")
    mod = lax.axis_index("mod")
    place = lax.dynamic_slice(jnp.asarray(PLACES), ((depth & 1) * 4 + (mod & 3), 0), (1, D))
    first = ((depth * 8 + mod) * 6).astype(jnp.int32).reshape(1)
    packed = pl.pallas_call(
        pack_kernel, out_shape=shape(32, 2, 16, D), in_specs=[HBM] * 3, out_specs=HBM,
        scratch_shapes=[
            pltpu.VMEM((4, 128, D), BF), pltpu.VMEM((4, 128, D), BF), pltpu.VMEM((4, 128), jnp.int32),
            pltpu.VMEM((2, 32, 16, D), BF), DMA((11,)),
        ],
        compiler_params=params(60), cost_estimate=cost(1e9, 4e6), name="pack",
    )(tokens, cotangent, lesion)
    recv = lax.all_to_all(packed, AXES, 0, 0, tiled=True, axis_index_groups=PLANE)
    keep, send, attn, dqkv = pl.pallas_call(
        main_kernel,
        out_shape=(shape(384, 4 * D), shape(384, 4 * D), shape(TOK, D), shape(TOK, 3 * D)),
        in_specs=[HBM, VM, VM, HBM, HBM],
        scratch_shapes=[
            pltpu.VMEM((32, 2, 16, D), BF), pltpu.VMEM((D, 3 * D), BF), pltpu.VMEM((D, D), BF),
            pltpu.VMEM((TOK, 3 * D), BF), pltpu.VMEM((TOK, D), BF), pltpu.VMEM((TOK, D), BF),
            pltpu.VMEM((TOK, D), BF), pltpu.VMEM((D, TOK), BF), DMA((3,)),
        ],
        compiler_params=params(MAIN_MB), cost_estimate=cost(1e10, 1.5e7), name="main",
    )(recv, gain, place, w_qkv, w_out)
    got = lax.ppermute(send, AXES, CORE_SWAP)
    grads = pl.pallas_call(
        token_kernel, out_shape=shape(32, 104, 128),
        compiler_params=params(TOKEN_MB), cost_estimate=cost(2.8e9, 9e6), name="token_grads",
    )(recv, gain, dqkv, w_qkv)
    ret = pl.pallas_call(
        mixed_kernel, out_shape=shape(32, 200, 128), out_specs=HBM,
        scratch_shapes=[pltpu.VMEM((32, 96, 128), BF), DMA((3,))],
        compiler_params=params(14), cost_estimate=cost(1e9, 5e6), name="mixed",
    )(recv, attn, w_out, grads)
    quarters = pl.pallas_call(
        pair_sum_kernel, out_shape=tuple(shape(96, 4 * D) for _ in range(4)),
        out_specs=(VM, HBM, HBM, VM),
        scratch_shapes=[pltpu.VMEM((96, 4 * D), BF), pltpu.VMEM((96, 4 * D), BF), DMA((2,))],
        compiler_params=params(6), cost_estimate=cost(1e6, 7e6), name="pair_sum",
    )(keep, got)
    own, up, down, hold, ret = lax.optimization_barrier((*quarters, ret))
    up = lax.ppermute(up, AXES, y_shift(1))
    down = lax.ppermute(down, AXES, y_shift(3))
    up_far, down_far, near = pl.pallas_call(
        pass_on_kernel,
        out_shape=(shape(96, HALF), shape(96, HALF), shape(96, 4 * D, dtype=F32)),
        compiler_params=params(6), cost_estimate=cost(PASS, 3e6), name="pass_on",
    )(hold, up, down, own)
    up_far = lax.ppermute(up_far, AXES, y_shift(1))
    down_far = lax.ppermute(down_far, AXES, y_shift(3))
    back = lax.all_to_all(ret, AXES, 0, 0, tiled=True, axis_index_groups=PLANE)
    mine = pl.pallas_call(
        ring_sum_kernel, out_shape=shape(16, 144, 128),
        compiler_params=params(6), cost_estimate=cost(RING, 3e6), name="ring_sum",
    )(near, up_far, down_far)
    mixed, grad_tokens, gain_part = pl.pallas_call(
        unpack_kernel,
        out_shape=(shape(4, 128, D), shape(4, 128, D), shape(8, 128, dtype=F32)),
        compiler_params=params(14), cost_estimate=cost(1e9, 4e6), name="unpack",
    )(back)
    last = lax.all_to_all(mine, AXES, 0, 0, tiled=True, axis_index_groups=CHIPS)
    gains = [gain_part] + [lax.ppermute(gain_part, AXES, y_shift(s)) for s in range(1, 4)]
    grad_qkv, grad_out, grad_gain = pl.pallas_call(
        final_kernel,
        out_shape=(shape(6, 3 * D, dtype=F32), shape(6, D, dtype=F32), shape(1, 6, dtype=F32)),
        in_specs=[pl.BlockSpec(memory_space=pltpu.SMEM)] + [VM] * 5,
        scratch_shapes=[pltpu.VMEM((144, 128), F32)],
        compiler_params=params(6), cost_estimate=cost(1e6, 1e6), name="final",
    )(first, last, *gains)
    return mixed, grad_tokens, grad_qkv, grad_out, grad_gain.reshape(6)


def solution(mesh):
    in_specs = (P("depth", "mod", None), P("depth", "mod", None), P("depth", "mod"), P(), P(), P())
    out_specs = (
        P("depth", "mod", None),
        P("depth", "mod", None),
        P(("depth", "mod"), None),
        P(("depth", "mod"), None),
        P(("depth", "mod")),
    )
    return jax.shard_map(
        per_device, mesh=mesh, in_specs=in_specs, out_specs=out_specs, check_vma=False
    )
```

```python
import jax
import jax.numpy as jnp
import numpy as np
from jax import lax
from jax.experimental import pallas as pl
from jax.experimental.pallas import tpu as pltpu
from jax.sharding import PartitionSpec as P

HEADS = 12
HEAD_DIM = 64
EPS = 1e-06
LESION_GAIN = 3.0
D = 768
TOK = 512
AXES = ("depth", "mod")
BF = jnp.bfloat16
F32 = jnp.float32
MB = 1024 * 1024
PASS = 1e6
RING = 1e10
MAIN_MB = 42
TOKEN_MB = 14


def place(xlo, z, c, xhi, y):
    return (xlo * 8 + z * 2 + c) * 8 + xhi * 4 + y


def parts_of(i):
    d, m = divmod(i, 8)
    return d // 8, (d // 2) % 4, d % 2, m // 4, m % 4


PLANE = [
    [place(a, z, c, b, y) for a in range(2) for z in range(4) for c in range(2) for b in range(2)]
    for y in range(4)
]
CHIPS = [
    [place(a, z, c, b, y) for a in range(2) for z in range(4) for b in range(2)]
    for c in range(2)
    for y in range(4)
]
CORE_SWAP = [(i, i ^ 8) for i in range(128)]


def y_shift(s):
    out = []
    for i in range(128):
        a, z, c, b, y = parts_of(i)
        out.append((i, place(a, z, c, b, (y + s) % 4)))
    return out


def place_table():
    table = np.zeros((8, D), np.int32)
    for c in range(2):
        for y in range(4):
            n = 0
            for rc in range(2):
                for ry in range(4):
                    for a in range(2):
                        for z in range(4):
                            for b in range(2):
                                i = place(a, z, c ^ rc, b, (y + ry) % 4)
                                for r in range(6):
                                    table[c * 4 + y, 6 * i + r] = n
                                    n += 1
    return table


PLACES = place_table()


def dot(a, b, ca, cb):
    return lax.dot_general(a, b, (((ca,), (cb,)), ((), ())), preferred_element_type=F32)


def onehot(mask):
    return jnp.where(mask, 1.0, 0.0).astype(BF)


def rows_and_columns():
    i = lax.broadcasted_iota(jnp.int32, (128, 128), 0)
    return i, lax.broadcasted_iota(jnp.int32, (128, 128), 1)


def send_order():
    i, s = rows_and_columns()
    return s == ((i >> 2) & 3) * 32 + (i >> 4) * 4 + (i & 3)


def position_order():
    i, s = rows_and_columns()
    return onehot(s == ((i >> 2) & 7) * 16 + (i & 3) * 4 + (i >> 5))


def by_position(x):
    order = position_order()
    parts = [dot(order, x[n * 128 : n * 128 + 128], 1, 0).astype(BF) for n in range(4)]
    return jnp.concatenate(
        [parts[n][p * 32 : p * 32 + 32] for p in range(4) for n in range(4)], axis=0
    )


def by_source(x):
    order = position_order()
    parts = [
        jnp.concatenate([x[p * 128 + n * 32 : p * 128 + n * 32 + 32] for p in range(4)], axis=0)
        for n in range(4)
    ]
    return jnp.concatenate([dot(order, part, 0, 0).astype(BF) for part in parts], axis=0)


def pack_kernel(tok_hbm, cot_hbm, les_hbm, out_hbm, tok_ref, cot_ref, les_ref, out_ref, sems):
    loads = [
        pltpu.make_async_copy(src, dst, sems.at[n])
        for n, (src, dst) in enumerate(
            ((les_hbm, les_ref), (tok_hbm, tok_ref), (cot_hbm, cot_ref))
        )
    ]
    for c in loads:
        c.start()
    mask = send_order()
    plain = onehot(mask)

    def block(ref, n):
        return jnp.concatenate([ref[d, n * 32 : n * 32 + 32] for d in range(4)], axis=0)

    stores = []

    def put(which, n, x):
        out_ref[which, n * 8 : n * 8 + 8] = x.reshape(8, 16, D)
        store = pltpu.make_async_copy(
            out_ref.at[which, pl.ds(n * 8, 8)],
            out_hbm.at[pl.ds(n * 8, 8), which],
            sems.at[3 + which * 4 + n],
        )
        store.start()
        stores.append(store)

    loads[1].wait()
    for n in range(4):
        t = dot(plain, block(tok_ref, n), 1, 0).astype(BF)
        put(0, n, t)
    loads[0].wait()
    weight = 1.0 + LESION_GAIN * les_ref[...].astype(F32)
    loads[2].wait()
    for n in range(4):
        row = jnp.concatenate([weight[d : d + 1, n * 32 : n * 32 + 32] for d in range(4)], axis=1)
        scaled = jnp.where(mask, row, 0.0).astype(BF)
        g = dot(scaled, block(cot_ref, n), 1, 0).astype(BF)
        put(1, n, g)
    for c in stores:
        c.wait()


def unpack_kernel(in_ref, mixed_ref, grad_ref, gain_ref):
    sel = onehot(send_order())
    for n, out in enumerate((mixed_ref, grad_ref)):
        base = n * 96
        x = jnp.concatenate(
            [in_ref[:, base + l * 16 : base + l * 16 + 16].reshape(TOK, 128) for l in range(6)],
            axis=1,
        )
        for b in range(4):
            y = dot(sel, x[b * 128 : b * 128 + 128], 0, 0).astype(BF)
            for d in range(4):
                out[d, b * 32 : b * 32 + 32] = y[d * 32 : d * 32 + 32]
    g = jnp.sum(in_ref[:, 192:].astype(F32), axis=0)
    gain_ref[...] = jnp.broadcast_to(jnp.sum(g, axis=0, keepdims=True), (8, 128))


def normalise(x):
    xf = x.astype(F32)
    inv_rms = lax.rsqrt(jnp.mean(xf * xf, axis=-1, keepdims=True) + EPS)
    return xf, inv_rms, xf * inv_rms


def main_kernel(
    recv_hbm, gain_ref, place_ref, wqkv_hbm, wout_hbm,
    keep_ref, send_ref, attn_ref, dqkv_ref,
    recv_ref, wqkv_ref, wout_ref, qkv_ref, ga_ref, norm_ref, gy_ref, lhs_ref, sems,
):
    scale = float(HEAD_DIM) ** (-0.5)
    loads = [
        pltpu.make_async_copy(src, dst, sems.at[n])
        for n, (src, dst) in enumerate(
            ((recv_hbm, recv_ref), (wout_hbm, wout_ref), (wqkv_hbm, wqkv_ref))
        )
    ]
    for c in loads:
        c.start()
    loads[0].wait()
    _, _, unit = normalise(recv_ref[:, 0].reshape(TOK, D))
    normed = (unit * gain_ref[...]).astype(BF)
    norm_ref[...] = by_position(normed)
    gy_ref[...] = by_position(recv_ref[:, 1].reshape(TOK, D))
    loads[1].wait()
    ga_ref[...] = dot(gy_ref[...], wout_ref[...], 1, 1).astype(BF)
    loads[2].wait()

    def span(n, part):
        return slice(part * D + n * 256, part * D + n * 256 + 256)

    def project(n):
        for part in range(3):
            cols = span(n, part)
            qkv_ref[:, cols] = dot(norm_ref[...], wqkv_ref[:, cols], 1, 0).astype(BF)

    def weight_grad(n, parts):
        for part in parts:
            cols = span(n, part)
            g = dot(lhs_ref[...], dqkv_ref[:, cols], 1, 0).astype(BF)
            keep_ref[:, cols] = g[:384]
            send_ref[:, cols] = g[384:]

    pick = onehot(lax.broadcasted_iota(jnp.int32, (D, D), 0) == place_ref[...])

    def turn():
        lhs_ref[...] = dot(pick, norm_ref[...], 1, 1).astype(BF)

    beside = {
        0: lambda: project(1),
        1: lambda: project(2),
        2: turn,
        3: lambda: weight_grad(0, (0, 1, 2)),
        4: lambda: weight_grad(1, (0, 1)),
        5: lambda: weight_grad(1, (2,)),
    }
    project(0)
    first = lax.broadcasted_iota(jnp.int32, (128, 128), 1) < 64

    def split(x):
        zero = jnp.zeros_like(x)
        return jnp.concatenate([jnp.where(first, x, zero), jnp.where(first, zero, x)], axis=0)

    def stack(x):
        return jnp.concatenate([x[:, :128], x[:, 128:]], axis=0)

    def heads(hp):
        base = hp * 128
        rows = [slice(p * 128, (p + 1) * 128) for p in range(4)]
        q = [qkv_ref[r, pl.ds(base, 128)] for r in rows]
        k = [qkv_ref[r, pl.ds(base + D, 128)] for r in rows]
        v = [qkv_ref[r, pl.ds(base + 2 * D, 128)] for r in rows]
        qb = [split(x) for x in q]
        gb = [split(ga_ref[r, pl.ds(base, 128)]) for r in rows]
        s = [dot(k[p], qb[p], 1, 1) for p in range(4)]
        dp = [dot(v[p], gb[p], 1, 1) for p in range(4)]
        beside[hp]()
        pb, ds = [], []
        for p in range(4):
            sp = s[p] * scale
            e = jnp.exp(sp - jnp.max(sp, axis=0, keepdims=True))
            probs = e * (1.0 / jnp.sum(e, axis=0, keepdims=True))
            delta = jnp.sum(probs * dp[p], axis=0, keepdims=True)
            ds.append((probs * (dp[p] - delta) * scale).astype(BF))
            pb.append(probs.astype(BF))
        for p in range(4):
            attn_ref[rows[p], pl.ds(base, 128)] = dot(stack(pb[p]), split(v[p]), 0, 0).astype(BF)
            dqkv_ref[rows[p], pl.ds(base, 128)] = dot(stack(ds[p]), split(k[p]), 0, 0).astype(BF)
            dqkv_ref[rows[p], pl.ds(base + D, 128)] = dot(ds[p], qb[p], 1, 0).astype(BF)
            dqkv_ref[rows[p], pl.ds(base + 2 * D, 128)] = dot(pb[p], gb[p], 1, 0).astype(BF)

    for hp in range(HEADS // 2):
        heads(hp)
    weight_grad(2, (0, 1, 2))
    lhs_ref[...] = dot(pick, attn_ref[...], 1, 1).astype(BF)
    g = dot(lhs_ref[...], gy_ref[...], 1, 0).astype(BF)
    keep_ref[:, 3 * D :] = g[:384]
    send_ref[:, 3 * D :] = g[384:]


def token_kernel(recv_ref, gain_ref, dqkv_ref, wqkv_ref, ret_ref):
    gn = dot(dqkv_ref[...], wqkv_ref[...], 1, 1).astype(BF)
    gn = by_source(gn).astype(F32)
    _, inv_rms, unit = normalise(recv_ref[:, 0].reshape(TOK, D))
    g = jnp.sum(gn * unit, axis=0, keepdims=True)
    dunit = gn * gain_ref[...]
    back = inv_rms * (dunit - unit * jnp.mean(dunit * unit, axis=-1, keepdims=True))
    gy = recv_ref[:, 1].reshape(TOK, D).astype(F32)
    grad = (gy + back).astype(BF)
    for l in range(6):
        ret_ref[:, l * 16 : l * 16 + 16] = grad[:, l * 128 : l * 128 + 128].reshape(32, 16, 128)
    k = lax.broadcasted_iota(jnp.int32, (32, 8, 128), 0) * 24
    lane = lax.broadcasted_iota(jnp.int32, (32, 8, 128), 2)
    own = jnp.zeros((32, 8, 128), F32)
    for l in range(6):
        f = lane + l * 128
        part = g[:, l * 128 : l * 128 + 128].reshape(1, 1, 128)
        own = own + jnp.where(jnp.logical_and(f >= k, f < k + 24), part, 0.0)
    high = own.astype(BF).astype(F32)
    mid = (own - high).astype(BF).astype(F32)
    row = lax.broadcasted_iota(jnp.int32, (32, 8, 128), 1)
    low = own - high - mid
    terms = jnp.where(row == 0, high, jnp.where(row == 1, mid, jnp.where(row == 2, low, 0.0)))
    ret_ref[:, 96:] = terms.astype(BF)


def mixed_kernel(recv_ref, attn_ref, wout_ref, grad_ref, ret_hbm, ret_ref, sems):
    store_g = pltpu.make_async_copy(grad_ref, ret_hbm.at[:, 96:], sems.at[0])
    store_g.start()
    attn = by_source(attn_ref[...])
    stores = [store_g]
    for n in range(2):
        proj = dot(attn[n * 256 : n * 256 + 256], wout_ref[...], 1, 0).astype(BF)
        x = recv_ref[n * 16 : n * 16 + 16, 0].reshape(256, D).astype(F32)
        mixed = (x + proj.astype(F32)).astype(BF)
        for l in range(6):
            ret_ref[n * 16 : n * 16 + 16, l * 16 : l * 16 + 16] = mixed[
                :, l * 128 : l * 128 + 128
            ].reshape(16, 16, 128)
        part = pl.ds(n * 16, 16)
        store = pltpu.make_async_copy(ret_ref.at[part], ret_hbm.at[part, :96], sems.at[1 + n])
        store.start()
        stores.append(store)
    for c in stores:
        c.wait()


HALF = 2 * D


def pair_sum_kernel(a_ref, b_ref, own, up_hbm, down_hbm, hold, up, down, sems):
    def block(n, cols):
        rows = slice(n * 96, n * 96 + 96)
        return (a_ref[rows, cols].astype(F32) + b_ref[rows, cols].astype(F32)).astype(BF)

    left, right = slice(0, HALF), slice(HALF, 2 * HALF)
    up[:, left] = block(2, left)
    up[:, right] = block(1, right)
    store_up = pltpu.make_async_copy(up, up_hbm, sems.at[0])
    store_up.start()
    down[:, left] = block(3, left)
    down[:, right] = block(2, right)
    store_down = pltpu.make_async_copy(down, down_hbm, sems.at[1])
    store_down.start()
    own[:, left] = block(0, left)
    own[:, right] = block(0, right)
    hold[:, left] = block(1, left)
    hold[:, right] = block(3, right)
    store_up.wait()
    store_down.wait()


def pass_on_kernel(hold, up, down_hbm, own, up_out, down_out, sum_out, down, sem):
    load = pltpu.make_async_copy(down_hbm, down, sem)
    load.start()
    left, right = slice(0, HALF), slice(HALF, 2 * HALF)
    up_out[...] = (hold[:, left].astype(F32) + up[:, left].astype(F32)).astype(BF)
    sum_out[:, right] = own[:, right].astype(F32) + up[:, right].astype(F32)
    load.wait()
    down_out[...] = (hold[:, right].astype(F32) + down[:, right].astype(F32)).astype(BF)
    sum_out[:, left] = own[:, left].astype(F32) + down[:, left].astype(F32)


def ring_sum_kernel(near, up_far, down_far, o):
    for q in range(4):
        r = slice(q * 24, q * 24 + 24)
        x = near[r, :HALF] + up_far[r].astype(F32)
        y = near[r, HALF:] + down_far[r].astype(F32)
        for k in range(4):
            pieces = [
                v[k * 6 : k * 6 + 6, l * 128 : l * 128 + 128] for v in (x, y) for l in range(12)
            ]
            o[q * 4 + k] = jnp.concatenate(pieces, axis=0).astype(BF)


def final_kernel(first_ref, in_ref, g0, g1, g2, g3, qkv_ref, out_ref, gain_ref, sum_ref):
    sum_ref[...] = jnp.sum(in_ref[...].astype(F32), axis=0)
    for l in range(24):
        v = sum_ref[l * 6 : l * 6 + 6]
        if l < 18:
            qkv_ref[:, l * 128 : l * 128 + 128] = v
        else:
            out_ref[:, (l - 18) * 128 : (l - 17) * 128] = v
    g = (g0[...] + g1[...]) + (g2[...] + g3[...])
    r = lax.broadcasted_iota(jnp.int32, (8, 128), 0)
    lane = lax.broadcasted_iota(jnp.int32, (8, 128), 1)
    mine = jnp.sum(
        jnp.where(lane == ((first_ref[0] + r) & 127), g, 0.0), axis=1, keepdims=True
    )
    gain_ref[...] = jnp.sum(jnp.where(lane == r, mine, 0.0), axis=0, keepdims=True)[:, :6]


def params(mb):
    return pltpu.CompilerParams(vmem_limit_bytes=int(mb * MB))


def cost(flops, nbytes):
    return pl.CostEstimate(flops=int(flops), bytes_accessed=int(nbytes), transcendentals=0)


def shape(*dims, dtype=BF):
    return jax.ShapeDtypeStruct(dims, dtype)


HBM = pl.BlockSpec(memory_space=pltpu.HBM)
VM = pl.BlockSpec(memory_space=pltpu.VMEM)
DMA = pltpu.SemaphoreType.DMA


def per_device(tokens, cotangent, lesion, w_qkv, w_out, norm_gain):
    gain = norm_gain.reshape(1, D)
    depth = lax.axis_index("depth")
    mod = lax.axis_index("mod")
    place = lax.dynamic_slice(jnp.asarray(PLACES), ((depth & 1) * 4 + (mod & 3), 0), (1, D))
    first = ((depth * 8 + mod) * 6).astype(jnp.int32).reshape(1)
    packed = pl.pallas_call(
        pack_kernel, out_shape=shape(32, 2, 16, D), in_specs=[HBM] * 3, out_specs=HBM,
        scratch_shapes=[
            pltpu.VMEM((4, 128, D), BF), pltpu.VMEM((4, 128, D), BF), pltpu.VMEM((4, 128), jnp.int32),
            pltpu.VMEM((2, 32, 16, D), BF), DMA((11,)),
        ],
        compiler_params=params(60), cost_estimate=cost(1e9, 4e6), name="pack",
    )(tokens, cotangent, lesion)
    recv = lax.all_to_all(packed, AXES, 0, 0, tiled=True, axis_index_groups=PLANE)
    keep, send, attn, dqkv = pl.pallas_call(
        main_kernel,
        out_shape=(shape(384, 4 * D), shape(384, 4 * D), shape(TOK, D), shape(TOK, 3 * D)),
        in_specs=[HBM, VM, VM, HBM, HBM],
        scratch_shapes=[
            pltpu.VMEM((32, 2, 16, D), BF), pltpu.VMEM((D, 3 * D), BF), pltpu.VMEM((D, D), BF),
            pltpu.VMEM((TOK, 3 * D), BF), pltpu.VMEM((TOK, D), BF), pltpu.VMEM((TOK, D), BF),
            pltpu.VMEM((TOK, D), BF), pltpu.VMEM((D, TOK), BF), DMA((3,)),
        ],
        compiler_params=params(MAIN_MB), cost_estimate=cost(1e10, 1.5e7), name="main",
    )(recv, gain, place, w_qkv, w_out)
    got = lax.ppermute(send, AXES, CORE_SWAP)
    grads = pl.pallas_call(
        token_kernel, out_shape=shape(32, 104, 128),
        compiler_params=params(TOKEN_MB), cost_estimate=cost(2.8e9, 9e6), name="token_grads",
    )(recv, gain, dqkv, w_qkv)
    ret = pl.pallas_call(
        mixed_kernel, out_shape=shape(32, 200, 128), out_specs=HBM,
        scratch_shapes=[pltpu.VMEM((32, 96, 128), BF), DMA((3,))],
        compiler_params=params(14), cost_estimate=cost(1e9, 5e6), name="mixed",
    )(recv, attn, w_out, grads)
    quarters = pl.pallas_call(
        pair_sum_kernel, out_shape=tuple(shape(96, 4 * D) for _ in range(4)),
        out_specs=(VM, HBM, HBM, VM),
        scratch_shapes=[pltpu.VMEM((96, 4 * D), BF), pltpu.VMEM((96, 4 * D), BF), DMA((2,))],
        compiler_params=params(6), cost_estimate=cost(1e6, 7e6), name="pair_sum",
    )(keep, got)
    own, up, down, hold, ret = lax.optimization_barrier((*quarters, ret))
    up = lax.ppermute(up, AXES, y_shift(1))
    down = lax.ppermute(down, AXES, y_shift(3))
    up_far, down_far, near = pl.pallas_call(
        pass_on_kernel,
        out_shape=(shape(96, HALF), shape(96, HALF), shape(96, 4 * D, dtype=F32)),
        in_specs=[VM, VM, HBM, VM],
        scratch_shapes=[pltpu.VMEM((96, 4 * D), BF), DMA],
        compiler_params=params(6), cost_estimate=cost(PASS, 3e6), name="pass_on",
    )(hold, up, down, own)
    up_far = lax.ppermute(up_far, AXES, y_shift(1))
    down_far = lax.ppermute(down_far, AXES, y_shift(3))
    back = lax.all_to_all(ret, AXES, 0, 0, tiled=True, axis_index_groups=PLANE)
    mine = pl.pallas_call(
        ring_sum_kernel, out_shape=shape(16, 144, 128),
        compiler_params=params(6), cost_estimate=cost(RING, 3e6), name="ring_sum",
    )(near, up_far, down_far)
    mixed, grad_tokens, gain_part = pl.pallas_call(
        unpack_kernel,
        out_shape=(shape(4, 128, D), shape(4, 128, D), shape(8, 128, dtype=F32)),
        compiler_params=params(14), cost_estimate=cost(1e9, 4e6), name="unpack",
    )(back)
    last = lax.all_to_all(mine, AXES, 0, 0, tiled=True, axis_index_groups=CHIPS)
    gains = [gain_part] + [lax.ppermute(gain_part, AXES, y_shift(s)) for s in range(1, 4)]
    grad_qkv, grad_out, grad_gain = pl.pallas_call(
        final_kernel,
        out_shape=(shape(6, 3 * D, dtype=F32), shape(6, D, dtype=F32), shape(1, 6, dtype=F32)),
        in_specs=[pl.BlockSpec(memory_space=pltpu.SMEM)] + [VM] * 5,
        scratch_shapes=[pltpu.VMEM((144, 128), F32)],
        compiler_params=params(6), cost_estimate=cost(1e6, 1e6), name="final",
    )(first, last, *gains)
    return mixed, grad_tokens, grad_qkv, grad_out, grad_gain.reshape(6)


def solution(mesh):
    in_specs = (P("depth", "mod", None), P("depth", "mod", None), P("depth", "mod"), P(), P(), P())
    out_specs = (
        P("depth", "mod", None),
        P("depth", "mod", None),
        P(("depth", "mod"), None),
        P(("depth", "mod"), None),
        P(("depth", "mod")),
    )
    return jax.shard_map(
        per_device, mesh=mesh, in_specs=in_specs, out_specs=out_specs, check_vma=False
    )
```

```python
import jax
import jax.numpy as jnp
import numpy as np
from jax import lax
from jax.experimental import pallas as pl
from jax.experimental.pallas import tpu as pltpu
from jax.sharding import PartitionSpec as P

HEADS = 12
HEAD_DIM = 64
EPS = 1e-06
LESION_GAIN = 3.0
D = 768
TOK = 512
AXES = ("depth", "mod")
BF = jnp.bfloat16
F32 = jnp.float32
MB = 1024 * 1024
PASS = 1e6
RING = 1e10
MAIN_MB = 42
TOKEN_MB = 14


def place(xlo, z, c, xhi, y):
    return (xlo * 8 + z * 2 + c) * 8 + xhi * 4 + y


def parts_of(i):
    d, m = divmod(i, 8)
    return d // 8, (d // 2) % 4, d % 2, m // 4, m % 4


PLANE = [
    [place(a, z, c, b, y) for a in range(2) for z in range(4) for c in range(2) for b in range(2)]
    for y in range(4)
]
CHIPS = [
    [place(a, z, c, b, y) for a in range(2) for z in range(4) for b in range(2)]
    for c in range(2)
    for y in range(4)
]
CORE_SWAP = [(i, i ^ 8) for i in range(128)]


def y_shift(s):
    out = []
    for i in range(128):
        a, z, c, b, y = parts_of(i)
        out.append((i, place(a, z, c, b, (y + s) % 4)))
    return out


def place_table():
    table = np.zeros((8, D), np.int32)
    for c in range(2):
        for y in range(4):
            n = 0
            for rc in range(2):
                for ry in range(4):
                    for a in range(2):
                        for z in range(4):
                            for b in range(2):
                                i = place(a, z, c ^ rc, b, (y + ry) % 4)
                                for r in range(6):
                                    table[c * 4 + y, 6 * i + r] = n
                                    n += 1
    return table


PLACES = place_table()


def dot(a, b, ca, cb):
    return lax.dot_general(a, b, (((ca,), (cb,)), ((), ())), preferred_element_type=F32)


def onehot(mask):
    return jnp.where(mask, 1.0, 0.0).astype(BF)


def rows_and_columns():
    i = lax.broadcasted_iota(jnp.int32, (128, 128), 0)
    return i, lax.broadcasted_iota(jnp.int32, (128, 128), 1)


def send_order():
    i, s = rows_and_columns()
    return s == ((i >> 2) & 3) * 32 + (i >> 4) * 4 + (i & 3)


def position_order():
    i, s = rows_and_columns()
    return onehot(s == ((i >> 2) & 7) * 16 + (i & 3) * 4 + (i >> 5))


def by_position(x):
    order = position_order()
    parts = [dot(order, x[n * 128 : n * 128 + 128], 1, 0).astype(BF) for n in range(4)]
    return jnp.concatenate(
        [parts[n][p * 32 : p * 32 + 32] for p in range(4) for n in range(4)], axis=0
    )


def by_source(x):
    order = position_order()
    parts = [
        jnp.concatenate([x[p * 128 + n * 32 : p * 128 + n * 32 + 32] for p in range(4)], axis=0)
        for n in range(4)
    ]
    return jnp.concatenate([dot(order, part, 0, 0).astype(BF) for part in parts], axis=0)


def pack_kernel(tok_hbm, cot_hbm, les_hbm, out_hbm, tok_ref, cot_ref, les_ref, out_ref, sems):
    loads = [
        pltpu.make_async_copy(src, dst, sems.at[n])
        for n, (src, dst) in enumerate(
            ((les_hbm, les_ref), (tok_hbm, tok_ref), (cot_hbm, cot_ref))
        )
    ]
    for c in loads:
        c.start()
    mask = send_order()
    plain = onehot(mask)

    def block(ref, n):
        return jnp.concatenate([ref[d, n * 32 : n * 32 + 32] for d in range(4)], axis=0)

    stores = []

    def put(which, n, x):
        out_ref[which, n * 8 : n * 8 + 8] = x.reshape(8, 16, D)
        store = pltpu.make_async_copy(
            out_ref.at[which, pl.ds(n * 8, 8)],
            out_hbm.at[pl.ds(n * 8, 8), which],
            sems.at[3 + which * 4 + n],
        )
        store.start()
        stores.append(store)

    loads[1].wait()
    for n in range(4):
        t = dot(plain, block(tok_ref, n), 1, 0).astype(BF)
        put(0, n, t)
    loads[0].wait()
    weight = 1.0 + LESION_GAIN * les_ref[...].astype(F32)
    loads[2].wait()
    for n in range(4):
        row = jnp.concatenate([weight[d : d + 1, n * 32 : n * 32 + 32] for d in range(4)], axis=1)
        scaled = jnp.where(mask, row, 0.0).astype(BF)
        g = dot(scaled, block(cot_ref, n), 1, 0).astype(BF)
        put(1, n, g)
    for c in stores:
        c.wait()


def unpack_kernel(in_ref, mixed_ref, grad_ref, gain_ref):
    sel = onehot(send_order())
    for n, out in enumerate((mixed_ref, grad_ref)):
        base = n * 96
        x = jnp.concatenate(
            [in_ref[:, base + l * 16 : base + l * 16 + 16].reshape(TOK, 128) for l in range(6)],
            axis=1,
        )
        for b in range(4):
            y = dot(sel, x[b * 128 : b * 128 + 128], 0, 0).astype(BF)
            for d in range(4):
                out[d, b * 32 : b * 32 + 32] = y[d * 32 : d * 32 + 32]
    g = jnp.sum(in_ref[:, 192:].astype(F32), axis=0)
    gain_ref[...] = jnp.broadcast_to(jnp.sum(g, axis=0, keepdims=True), (8, 128))


def normalise(x):
    xf = x.astype(F32)
    inv_rms = lax.rsqrt(jnp.mean(xf * xf, axis=-1, keepdims=True) + EPS)
    return xf, inv_rms, xf * inv_rms


def main_kernel(
    recv_hbm, gain_ref, place_ref, wqkv_hbm, wout_hbm,
    keep_ref, send_ref, attn_ref, dqkv_ref,
    recv_ref, wqkv_ref, wout_ref, qkv_ref, ga_ref, norm_ref, gy_ref, lhs_ref, sems,
):
    scale = float(HEAD_DIM) ** (-0.5)
    loads = [
        pltpu.make_async_copy(src, dst, sems.at[n])
        for n, (src, dst) in enumerate(
            ((recv_hbm, recv_ref), (wout_hbm, wout_ref), (wqkv_hbm, wqkv_ref))
        )
    ]
    for c in loads:
        c.start()
    loads[0].wait()
    _, _, unit = normalise(recv_ref[:, 0].reshape(TOK, D))
    normed = (unit * gain_ref[...]).astype(BF)
    norm_ref[...] = by_position(normed)
    gy_ref[...] = by_position(recv_ref[:, 1].reshape(TOK, D))
    loads[1].wait()
    ga_ref[...] = dot(gy_ref[...], wout_ref[...], 1, 1).astype(BF)
    loads[2].wait()

    def span(n, part):
        return slice(part * D + n * 256, part * D + n * 256 + 256)

    def project(n):
        for part in range(3):
            cols = span(n, part)
            qkv_ref[:, cols] = dot(norm_ref[...], wqkv_ref[:, cols], 1, 0).astype(BF)

    def weight_grad(n, parts):
        for part in parts:
            cols = span(n, part)
            g = dot(lhs_ref[...], dqkv_ref[:, cols], 1, 0).astype(BF)
            keep_ref[:, cols] = g[:384]
            send_ref[:, cols] = g[384:]

    pick = onehot(lax.broadcasted_iota(jnp.int32, (D, D), 0) == place_ref[...])

    def turn():
        lhs_ref[...] = dot(pick, norm_ref[...], 1, 1).astype(BF)

    beside = {
        0: lambda: project(1),
        1: lambda: project(2),
        2: turn,
        3: lambda: weight_grad(0, (0, 1, 2)),
        4: lambda: weight_grad(1, (0, 1)),
        5: lambda: weight_grad(1, (2,)),
    }
    project(0)
    first = lax.broadcasted_iota(jnp.int32, (128, 128), 1) < 64

    def split(x):
        zero = jnp.zeros_like(x)
        return jnp.concatenate([jnp.where(first, x, zero), jnp.where(first, zero, x)], axis=0)

    def stack(x):
        return jnp.concatenate([x[:, :128], x[:, 128:]], axis=0)

    def heads(hp):
        base = hp * 128
        rows = [slice(p * 128, (p + 1) * 128) for p in range(4)]
        q = [qkv_ref[r, pl.ds(base, 128)] for r in rows]
        k = [qkv_ref[r, pl.ds(base + D, 128)] for r in rows]
        v = [qkv_ref[r, pl.ds(base + 2 * D, 128)] for r in rows]
        qb = [split(x) for x in q]
        gb = [split(ga_ref[r, pl.ds(base, 128)]) for r in rows]
        s = [dot(k[p], qb[p], 1, 1) for p in range(4)]
        dp = [dot(v[p], gb[p], 1, 1) for p in range(4)]
        beside[hp]()
        pb, ds = [], []
        for p in range(4):
            sp = s[p] * scale
            e = jnp.exp(sp - jnp.max(sp, axis=0, keepdims=True))
            probs = e * (1.0 / jnp.sum(e, axis=0, keepdims=True))
            delta = jnp.sum(probs * dp[p], axis=0, keepdims=True)
            ds.append((probs * (dp[p] - delta) * scale).astype(BF))
            pb.append(probs.astype(BF))
        for p in range(4):
            attn_ref[rows[p], pl.ds(base, 128)] = dot(stack(pb[p]), split(v[p]), 0, 0).astype(BF)
            dqkv_ref[rows[p], pl.ds(base, 128)] = dot(stack(ds[p]), split(k[p]), 0, 0).astype(BF)
            dqkv_ref[rows[p], pl.ds(base + D, 128)] = dot(ds[p], qb[p], 1, 0).astype(BF)
            dqkv_ref[rows[p], pl.ds(base + 2 * D, 128)] = dot(pb[p], gb[p], 1, 0).astype(BF)

    for hp in range(HEADS // 2):
        heads(hp)
    weight_grad(2, (0, 1, 2))
    lhs_ref[...] = dot(pick, attn_ref[...], 1, 1).astype(BF)
    g = dot(lhs_ref[...], gy_ref[...], 1, 0).astype(BF)
    keep_ref[:, 3 * D :] = g[:384]
    send_ref[:, 3 * D :] = g[384:]


def token_kernel(recv_ref, gain_ref, dqkv_ref, wqkv_ref, ret_ref):
    gn = dot(dqkv_ref[...], wqkv_ref[...], 1, 1).astype(BF)
    gn = by_source(gn).astype(F32)
    _, inv_rms, unit = normalise(recv_ref[:, 0].reshape(TOK, D))
    g = jnp.sum(gn * unit, axis=0, keepdims=True)
    dunit = gn * gain_ref[...]
    back = inv_rms * (dunit - unit * jnp.mean(dunit * unit, axis=-1, keepdims=True))
    gy = recv_ref[:, 1].reshape(TOK, D).astype(F32)
    grad = (gy + back).astype(BF)
    for l in range(6):
        ret_ref[:, l * 16 : l * 16 + 16] = grad[:, l * 128 : l * 128 + 128].reshape(32, 16, 128)
    k = lax.broadcasted_iota(jnp.int32, (32, 16, 128), 0) * 24
    lane = lax.broadcasted_iota(jnp.int32, (32, 16, 128), 2)
    own = jnp.zeros((32, 16, 128), F32)
    for l in range(6):
        f = lane + l * 128
        part = g[:, l * 128 : l * 128 + 128].reshape(1, 1, 128)
        own = own + jnp.where(jnp.logical_and(f >= k, f < k + 24), part, 0.0)
    high = own.astype(BF).astype(F32)
    mid = (own - high).astype(BF).astype(F32)
    row = lax.broadcasted_iota(jnp.int32, (32, 16, 128), 1)
    low = own - high - mid
    terms = jnp.where(row == 0, high, jnp.where(row == 1, mid, jnp.where(row == 2, low, 0.0)))
    ret_ref[:, 96:] = terms.astype(BF)


def mixed_kernel(recv_ref, attn_ref, wout_ref, grad_ref, ret_hbm, ret_ref, sems):
    store_g = pltpu.make_async_copy(grad_ref, ret_hbm.at[:, 96:], sems.at[0])
    store_g.start()
    attn = by_source(attn_ref[...])
    stores = [store_g]
    for n in range(2):
        proj = dot(attn[n * 256 : n * 256 + 256], wout_ref[...], 1, 0).astype(BF)
        x = recv_ref[n * 16 : n * 16 + 16, 0].reshape(256, D).astype(F32)
        mixed = (x + proj.astype(F32)).astype(BF)
        for l in range(6):
            ret_ref[n * 16 : n * 16 + 16, l * 16 : l * 16 + 16] = mixed[
                :, l * 128 : l * 128 + 128
            ].reshape(16, 16, 128)
        part = pl.ds(n * 16, 16)
        store = pltpu.make_async_copy(ret_ref.at[part], ret_hbm.at[part, :96], sems.at[1 + n])
        store.start()
        stores.append(store)
    for c in stores:
        c.wait()


HALF = 2 * D


def pair_sum_kernel(a_ref, b_ref, own, up_hbm, down_hbm, hold, up, down, sems):
    def block(n, cols):
        rows = slice(n * 96, n * 96 + 96)
        return (a_ref[rows, cols].astype(F32) + b_ref[rows, cols].astype(F32)).astype(BF)

    left, right = slice(0, HALF), slice(HALF, 2 * HALF)
    up[:, left] = block(2, left)
    up[:, right] = block(1, right)
    store_up = pltpu.make_async_copy(up, up_hbm, sems.at[0])
    store_up.start()
    down[:, left] = block(3, left)
    down[:, right] = block(2, right)
    store_down = pltpu.make_async_copy(down, down_hbm, sems.at[1])
    store_down.start()
    own[:, left] = block(0, left)
    own[:, right] = block(0, right)
    hold[:, left] = block(1, left)
    hold[:, right] = block(3, right)
    store_up.wait()
    store_down.wait()


def pass_on_kernel(hold, up, down_hbm, own, up_out, down_out, sum_out, down, sem):
    load = pltpu.make_async_copy(down_hbm, down, sem)
    load.start()
    left, right = slice(0, HALF), slice(HALF, 2 * HALF)
    up_out[...] = (hold[:, left].astype(F32) + up[:, left].astype(F32)).astype(BF)
    sum_out[:, right] = own[:, right].astype(F32) + up[:, right].astype(F32)
    load.wait()
    down_out[...] = (hold[:, right].astype(F32) + down[:, right].astype(F32)).astype(BF)
    sum_out[:, left] = own[:, left].astype(F32) + down[:, left].astype(F32)


def ring_sum_kernel(near, up_far, down_far, o):
    for q in range(2):
        r = slice(q * 48, q * 48 + 48)
        x = near[r, :HALF] + up_far[r].astype(F32)
        y = near[r, HALF:] + down_far[r].astype(F32)
        for k in range(8):
            pieces = [
                v[k * 6 : k * 6 + 6, l * 128 : l * 128 + 128] for v in (x, y) for l in range(12)
            ]
            o[q * 8 + k] = jnp.concatenate(pieces, axis=0).astype(BF)


def final_kernel(first_ref, in_ref, g0, g1, g2, g3, qkv_ref, out_ref, gain_ref, sum_ref):
    sum_ref[...] = jnp.sum(in_ref[...].astype(F32), axis=0)
    for l in range(24):
        v = sum_ref[l * 6 : l * 6 + 6]
        if l < 18:
            qkv_ref[:, l * 128 : l * 128 + 128] = v
        else:
            out_ref[:, (l - 18) * 128 : (l - 17) * 128] = v
    g = (g0[...] + g1[...]) + (g2[...] + g3[...])
    r = lax.broadcasted_iota(jnp.int32, (8, 128), 0)
    lane = lax.broadcasted_iota(jnp.int32, (8, 128), 1)
    mine = jnp.sum(
        jnp.where(lane == ((first_ref[0] + r) & 127), g, 0.0), axis=1, keepdims=True
    )
    gain_ref[...] = jnp.sum(jnp.where(lane == r, mine, 0.0), axis=0, keepdims=True)[:, :6]


def params(mb):
    return pltpu.CompilerParams(vmem_limit_bytes=int(mb * MB))


def cost(flops, nbytes):
    return pl.CostEstimate(flops=int(flops), bytes_accessed=int(nbytes), transcendentals=0)


def shape(*dims, dtype=BF):
    return jax.ShapeDtypeStruct(dims, dtype)


HBM = pl.BlockSpec(memory_space=pltpu.HBM)
VM = pl.BlockSpec(memory_space=pltpu.VMEM)
DMA = pltpu.SemaphoreType.DMA


def per_device(tokens, cotangent, lesion, w_qkv, w_out, norm_gain):
    gain = norm_gain.reshape(1, D)
    depth = lax.axis_index("depth")
    mod = lax.axis_index("mod")
    place = lax.dynamic_slice(jnp.asarray(PLACES), ((depth & 1) * 4 + (mod & 3), 0), (1, D))
    first = ((depth * 8 + mod) * 6).astype(jnp.int32).reshape(1)
    packed = pl.pallas_call(
        pack_kernel, out_shape=shape(32, 2, 16, D), in_specs=[HBM] * 3, out_specs=HBM,
        scratch_shapes=[
            pltpu.VMEM((4, 128, D), BF), pltpu.VMEM((4, 128, D), BF), pltpu.VMEM((4, 128), jnp.int32),
            pltpu.VMEM((2, 32, 16, D), BF), DMA((11,)),
        ],
        compiler_params=params(60), cost_estimate=cost(1e9, 4e6), name="pack",
    )(tokens, cotangent, lesion)
    recv = lax.all_to_all(packed, AXES, 0, 0, tiled=True, axis_index_groups=PLANE)
    keep, send, attn, dqkv = pl.pallas_call(
        main_kernel,
        out_shape=(shape(384, 4 * D), shape(384, 4 * D), shape(TOK, D), shape(TOK, 3 * D)),
        in_specs=[HBM, VM, VM, HBM, HBM],
        scratch_shapes=[
            pltpu.VMEM((32, 2, 16, D), BF), pltpu.VMEM((D, 3 * D), BF), pltpu.VMEM((D, D), BF),
            pltpu.VMEM((TOK, 3 * D), BF), pltpu.VMEM((TOK, D), BF), pltpu.VMEM((TOK, D), BF),
            pltpu.VMEM((TOK, D), BF), pltpu.VMEM((D, TOK), BF), DMA((3,)),
        ],
        compiler_params=params(MAIN_MB), cost_estimate=cost(1e10, 1.5e7), name="main",
    )(recv, gain, place, w_qkv, w_out)
    got = lax.ppermute(send, AXES, CORE_SWAP)
    grads = pl.pallas_call(
        token_kernel, out_shape=shape(32, 112, 128),
        compiler_params=params(TOKEN_MB), cost_estimate=cost(2.8e9, 9e6), name="token_grads",
    )(recv, gain, dqkv, w_qkv)
    ret = pl.pallas_call(
        mixed_kernel, out_shape=shape(32, 208, 128), out_specs=HBM,
        scratch_shapes=[pltpu.VMEM((32, 96, 128), BF), DMA((3,))],
        compiler_params=params(14), cost_estimate=cost(1e9, 5e6), name="mixed",
    )(recv, attn, w_out, grads)
    quarters = pl.pallas_call(
        pair_sum_kernel, out_shape=tuple(shape(96, 4 * D) for _ in range(4)),
        out_specs=(VM, HBM, HBM, VM),
        scratch_shapes=[pltpu.VMEM((96, 4 * D), BF), pltpu.VMEM((96, 4 * D), BF), DMA((2,))],
        compiler_params=params(6), cost_estimate=cost(1e6, 7e6), name="pair_sum",
    )(keep, got)
    own, up, down, hold, ret = lax.optimization_barrier((*quarters, ret))
    up = lax.ppermute(up, AXES, y_shift(1))
    down = lax.ppermute(down, AXES, y_shift(3))
    up_far, down_far, near = pl.pallas_call(
        pass_on_kernel,
        out_shape=(shape(96, HALF), shape(96, HALF), shape(96, 4 * D, dtype=F32)),
        in_specs=[VM, VM, HBM, VM],
        scratch_shapes=[pltpu.VMEM((96, 4 * D), BF), DMA],
        compiler_params=params(6), cost_estimate=cost(PASS, 3e6), name="pass_on",
    )(hold, up, down, own)
    up_far = lax.ppermute(up_far, AXES, y_shift(1))
    down_far = lax.ppermute(down_far, AXES, y_shift(3))
    back = lax.all_to_all(ret, AXES, 0, 0, tiled=True, axis_index_groups=PLANE)
    mine = pl.pallas_call(
        ring_sum_kernel, out_shape=shape(16, 144, 128),
        compiler_params=params(6), cost_estimate=cost(RING, 3e6), name="ring_sum",
    )(near, up_far, down_far)
    mixed, grad_tokens, gain_part = pl.pallas_call(
        unpack_kernel,
        out_shape=(shape(4, 128, D), shape(4, 128, D), shape(8, 128, dtype=F32)),
        compiler_params=params(14), cost_estimate=cost(1e9, 4e6), name="unpack",
    )(back)
    last = lax.all_to_all(mine, AXES, 0, 0, tiled=True, axis_index_groups=CHIPS)
    gains = [gain_part] + [lax.ppermute(gain_part, AXES, y_shift(s)) for s in range(1, 4)]
    grad_qkv, grad_out, grad_gain = pl.pallas_call(
        final_kernel,
        out_shape=(shape(6, 3 * D, dtype=F32), shape(6, D, dtype=F32), shape(1, 6, dtype=F32)),
        in_specs=[pl.BlockSpec(memory_space=pltpu.SMEM)] + [VM] * 5,
        scratch_shapes=[pltpu.VMEM((144, 128), F32)],
        compiler_params=params(6), cost_estimate=cost(1e6, 1e6), name="final",
    )(first, last, *gains)
    return mixed, grad_tokens, grad_qkv, grad_out, grad_gain.reshape(6)


def solution(mesh):
    in_specs = (P("depth", "mod", None), P("depth", "mod", None), P("depth", "mod"), P(), P(), P())
    out_specs = (
        P("depth", "mod", None),
        P("depth", "mod", None),
        P(("depth", "mod"), None),
        P(("depth", "mod"), None),
        P(("depth", "mod")),
    )
    return jax.shard_map(
        per_device, mesh=mesh, in_specs=in_specs, out_specs=out_specs, check_vma=False
    )
```
